32 devices in a mesh: batch: 4 (over x, core), mp: 8 (over z, y).
Axes of the slice: x: 2, y: 2, z: 4, core: 2. Of those that a mesh axis runs over, the one named last changes fastest.
Arguments:
- features: bfloat16 [256, 8192], P('mp', 'batch'), may hold values from -5 to 5
- counts: int32 [4], P('batch'), may hold values from 16 to 32, as said below
- labels: int32 [128], P('batch'), may hold values from 0 to 99
- teacher: float32 [128, 100], P('batch'), may hold values from -30 to 30
- conv1_weight: bfloat16 [256, 9, 256], P('mp'), may hold values from -0.125 to 0.125
- bn1_gain: float32 [256], P('mp'), may hold values from 0.5 to 1.5
- bn1_bias: float32 [256], P('mp'), may hold values from -3 to 3
- conv2_weight: bfloat16 [256, 9, 256], P('mp'), may hold values from -0.125 to 0.125
- bn2_gain: float32 [256], P('mp'), may hold values from 0.5 to 1.5
- bn2_bias: float32 [256], P('mp'), may hold values from -3 to 3
- head_weight: bfloat16 [256, 100], P('mp'), may hold values from -3 to 3
- head_bias: float32 [100], replicated, may hold values from -4 to 4
- run_mean1: float32 [256], P('mp'), may hold values from -3 to 3
- run_var1: float32 [256], P('mp'), may hold values from 0.5 to 2
- run_mean2: float32 [256], P('mp'), may hold values from -3 to 3
- run_var2: float32 [256], P('mp'), may hold values from 0.5 to 2
Outputs:
- loss: float32 [], replicated
- grad_features: float32 [256, 8192], P('mp', 'batch')
- grad_conv1: float32 [256, 9, 256], P('mp')
- grad_gain1: float32 [256], P('mp')
- grad_bias1: float32 [256], P('mp')
- grad_conv2: float32 [256, 9, 256], P('mp')
- grad_gain2: float32 [256], P('mp')
- grad_bias2: float32 [256], P('mp')
- grad_head: float32 [256, 100], P('mp')
- grad_head_bias: float32 [100], replicated
- new_mean1: float32 [256], P('mp')
- new_var1: float32 [256], P('mp')
- new_mean2: float32 [256], P('mp')
- new_var2: float32 [256], P('mp')
The draws below stay inside these ranges and needn't reach their ends.
Inputs may be any that keep to these rules, and one draw needn't show every extreme that they name: counts[b] live images stand first among the 32 slots of batch index b; some index holds 32 live images in every draw.
All inputs are finite; a program needn't handle non-finite values.
Results may differ from the reference program's by a relative error of at most 0.0048.
Values may be sent and summed in bfloat16 or wider, within the bound.
A program may use at most 128 MiB of HBM per device.

```python
import math
import jax
import jax.numpy as jnp
from jax import lax

C = 256
CLASSES = 100
SIDE = 8
TAPS = 9
IMG_DEV = 32
IMAGES = 128
CELLS = 8192
N_BATCH = 4


def draw_counts(key, part):
    key = jax.random.fold_in(key, 7)
    value_key, index_key = jax.random.split(key)
    values = jax.random.randint(value_key, (N_BATCH,), IMG_DEV // 2, IMG_DEV + 1)
    full_index = jax.random.randint(index_key, (), 0, N_BATCH)
    return jnp.where(jnp.arange(N_BATCH) == full_index, IMG_DEV, values).astype(jnp.int32)


def draw_features(key, part):
    key = jax.random.fold_in(key, 11)
    offset_key, noise_key = jax.random.split(key, 2)
    offset = jax.random.uniform(offset_key, (C, 1), jnp.float32, -1.5, 1.5)
    noise = jnp.clip(jax.random.normal(noise_key, (C, CELLS), jnp.float32), -3.5, 3.5)
    return (offset + noise).astype(jnp.bfloat16)


def place_ends(drawn, rng, least, top_value):
    shape = drawn.shape
    index_at = [jax.random.randint(jax.random.fold_in(rng, axis), (), 0, shape[axis]) for axis in range(len(shape))]
    drawn = drawn.at[tuple(index_at)].set(least)
    longest = shape.index(max(shape))
    index_at[longest] = (index_at[longest] + 1) % shape[longest]
    return drawn.at[tuple(index_at)].set(top_value)


def steps_of(rng, extent, cuts, low, high):
    factor_of, own = 1.0, jax.random.fold_in(rng, 6)
    for position, blocks in cuts:
        draws = jnp.exp(jax.random.uniform(jax.random.fold_in(own, position), (blocks,), jnp.float32, low / len(cuts), high / len(cuts)))
        factor_of = factor_of * jnp.repeat(draws, extent[position] // blocks).reshape([-1 if axis == position else 1 for axis in range(len(extent))])
    return factor_of


def scatter_about(rng, shape, deviation, reach, shards=(), held_as=jnp.bfloat16):
    array = deviation * jax.random.normal(rng, shape, jnp.float32)
    if shards:
        array = array * steps_of(rng, shape, shards, -0.22, 0.18)
    return jnp.clip(array, -reach, reach).astype(held_as)


def setup_inputs(seed: int = 0) -> dict:
    arg_keys = jax.random.split(jax.random.key(seed), 17)
    features = draw_features(jax.random.fold_in(arg_keys[16], 71), 0)
    counts = draw_counts(jax.random.fold_in(arg_keys[16], 71), 0)
    labels = place_ends(jax.random.randint(arg_keys[2], (IMAGES,), 0, CLASSES), jax.random.fold_in(arg_keys[2], 1), 0, CLASSES - 1).astype(jnp.int32)
    teacher = scatter_about(arg_keys[3], (IMAGES, CLASSES), 6.0, 30.0, ((0, 4),), jnp.float32)
    conv1_weight = scatter_about(arg_keys[4], (C, TAPS, C), (TAPS * C) ** -0.5, 0.125, ((0, 8),))
    bn1_gain = jnp.clip(1.0 + 0.1 * jax.random.normal(arg_keys[5], (C,), jnp.float32), 0.5, 1.5)
    bn1_bias = scatter_about(arg_keys[6], (C,), 0.5, 3.0, ((0, 8),), jnp.float32)
    conv2_weight = scatter_about(arg_keys[7], (C, TAPS, C), (TAPS * C) ** -0.5, 0.125, ((0, 8),))
    bn2_gain = jnp.clip(1.0 + 0.1 * jax.random.normal(arg_keys[8], (C,), jnp.float32), 0.5, 1.5)
    bn2_bias = scatter_about(arg_keys[9], (C,), 0.5, 3.0, ((0, 8),), jnp.float32)
    head_weight = scatter_about(arg_keys[10], (C, CLASSES), 4 ** -0.5, 3.0, ((0, 8),))
    head_bias = scatter_about(arg_keys[11], (CLASSES,), 1.0, 4.0, (), jnp.float32)
    run_mean1 = scatter_about(arg_keys[12], (C,), 0.5, 3.0, ((0, 8),), jnp.float32)
    run_var1 = jnp.clip(jnp.exp(math.log(2.0) - 1.3862944 * jax.random.uniform(arg_keys[13], (C,), jnp.float32) ** steps_of(arg_keys[13], (C,), ((0, 8),), -0.2, 0.2)), 0.5, 2.0)
    run_mean2 = scatter_about(arg_keys[14], (C,), 0.5, 3.0, ((0, 8),), jnp.float32)
    run_var2 = jnp.clip(jnp.exp(math.log(2.0) - 1.3862944 * jax.random.uniform(arg_keys[15], (C,), jnp.float32) ** steps_of(arg_keys[15], (C,), ((0, 8),), -0.2, 0.2)), 0.5, 2.0)
    return {"features": features, "counts": counts, "labels": labels, "teacher": teacher, "conv1_weight": conv1_weight, "bn1_gain": bn1_gain, "bn1_bias": bn1_bias, "conv2_weight": conv2_weight, "bn2_gain": bn2_gain, "bn2_bias": bn2_bias, "head_weight": head_weight, "head_bias": head_bias, "run_mean1": run_mean1, "run_var1": run_var1, "run_mean2": run_mean2, "run_var2": run_var2}


epsilon = 1e-05
softening_heat = 4.0
target_weight = 1.0
other_weight = 8.0
loss_scale = 1024.0
momentum = 0.1
highest = lax.Precision.HIGHEST

@jax.custom_vjp
def low(v):
    return lax.optimization_barrier(v.astype(jnp.bfloat16)).astype(jnp.float32)

@jax.custom_vjp
def low_back(v):
    return v

def low_keep(v):
    return (low(v), None)

def low_pass(kept, grad):
    return (grad,)

def back_keep(v):
    return (v, None)

def back_low(kept, grad):
    return (low(grad),)
low.defvjp(low_keep, low_pass)
low_back.defvjp(back_keep, back_low)

def shifted_taps(field, sign):
    channels = field.shape[0]
    planes = field.reshape(channels, -1, SIDE, SIDE)
    padded = jnp.pad(planes, ((0, 0), (0, 0), (1, 1), (1, 1)))
    pieces = []
    for vertical in range(3):
        for lateral in range(3):
            row_start = 1 + sign * (vertical - 1)
            col_start = 1 + sign * (lateral - 1)
            pieces.append(padded[:, :, row_start:row_start + SIDE, col_start:col_start + SIDE].reshape(channels, -1))
    return jnp.stack(pieces)

def image_losses(class_logits, teacher, labels):
    onehot = (labels[:, None] == jnp.arange(class_logits.shape[1])[None, :]).astype(class_logits.dtype)
    cross = jax.nn.logsumexp(class_logits, axis=1) - lax.optimization_barrier(jnp.sum(onehot * class_logits, axis=1))
    pupil_network = class_logits / softening_heat
    mentor_network = teacher / softening_heat
    student_rest = pupil_network - 1000.0 * onehot
    tutor_rest = mentor_network - 1000.0 * onehot
    student_all = jax.nn.logsumexp(pupil_network, axis=1)
    tutor_all = jax.nn.logsumexp(mentor_network, axis=1)
    student_other = jax.nn.logsumexp(student_rest, axis=1)
    tutor_other = jax.nn.logsumexp(tutor_rest, axis=1)
    student_hit = lax.optimization_barrier(jnp.sum(onehot * pupil_network, axis=1)) - student_all
    tutor_hit = lax.optimization_barrier(jnp.sum(onehot * mentor_network, axis=1)) - tutor_all
    student_miss = student_other - student_all
    tutor_miss = tutor_other - tutor_all
    binary = jnp.exp(tutor_hit) * (tutor_hit - student_hit) + jnp.exp(tutor_miss) * (tutor_miss - student_miss)
    tutor_log = tutor_rest - tutor_other[:, None]
    student_log = student_rest - student_other[:, None]
    spread = lax.optimization_barrier(jnp.sum(jnp.exp(tutor_log) * (tutor_log - student_log), axis=1))
    squared_value = softening_heat * softening_heat
    return cross + squared_value * (target_weight * binary + other_weight * spread)

def batch_norm(field, gain, shift, live_cell, cells):
    mean = lax.optimization_barrier(jnp.sum(field * live_cell[None, :], axis=1)) / cells
    var = lax.optimization_barrier(jnp.sum(field * field * live_cell[None, :], axis=1)) / cells - mean * mean
    normed = (field - mean[:, None]) * lax.rsqrt(var + epsilon)[:, None]
    return (gain[:, None] * normed + shift[:, None], mean, var)

def reference(features, counts, labels, teacher, conv1_weight, bn1_gain, bn1_bias, conv2_weight, bn2_gain, bn2_bias, head_weight, head_bias, run_mean1, run_var1, run_mean2, run_var2):
    image_total = labels.shape[0]
    slots = jnp.arange(image_total).astype(jnp.int32)
    owners = (slots // IMG_DEV).astype(jnp.int32)
    live_img = (slots % IMG_DEV < counts[owners]).astype(jnp.float32)
    live_cell = jnp.repeat(live_img, SIDE * SIDE)
    image_batch = jnp.sum(counts).astype(jnp.float32)
    cells = image_batch * (SIDE * SIDE)
    teacher_f = teacher.astype(jnp.float32)

    def forward(inputs, weight_one, gain_one, bias_one, weight_two, gain_two, bias_two, head_w, head_b):
        first = low_back(jnp.einsum('otc,tcn->on', weight_one, shifted_taps(inputs, 1), precision=highest))
        pre1, mean1, var1 = batch_norm(first, gain_one, bias_one, live_cell, cells)
        hidden = low(jax.nn.silu(pre1))
        second = low_back(jnp.einsum('otc,tcn->on', weight_two, shifted_taps(hidden, 1), precision=highest))
        normed2, mean2, var2 = batch_norm(second, gain_two, bias_two, live_cell, cells)
        block_out = jax.nn.silu(normed2 + inputs)
        pooled = lax.optimization_barrier(jnp.mean(block_out.reshape(block_out.shape[0], image_total, SIDE * SIDE), axis=2))
        class_logits = jnp.einsum('cm,ck->mk', pooled, head_w, precision=highest) + head_b[None, :]
        per_image = image_losses(class_logits, teacher_f, labels)
        loss = jnp.sum(live_img * per_image) / image_batch
        return (loss, (mean1, var1, mean2, var2))
    float_args = tuple((value.astype(jnp.float32) for value in (features, conv1_weight, bn1_gain, bn1_bias, conv2_weight, bn2_gain, bn2_bias, head_weight, head_bias)))
    loss, pullback, stats = jax.vjp(forward, *float_args, has_aux=True)
    grads = pullback(jnp.full_like(loss, loss_scale))
    mean1, var1, mean2, var2 = stats
    bias_adjustment = cells / (cells - 1.0)
    new_mean1 = (1.0 - momentum) * run_mean1 + momentum * mean1
    new_var1 = (1.0 - momentum) * run_var1 + momentum * var1 * bias_adjustment
    new_mean2 = (1.0 - momentum) * run_mean2 + momentum * mean2
    new_var2 = (1.0 - momentum) * run_var2 + momentum * var2 * bias_adjustment
    return (loss, grads[0], grads[1], grads[2], grads[3], grads[4], grads[5], grads[6], grads[7], grads[8], new_mean1, new_var1, new_mean2, new_var2)
```

```python
import functools

import jax
import jax.numpy as jnp
from jax import lax
from jax.experimental import pallas as pl
from jax.experimental.pallas import tpu as pltpu
from jax.sharding import PartitionSpec as P

SIDE = 8


epsilon = 1e-05
softening_heat = 4.0
target_weight = 1.0
other_weight = 8.0
loss_scale = 1024.0
momentum = 0.1
highest = lax.Precision.HIGHEST


def shifted_taps(field, sign):
    channels = field.shape[0]
    planes = field.reshape(channels, -1, SIDE, SIDE)
    padded = jnp.pad(planes, ((0, 0), (0, 0), (1, 1), (1, 1)))
    pieces = []
    for vertical in range(3):
        for lateral in range(3):
            row_start = 1 + sign * (vertical - 1)
            col_start = 1 + sign * (lateral - 1)
            pieces.append(
                padded[:, :, row_start : row_start + SIDE, col_start : col_start + SIDE].reshape(
                    channels, -1
                )
            )
    return jnp.stack(pieces)


def image_losses(class_logits, teacher, labels):
    onehot = (labels[:, None] == jnp.arange(class_logits.shape[1])[None, :]).astype(
        class_logits.dtype
    )
    cross = jax.nn.logsumexp(class_logits, axis=1) - jnp.sum(onehot * class_logits, axis=1)
    pupil_network = class_logits / softening_heat
    mentor_network = teacher / softening_heat
    student_rest = pupil_network - 1000.0 * onehot
    tutor_rest = mentor_network - 1000.0 * onehot
    student_all = jax.nn.logsumexp(pupil_network, axis=1)
    tutor_all = jax.nn.logsumexp(mentor_network, axis=1)
    student_other = jax.nn.logsumexp(student_rest, axis=1)
    tutor_other = jax.nn.logsumexp(tutor_rest, axis=1)
    student_hit = jnp.sum(onehot * pupil_network, axis=1) - student_all
    tutor_hit = jnp.sum(onehot * mentor_network, axis=1) - tutor_all
    student_miss = student_other - student_all
    tutor_miss = tutor_other - tutor_all
    binary = jnp.exp(tutor_hit) * (tutor_hit - student_hit) + jnp.exp(tutor_miss) * (
        tutor_miss - student_miss
    )
    tutor_log = tutor_rest - tutor_other[:, None]
    student_log = student_rest - student_other[:, None]
    spread = jnp.sum(jnp.exp(tutor_log) * (tutor_log - student_log), axis=1)
    squared_value = softening_heat * softening_heat
    return cross + squared_value * (target_weight * binary + other_weight * spread)


def silu_slope(values):
    sigma = jax.nn.sigmoid(values)
    return sigma * (1.0 + values * (1.0 - sigma))


def conv_piece(weight, piece):
    return jnp.einsum(
        "otc,tcn->on", weight, shifted_taps(piece, 1), preferred_element_type=jnp.float32
    )


def weight_piece(grad_low, piece):
    return jnp.einsum(
        "on,tcn->otc", grad_low, shifted_taps(piece, 1), preferred_element_type=jnp.float32
    )


def input_piece(weight, back_taps):
    return jnp.einsum("otc,ton->cn", weight, back_taps, preferred_element_type=jnp.float32)


def plain_device(
    features,
    counts,
    labels,
    teacher,
    conv1_weight,
    bn1_gain,
    bn1_bias,
    conv2_weight,
    bn2_gain,
    bn2_bias,
    head_weight,
    head_bias,
    run_mean1,
    run_var1,
    run_mean2,
    run_var2,
):
    channels, cell_count = features.shape
    image_area = SIDE * SIDE
    image_slots = cell_count // image_area
    image_present = (lax.broadcasted_iota(jnp.int32, (image_slots,), 0) < counts[0]).astype(
        jnp.float32
    )
    cell_live = jnp.broadcast_to(image_present[:, None], (image_slots, image_area)).reshape(-1)
    residual_in = features.astype(jnp.float32)
    first = conv_piece(conv1_weight, lax.all_gather(features, "mp", axis=0, tiled=True))
    first_sum, first_square, cells = lax.psum(
        (
            jnp.sum(first * cell_live[None, :], axis=1),
            jnp.sum(first * first * cell_live[None, :], axis=1),
            jnp.sum(cell_live),
        ),
        "batch",
    )
    mean1 = first_sum / cells
    var1 = first_square / cells - mean1 * mean1
    rstd1 = lax.rsqrt(var1 + epsilon)
    normed1 = (first - mean1[:, None]) * rstd1[:, None]
    pre1 = bn1_gain[:, None] * normed1 + bn1_bias[:, None]
    hidden = jax.nn.silu(pre1).astype(jnp.bfloat16)
    second = conv_piece(conv2_weight, lax.all_gather(hidden, "mp", axis=0, tiled=True))
    second_sum, second_square = lax.psum(
        (
            jnp.sum(second * cell_live[None, :], axis=1),
            jnp.sum(second * second * cell_live[None, :], axis=1),
        ),
        "batch",
    )
    mean2 = second_sum / cells
    var2 = second_square / cells - mean2 * mean2
    rstd2 = lax.rsqrt(var2 + epsilon)
    normed2 = (second - mean2[:, None]) * rstd2[:, None]
    pre2 = bn2_gain[:, None] * normed2 + bn2_bias[:, None] + residual_in
    block_out = jax.nn.silu(pre2)
    pooled = jnp.mean(block_out.reshape(channels, image_slots, image_area), axis=2)
    head_local = head_weight.astype(jnp.float32)
    partial_logits = jnp.einsum("cm,ck->mk", pooled, head_local, precision=highest)
    class_logits = lax.psum(partial_logits, "mp") + head_bias[None, :]
    image_batch = cells / image_area

    def losses_of(values):
        return image_losses(values, teacher, labels)

    per_image, pullback = jax.vjp(losses_of, class_logits)
    loss_part = jnp.sum(image_present * per_image)
    (grad_logits,) = pullback(image_present * (loss_scale / image_batch))
    head_grad = jnp.einsum("cm,mk->ck", pooled, grad_logits, precision=highest)
    head_bias_grad = jnp.sum(grad_logits, axis=0)
    grad_pooled = jnp.einsum("mk,ck->cm", grad_logits, head_local, precision=highest) / image_area
    grad_out = jnp.broadcast_to(
        grad_pooled[:, :, None], (channels, image_slots, image_area)
    ).reshape(channels, -1)
    grad_pre2 = grad_out * silu_slope(pre2)
    loss_total = lax.psum(loss_part, "batch")
    bias2_grad, gain2_grad = lax.psum(
        (jnp.sum(grad_pre2, axis=1), jnp.sum(grad_pre2 * normed2, axis=1)), "batch"
    )
    loss = loss_total / image_batch
    grad_second = (bn2_gain * rstd2)[:, None] * (
        grad_pre2
        - cell_live[None, :] * (bias2_grad[:, None] + normed2 * gain2_grad[:, None]) / cells
    )
    second_low = grad_second.astype(jnp.bfloat16)
    conv2_grad = weight_piece(second_low, lax.all_gather(hidden, "mp", axis=0, tiled=True))
    back_second = shifted_taps(second_low, -1)
    grad_hidden = lax.psum_scatter(
        input_piece(conv2_weight, back_second), "mp", scatter_dimension=0, tiled=True
    )
    grad_pre1 = grad_hidden * silu_slope(pre1)
    bias1_grad, gain1_grad = lax.psum(
        (jnp.sum(grad_pre1, axis=1), jnp.sum(grad_pre1 * normed1, axis=1)), "batch"
    )
    grad_first = (bn1_gain * rstd1)[:, None] * (
        grad_pre1
        - cell_live[None, :] * (bias1_grad[:, None] + normed1 * gain1_grad[:, None]) / cells
    )
    first_low = grad_first.astype(jnp.bfloat16)
    conv1_grad = weight_piece(first_low, lax.all_gather(features, "mp", axis=0, tiled=True))
    back_first = shifted_taps(first_low, -1)
    input_term = lax.psum_scatter(
        input_piece(conv1_weight, back_first), "mp", scatter_dimension=0, tiled=True
    )
    grad_features = input_term + grad_pre2
    conv1_grad, conv2_grad, head_grad, head_bias_grad = lax.psum(
        (conv1_grad, conv2_grad, head_grad, head_bias_grad), "batch"
    )
    bias_adjustment = cells / (cells - 1.0)
    new_mean1 = (1.0 - momentum) * run_mean1 + momentum * mean1
    new_var1 = (1.0 - momentum) * run_var1 + momentum * var1 * bias_adjustment
    new_mean2 = (1.0 - momentum) * run_mean2 + momentum * mean2
    new_var2 = (1.0 - momentum) * run_var2 + momentum * var2 * bias_adjustment
    return (
        loss,
        grad_features,
        conv1_grad,
        gain1_grad,
        bias1_grad,
        conv2_grad,
        gain2_grad,
        bias2_grad,
        head_grad,
        head_bias_grad,
        new_mean1,
        new_var1,
        new_mean2,
        new_var2,
    )


MESH = pl.DeviceIdType.MESH
F32 = jnp.float32
BF16 = jnp.bfloat16
LANES = 128
PLANE = 2


def nn(a, b, precision=None):
    return lax.dot_general(
        a, b, (((1,), (0,)), ((), ())), precision=precision, preferred_element_type=F32
    )


def nt(a, b, precision=None):
    return lax.dot_general(
        a, b, (((1,), (1,)), ((), ())), precision=precision, preferred_element_type=F32
    )


def tn(a, b, precision=None):
    return lax.dot_general(
        a, b, (((0,), (0,)), ((), ())), precision=precision, preferred_element_type=F32
    )


def rows_first(field, images):
    return jnp.concatenate(
        [
            field[(m * SIDE + i) * SIDE : (m * SIDE + i + 1) * SIDE]
            for i in range(SIDE)
            for m in range(images)
        ]
    )


def images_first(field, images):
    return jnp.concatenate(
        [
            field[(i * images + m) * SIDE : (i * images + m + 1) * SIDE]
            for m in range(images)
            for i in range(SIDE)
        ]
    )


def store_taps(put, field, block):
    cells, width = field.shape
    tiles = field.reshape(cells // SIDE, SIDE, width)
    column = lax.broadcasted_iota(jnp.int32, tiles.shape, 1)
    left = jnp.where(column == 0, 0.0, pltpu.roll(tiles, 1, 1)).reshape(cells, width)
    right = jnp.where(column == SIDE - 1, 0.0, pltpu.roll(tiles, SIDE - 1, 1)).reshape(
        cells, width
    )
    for lateral, shifted in enumerate((left, field, right)):
        put(lateral, pl.ds(block, cells), shifted.astype(BF16))


def row_sum(field):
    return jnp.sum(field, axis=0, keepdims=True)


def halves(row):
    return [row[:, at : at + LANES] for at in range(0, row.shape[1], LANES)]


def image_terms(logits, teacher, labels):
    def parts(values):
        top = jnp.max(values, axis=1, keepdims=True)
        weights = jnp.exp(values - top)
        total = jnp.sum(weights, axis=1, keepdims=True)
        return top + jnp.log(total), weights / total

    onehot = (
        labels == lax.broadcasted_iota(jnp.int32, logits.shape, 1)
    ).astype(F32)
    full_lse, full_soft = parts(logits)
    pupil = logits / softening_heat
    mentor = teacher / softening_heat
    pupil_rest = pupil - 1000.0 * onehot
    mentor_rest = mentor - 1000.0 * onehot
    pupil_all, pupil_soft = parts(pupil)
    mentor_all, _ = parts(mentor)
    pupil_other, pupil_rest_soft = parts(pupil_rest)
    mentor_other, mentor_rest_soft = parts(mentor_rest)

    def pick(values):
        return jnp.sum(onehot * values, axis=1, keepdims=True)

    pupil_hit = pick(pupil) - pupil_all
    mentor_hit = pick(mentor) - mentor_all
    pupil_miss = pupil_other - pupil_all
    mentor_miss = mentor_other - mentor_all
    hit_weight, miss_weight = jnp.exp(mentor_hit), jnp.exp(mentor_miss)
    binary = hit_weight * (mentor_hit - pupil_hit) + miss_weight * (
        mentor_miss - pupil_miss
    )
    gap = (mentor_rest - mentor_other) - (pupil_rest - pupil_other)
    spread = jnp.sum(mentor_rest_soft * gap, axis=1, keepdims=True)
    squared = softening_heat * softening_heat
    value = (
        full_lse
        - pick(logits)
        + squared * (target_weight * binary + other_weight * spread)
    )
    binary_slope = (
        (hit_weight + miss_weight) * pupil_soft
        - hit_weight * onehot
        - miss_weight * pupil_rest_soft
    )
    spread_slope = pupil_rest_soft - mentor_rest_soft
    slope = (
        full_soft
        - onehot
        + softening_heat
        * (target_weight * binary_slope + other_weight * spread_slope)
    )
    return value, slope


def block_kernel(
    sizes,
    features,
    counts,
    labels,
    teacher,
    conv1,
    conv2,
    head_weight,
    head_bias,
    *rest,
):
    params, rest = rest[:8], rest[8:]
    (
        out_features,
        out_conv1,
        out_conv2,
        out_small,
        weight1,
        weight2,
        teacher_here,
        labels_here,
        head_here,
        head_bias_here,
        params_here,
        cells_in,
        params_all,
        counts_all,
        head_all,
        sums_all,
        logit_stage,
        logit_all,
        field,
        normed1,
        slope1,
        normed2,
        grad_pre2,
        taps_x,
        taps_h,
        taps_g,
        raw_x,
        raw_h,
        layer_x,
        layer_h,
        grad_stage,
        grad_all,
        column_part,
        column_stage,
        column_all,
        mean_all,
        edge_part,
        edge_all,
        quarter_all,
        cells_stage,
        cells_out,
        load_sem,
        send_sem,
        sums_send,
        sums_recv,
        logit_send,
        logit_recv,
        cells_recv,
        params_recv,
        counts_recv,
        head_recv,
        weight_recv,
        raw_recv,
        grad_recv,
        column_recv,
        mean_recv,
        edge_recv,
        quarter_recv,
        out_recv,
    ) = rest
    n_batch, n_mp, channels, images = sizes
    n_z = n_mp // PLANE
    width = channels // n_mp
    quarter = width // n_batch
    block = images * SIDE
    cells = block * SIDE
    everyone = n_batch * n_mp
    b, p = lax.axis_index("batch"), lax.axis_index("mp")
    x, c = b // PLANE, b % PLANE
    z, y = p // PLANE, p % PLANE
    me = b * n_mp + p
    seat = y * n_batch + b
    tall = column_part.shape[2]
    means_end_value = {}
    sent = []

    def send(src, dst, recv, to_b, to_p):
        copy = pltpu.make_async_remote_copy(
            src_ref=src,
            dst_ref=dst,
            send_sem=send_sem.at[len(sent)],
            recv_sem=recv,
            device_id=(to_b, to_p),
            device_id_type=MESH,
        )
        copy.start()
        sent.append(copy)

    def await_bytes(ref, sem):
        pltpu.make_async_copy(ref, ref, sem).wait()

    others = [
        ((b + j) % n_batch, (p + k) % n_mp)
        for k in range(n_mp)
        for j in range(n_batch)
        if j or k
    ]

    loads = [
        (conv1, weight1.at[:, pl.ds(pl.multiple_of(p * width, width), width), :]),
        (conv2, weight2.at[:, pl.ds(pl.multiple_of(p * width, width), width), :]),
        (teacher, teacher_here),
        (labels, labels_here),
        (head_weight, head_here),
        (head_bias, head_bias_here),
    ] + [(ref, params_here.at[i]) for i, ref in enumerate(params)]
    loads = [
        pltpu.make_async_copy(src, dst, load_sem.at[i])
        for i, (src, dst) in enumerate(loads)
    ]
    for load in loads:
        load.start()
    barrier = pltpu.get_barrier_semaphore()
    for to_b, to_p in others:
        pl.semaphore_signal(
            barrier, inc=1, device_id=(to_b, to_p), device_id_type=MESH
        )

    for taps in (taps_x, taps_h, taps_g):
        for lateral in range(3):
            taps[lateral, 0:block] = jnp.zeros((block, channels), BF16)
            taps[lateral, block + cells : 2 * block + cells] = jnp.zeros(
                (block, channels), BF16
            )
    for layer in (layer_x, layer_h):
        for s in range(n_batch * PLANE):
            for lateral in range(3):
                layer[s, lateral, 0:block] = jnp.zeros((block, channels), BF16)
                layer[s, lateral, block + cells : 2 * block + cells] = jnp.zeros(
                    (block, channels), BF16
                )
    for load in loads:
        load.wait()
    group = LANES // width
    place = pl.multiple_of((p % group) * width, width)
    own_params = jnp.concatenate(
        [params_here[i] for i in range(4)] + [jnp.zeros((4, width), F32)]
    )
    own_params = jnp.concatenate(
        [own_params, jnp.zeros((8, LANES - width), F32)], axis=1
    )
    params_all[p] = pltpu.roll(own_params, place, 1)
    count = counts[0]
    counts_all[b] = jnp.zeros((8, LANES), F32) + count.astype(F32)
    head_all[p] = head_here[...]

    pl.semaphore_wait(barrier, everyone - 1)

    half = pl.ds(pl.multiple_of(c * LANES, LANES), LANES)
    strip = width // PLANE

    def rows_of(at_z, at_y, at_x):
        start = (at_z * PLANE + at_y) * width + at_x * strip
        return pl.ds(pl.multiple_of(start, strip), strip)

    far = [lambda v: n_z - 1 - v, lambda v: (v + n_z // 2) % n_z]
    if n_z == 4:
        far.append(lambda v: v + 1 - 2 * (v % 2))
    mates = [(1, 1), (1, 0), (0, 1)]

    def column_start(which, weight):
        part = weight.at[:, rows_of(z, y, x), half]
        for k, other in enumerate(far):
            send(part, part, weight_recv.at[which, k], b, other(z) * PLANE + y)

    def shard_start(which, weight):
        part = weight.at[
            :, pl.ds(pl.multiple_of(p * width, width), width), half
        ]
        send(part, part, weight_recv.at[which, 3], b, z * PLANE + 1 - y)

    def layer_start(which, weight):
        for k, other in enumerate(far):
            part = weight.at[:, rows_of(other(z), y, x), half]
            await_bytes(part, weight_recv.at[which, k])
            for i, (dx, dy) in enumerate(mates):
                send(
                    part,
                    part,
                    weight_recv.at[which, 4 + 3 * k + i],
                    ((x + dx) % 2) * PLANE + c,
                    z * PLANE + (y + dy) % 2,
                )

    def core_start(which, weight):
        part = weight.at[
            :,
            pl.ds(
                pl.multiple_of((z * PLANE + 1 - y) * width, width), width
            ),
            half,
        ]
        await_bytes(part, weight_recv.at[which, 3])
        send(part, part, weight_recv.at[which, 13], x * PLANE + 1 - c, p)
        for k, other in enumerate(far):
            for i, (dx, dy) in enumerate(mates):
                part = weight.at[
                    :, rows_of(other(z), (y + dy) % 2, (x + dx) % 2), half
                ]
                await_bytes(part, weight_recv.at[which, 4 + 3 * k + i])
            part = weight.at[
                :,
                pl.ds(
                    pl.multiple_of(other(z) * PLANE * width, PLANE * width),
                    PLANE * width,
                ),
                half,
            ]
            send(part, part, weight_recv.at[which, 14 + k], x * PLANE + 1 - c, p)

    def core_end(which, weight):
        theirs = pl.ds(pl.multiple_of((1 - c) * LANES, LANES), LANES)
        part = weight.at[
            :,
            pl.ds(
                pl.multiple_of((z * PLANE + 1 - y) * width, width), width
            ),
            theirs,
        ]
        await_bytes(part, weight_recv.at[which, 13])
        for k, other in enumerate(far):
            part = weight.at[
                :,
                pl.ds(
                    pl.multiple_of(other(z) * PLANE * width, PLANE * width),
                    PLANE * width,
                ),
                theirs,
            ]
            await_bytes(part, weight_recv.at[which, 14 + k])

    column_start(0, weight1)
    shard_start(0, weight1)

    def cells_of(q):
        return pl.ds(pl.multiple_of(q * cells, cells), cells)

    own_cells = pltpu.make_async_copy(
        features.at[:, cells_of(p)], cells_in.at[p], load_sem.at[0]
    )
    own_cells.start()
    for k in range(1, n_mp):
        q = (p + k) % n_mp
        send(features.at[:, cells_of(q)], cells_in.at[p], cells_recv.at[k], b, q)
    for k in range(1, n_mp):
        q = (p + k) % n_mp
        send(params_all.at[p], params_all.at[p], params_recv.at[k], b, q)
        send(head_all.at[p], head_all.at[p], head_recv.at[k], b, q)
    for j in range(1, n_batch):
        send(
            counts_all.at[b],
            counts_all.at[b],
            counts_recv.at[j],
            (b + j) % n_batch,
            p,
        )

    layer_start(0, weight1)
    column_start(1, weight2)
    own_cells.wait()
    for k in range(1, n_mp):
        q = (p + n_mp - k) % n_mp
        await_bytes(cells_in.at[q], cells_recv.at[k])
    by_channel = cells_in[...].reshape(channels, cells).astype(F32)
    by_cell = rows_first(by_channel.T, images)
    field[...] = by_cell

    def put_x(lateral, where, value):
        taps_x[lateral, where] = value

    store_taps(put_x, by_cell, block)
    raw_x[seat] = by_cell.astype(BF16)

    core_start(0, weight1)

    for k in range(1, n_mp):
        q = (p + n_mp - k) % n_mp
        await_bytes(params_all.at[q], params_recv.at[k])
        await_bytes(head_all.at[q], head_recv.at[k])
    for j in range(1, n_batch):
        await_bytes(counts_all.at[(b + n_batch - j) % n_batch], counts_recv.at[j])
    full_params = jnp.concatenate(
        [
            sum(params_all[q] for q in range(at, at + group))
            for at in range(0, n_mp, group)
        ],
        axis=1,
    )
    gain1, bias1, gain2, bias2 = (full_params[i : i + 1] for i in range(4))
    live_images = sum(counts_all[i] for i in range(n_batch))[0:1, 0:1]
    live_cells = live_images * float(SIDE * SIDE)

    slot = (lax.broadcasted_iota(jnp.int32, (cells, channels), 0) // SIDE) % images
    live = (slot + p * images < count).astype(F32)

    shape = (cells, LANES)
    cell = lax.broadcasted_iota(jnp.int32, shape, 0)
    tap_at = lax.broadcasted_iota(jnp.int32, shape, 1)
    down = (tap_at >= 3).astype(jnp.int32) + (tap_at >= 6).astype(jnp.int32)
    across = tap_at - 3 * down
    at_row = cell // block + down - 1
    at_column = cell % SIDE + across - 1
    within = (at_row >= 0) & (at_row < SIDE) & (at_column >= 0) & (at_column < SIDE)
    inside = jnp.where(within & (tap_at < 9), 1.0, 0.0).astype(BF16)

    def conv(taps, weight):
        total = None
        for tap in range(9):
            vertical, lateral = divmod(tap, 3)
            term = nt(
                taps[lateral, block * vertical : block * vertical + cells],
                weight[tap],
            )
            total = term if total is None else total + term
        return total

    def conv_back(taps, weight):
        total = None
        for tap in range(9):
            vertical, lateral = divmod(tap, 3)
            up = block * (2 - vertical)
            term = nn(taps[2 - lateral, up : up + cells], weight[tap])
            total = term if total is None else total + term
        return total

    def sums_start(which, one, two):
        mine = sums_all.at[which, me, pl.ds(0, 4)]
        sums_all[which, me, 0:4] = jnp.concatenate(halves(one) + halves(two))
        for to_b, to_p in reversed(others):
            pltpu.make_async_remote_copy(
                src_ref=mine,
                dst_ref=mine,
                send_sem=sums_send.at[which],
                recv_sem=sums_recv.at[which],
                device_id=(to_b, to_p),
                device_id_type=MESH,
            ).start()

    def sums_end(which):
        everything = sums_all.at[which, pl.ds(0, everyone - 1), pl.ds(0, 4)]
        await_bytes(everything, sums_recv.at[which])
        total = jnp.sum(sums_all[which], axis=0)
        return (
            jnp.concatenate([total[0:1], total[1:2]], axis=1),
            jnp.concatenate([total[2:3], total[3:4]], axis=1),
        )

    def means_start(which, value):
        mean_all[which, z] = jnp.concatenate(
            halves(row_sum(value) / float(cells))
            + [jnp.zeros((8 - channels // LANES, LANES), F32)]
        )
        part = mean_all.at[which, z]
        for k, other in enumerate(far):
            send(part, part, mean_recv.at[which, k], b, other(z) * PLANE + y)

    def means_end(which):
        for k, other in enumerate(far):
            await_bytes(mean_all.at[which, other(z)], mean_recv.at[which, k])
        total = sum(mean_all[which, at_z] for at_z in range(n_z)) / float(n_z)
        return jnp.concatenate(
            [total[i : i + 1] for i in range(channels // LANES)], axis=1
        )

    def raw_start(which, raw):
        part = raw.at[seat]
        for i, (dx, dy) in enumerate(mates):
            send(
                part,
                part,
                raw_recv.at[which, i],
                ((x + dx) % 2) * PLANE + c,
                z * PLANE + (y + dy) % 2,
            )
        send(part, part, raw_recv.at[which, 3], x * PLANE + 1 - c, p)

    def seat_of(dx, dy, dc):
        return ((y + dy) % 2) * n_batch + ((x + dx) % 2) * PLANE + (c + dc) % 2

    def raw_forward(which, raw):
        for i, (dx, dy) in enumerate(mates):
            part = raw.at[seat_of(dx, dy, 0)]
            await_bytes(part, raw_recv.at[which, i])
            send(part, part, raw_recv.at[which, 4 + i], x * PLANE + 1 - c, p)

    def raw_end(which, raw, layer):
        await_bytes(raw.at[seat_of(0, 0, 1)], raw_recv.at[which, 3])
        for i, (dx, dy) in enumerate(mates):
            await_bytes(raw.at[seat_of(dx, dy, 1)], raw_recv.at[which, 4 + i])

        def build(s, carry):
            def put(lateral, where, value):
                layer[s, lateral, where] = value

            store_taps(put, raw[s].astype(F32), block)
            return carry

        lax.fori_loop(0, n_batch * PLANE, build, 0)

    seats = [
        (dx, dy, dc)
        for dy in (1, 0)
        for dx in (1, 0)
        for dc in (1, 0)
        if dx or dy or dc
    ]

    def grads_start(which, grad):
        by_row = grad.T
        for s in range(n_batch * PLANE):
            at_y, at_b = divmod(s, n_batch)
            grad_stage[which, s] = jnp.concatenate(
                [
                    by_row[start : start + quarter]
                    for start in (
                        (at_z * PLANE + at_y) * width + at_b * quarter
                        for at_z in range(n_z)
                    )
                ]
            ).astype(BF16)
        for i, (dx, dy, dc) in enumerate(seats):
            send(
                grad_stage.at[which, seat_of(dx, dy, dc)],
                grad_all.at[which, seat],
                grad_recv.at[which, i],
                ((x + dx) % 2) * PLANE + (c + dc) % 2,
                z * PLANE + (y + dy) % 2,
            )
        grad_all[which, seat] = grad_stage[which, seat]

    def grads_end(which, layer):
        for i, (dx, dy, dc) in enumerate(seats):
            await_bytes(grad_all.at[which, seat_of(dx, dy, dc)], grad_recv.at[which, i])
        mean = means_end(1 - which)
        means_end_value[which] = mean
        edges = sum(nn(grad_all[which, s], inside) for s in range(n_batch * PLANE))
        for at_z in range(n_z):
            edge_part[which, at_z] = edges[at_z * quarter : (at_z + 1) * quarter]
        for tap in range(9):
            vertical, lateral = divmod(tap, 3)
            total = -edges[:, tap : tap + 1] * mean
            for s in range(n_batch * PLANE):
                term = nn(
                    grad_all[which, s],
                    layer[s, lateral, block * vertical : block * vertical + cells],
                )
                total = total + term
            for at_z in range(n_z):
                column_part[which, at_z, tap * quarter : (tap + 1) * quarter] = total[
                    at_z * quarter : (at_z + 1) * quarter
                ]
        for at_z in range(n_z):
            column_stage[which, at_z] = column_part[which, at_z].astype(BF16)
        for k, other in enumerate(far):
            send(
                column_stage.at[which, other(z)],
                column_all.at[which, k],
                column_recv.at[which, k],
                b,
                other(z) * PLANE + y,
            )
            send(
                edge_part.at[which, other(z)],
                edge_all.at[which, k],
                edge_recv.at[which, k],
                b,
                other(z) * PLANE + y,
            )

    def quarters_start(which):
        for k in range(len(far)):
            await_bytes(column_all.at[which, k], column_recv.at[which, k])
            await_bytes(edge_all.at[which, k], edge_recv.at[which, k])
        mean = means_end_value[which]
        edges = edge_part[which, z]
        total = column_part[which, z]
        for k in range(len(far)):
            edges = edges + edge_all[which, k]
            total = total + column_all[which, k].astype(F32)
        back = jnp.concatenate(
            [edges[:, tap : tap + 1] * mean for tap in range(9)]
            + [jnp.zeros((tall - 9 * quarter, channels), F32)]
        )
        quarter_all[which, b] = (total + back).astype(BF16)
        for j in range(1, n_batch):
            part = quarter_all.at[which, b]
            send(part, part, quarter_recv.at[which, j], (b + j) % n_batch, p)

    def quarters_end(which, out):
        for j in range(1, n_batch):
            await_bytes(
                quarter_all.at[which, (b + n_batch - j) % n_batch],
                quarter_recv.at[which, j],
            )
        for at_b in range(n_batch):
            whole = quarter_all[which, at_b].astype(F32)
            for tap in range(9):
                out[tap, at_b * quarter : (at_b + 1) * quarter] = whole[
                    tap * quarter : (tap + 1) * quarter
                ]

    for which in range(2):
        for at_z in range(n_z):
            column_part[which, at_z, 9 * quarter :] = jnp.zeros(
                (tall - 9 * quarter, channels), F32
            )

    means_start(0, by_cell)
    core_end(0, weight1)
    first = conv(taps_x, weight1)
    masked = first * live
    sums_start(0, row_sum(masked), row_sum(masked * first))
    shard_start(1, weight2)
    layer_start(1, weight2)
    total, square = sums_end(0)
    mean1 = total / live_cells
    var1 = square / live_cells - mean1 * mean1
    rstd1 = lax.rsqrt(var1 + epsilon)
    flat = (first - mean1) * rstd1
    normed1[...] = flat
    pre1 = gain1 * flat + bias1
    sigma1 = jax.nn.sigmoid(pre1)
    slope1[...] = sigma1 * (1.0 + pre1 * (1.0 - sigma1))
    hidden = pre1 * sigma1

    def put_h(lateral, where, value):
        taps_h[lateral, where] = value

    store_taps(put_h, hidden, block)
    raw_h[seat] = hidden.astype(BF16)
    means_start(1, hidden)
    core_start(1, weight2)
    core_end(1, weight2)

    second = conv(taps_h, weight2)
    masked = second * live
    sums_start(1, row_sum(masked), row_sum(masked * second))
    raw_start(1, raw_h)
    total, square = sums_end(1)
    mean2 = total / live_cells
    var2 = square / live_cells - mean2 * mean2
    rstd2 = lax.rsqrt(var2 + epsilon)
    flat2 = (second - mean2) * rstd2
    normed2[...] = flat2
    pre2 = gain2 * flat2 + bias2 + field[...]
    sigma2 = jax.nn.sigmoid(pre2)
    block_out = pre2 * sigma2

    pooled = sum(block_out[i * block : (i + 1) * block] for i in range(SIDE))
    pooled = jnp.sum(pooled.reshape(images, SIDE, channels), axis=1) / float(
        SIDE * SIDE
    )
    head = head_all[...].reshape(channels, head_all.shape[2]).astype(F32)
    logits = nn(pooled, head, highest) + head_bias_here[...]
    slots = labels_here.shape[1]
    image_at = lax.broadcasted_iota(jnp.int32, (images, slots), 0) + p * images
    picked = lax.broadcasted_iota(jnp.int32, (images, slots), 1) == image_at
    own_labels = jnp.sum(
        jnp.where(picked, labels_here[...], 0), axis=1, keepdims=True
    )
    own_teacher = nn(picked.astype(F32), teacher_here[...], highest)
    own_live = (image_at[:, 0:1] < count).astype(F32)
    per_image, slope = image_terms(logits, own_teacher, own_labels)
    grad_logits = slope * (own_live * (loss_scale / live_images))
    grad_pooled = nt(grad_logits, head, highest) / float(SIDE * SIDE)
    spread = jnp.concatenate(
        [
            jnp.broadcast_to(grad_pooled[m : m + 1], (SIDE, channels))
            for m in range(images)
        ]
    )
    spread = jnp.concatenate([spread] * SIDE)
    pre_grad2 = spread * (sigma2 * (1.0 + pre2 * (1.0 - sigma2)))
    grad_pre2[...] = pre_grad2
    sums_start(2, row_sum(pre_grad2), row_sum(pre_grad2 * flat2))

    raw_start(0, raw_x)
    raw_forward(1, raw_h)
    raw_end(1, raw_h, layer_h)

    bias_grad2, gain_grad2 = sums_end(2)
    grad_second = (gain2 * rstd2) * (
        grad_pre2[...]
        - live * (bias_grad2 + normed2[...] * gain_grad2) / live_cells
    )
    grads_start(0, grad_second)

    def put_g(lateral, where, value):
        taps_g[lateral, where] = value

    store_taps(put_g, grad_second.astype(BF16).astype(F32), block)
    pre_grad1 = conv_back(taps_g, weight2) * slope1[...]
    sums_start(3, row_sum(pre_grad1), row_sum(pre_grad1 * normed1[...]))
    classes = logits.shape[1]
    for q in range(n_mp):
        logit_stage[q] = jnp.zeros((2 * images, LANES), F32)
        logit_stage[q, 0:images, 0:classes] = grad_logits
        logit_stage[q, 0:images, classes : classes + 1] = own_live * per_image
        logit_stage[q, images : 2 * images, 0:width] = pooled[
            :, q * width : (q + 1) * width
        ]
    for to_b, to_p in others:
        pltpu.make_async_remote_copy(
            src_ref=logit_stage.at[to_p],
            dst_ref=logit_all.at[me],
            send_sem=logit_send,
            recv_sem=logit_recv,
            device_id=(to_b, to_p),
            device_id_type=MESH,
        ).start()
    logit_all[me] = logit_stage[p]
    grads_end(0, layer_h)
    raw_forward(0, raw_x)
    raw_end(0, raw_x, layer_x)
    bias_grad1, gain_grad1 = sums_end(3)
    grad_first = (gain1 * rstd1) * (
        pre_grad1 - live * (bias_grad1 + normed1[...] * gain_grad1) / live_cells
    )
    grads_start(1, grad_first)
    store_taps(put_g, grad_first.astype(BF16).astype(F32), block)
    grad_in = conv_back(taps_g, weight1) + grad_pre2[...]
    cells_stage[...] = (
        images_first(grad_in, images).T.astype(BF16).reshape(n_mp, width, cells)
    )
    for k in range(1, n_mp):
        q = (p + k) % n_mp
        send(cells_stage.at[q], cells_out.at[p], out_recv.at[k], b, q)
    cells_out[p] = cells_stage[p]
    grads_end(1, layer_x)
    quarters_start(0)
    quarters_start(1)

    def own(row):
        pieces = halves(row)
        mine = pieces[0]
        for i in range(1, len(pieces)):
            mine = jnp.where(p // group == i, pieces[i], mine)
        return pltpu.roll(mine, (LANES - place) % LANES, 1)[:, 0:width]

    adjust = live_cells / (live_cells - 1.0)
    kept = 1.0 - momentum
    rows = [
        own(gain_grad1),
        own(bias_grad1),
        own(gain_grad2),
        own(bias_grad2),
        kept * params_here[4] + momentum * own(mean1),
        kept * params_here[5] + momentum * own(var1 * adjust),
        kept * params_here[6] + momentum * own(mean2),
        kept * params_here[7] + momentum * own(var2 * adjust),
    ]
    out_small[...] = jnp.zeros_like(out_small)
    for i, row in enumerate(rows):
        out_small[i : i + 1, 0:width] = row
    await_bytes(logit_all.at[pl.ds(0, everyone - 1)], logit_recv)
    tall = logit_all[...]
    upper = lax.broadcasted_iota(jnp.int32, tall.shape, 1) < images
    upper_logits = jnp.where(upper, tall, 0.0).reshape(-1, LANES)
    lifted = jnp.where(upper, pltpu.roll(tall, images, 1), 0.0).reshape(-1, LANES)
    out_small[16 : 16 + width] = tn(lifted, upper_logits, highest)[0:width]
    columns = row_sum(upper_logits)
    out_small[8:9] = columns
    out_small[9:10] = jnp.broadcast_to(
        columns[:, classes : classes + 1] / live_images, (1, LANES)
    )

    quarters_end(0, out_conv2)
    for k in range(1, n_mp):
        q = (p + n_mp - k) % n_mp
        await_bytes(cells_out.at[q], out_recv.at[k])
    for q in range(n_mp):
        out_features[:, q * cells : (q + 1) * cells] = cells_out[q].astype(F32)
    quarters_end(1, out_conv1)

    for copy in sent:
        copy.wait_send()
    for which in range(4):
        await_bytes(
            sums_all.at[which, pl.ds(0, everyone - 1), pl.ds(0, 4)],
            sums_send.at[which],
        )
    await_bytes(logit_all.at[pl.ds(0, everyone - 1)], logit_send)


def finish_kernel(
    features_in,
    conv1_in,
    conv2_in,
    small,
    loss,
    features_out,
    conv1_out,
    gain1_out,
    bias1_out,
    conv2_out,
    gain2_out,
    bias2_out,
    head_out,
    head_bias_out,
    *stats_out,
):
    features_out[...] = features_in[...]
    conv1_out[...] = conv1_in[...]
    conv2_out[...] = conv2_in[...]
    vectors = (gain1_out, bias1_out, gain2_out, bias2_out) + stats_out
    for i, out in enumerate(vectors):
        out[...] = small[i : i + 1, 0 : out.shape[1]]
    head_bias_out[...] = small[8:9, 0 : head_bias_out.shape[1]]
    loss[0] = small[9, 0]
    head_out[...] = small[16 : 16 + head_out.shape[0], 0 : head_out.shape[1]]


def block_device(
    n_batch,
    n_mp,
    features,
    counts,
    labels,
    teacher,
    conv1_weight,
    bn1_gain,
    bn1_bias,
    conv2_weight,
    bn2_gain,
    bn2_bias,
    head_weight,
    head_bias,
    run_mean1,
    run_var1,
    run_mean2,
    run_var2,
):
    width, cell_count = features.shape
    channels = width * n_mp
    classes = head_weight.shape[1]
    slots = cell_count // (SIDE * SIDE)
    images = slots // n_mp
    block = images * SIDE
    cells = block * SIDE
    n_z = n_mp // PLANE
    quarter = width // n_batch
    seats = n_batch * PLANE
    everyone = n_batch * n_mp
    tall = -(-9 * quarter // 16) * 16
    padded = cells + 2 * block

    def row(values):
        return values.reshape(1, -1)

    def taps_out(values):
        return values.transpose(1, 0, 2)

    def vmem(*shape, dtype=F32):
        return pltpu.VMEM(shape, dtype)

    def low(*shape):
        return pltpu.VMEM(shape, BF16)

    any_space = pl.BlockSpec(memory_space=pl.ANY)
    in_vmem = pl.BlockSpec(memory_space=pltpu.VMEM)
    in_smem = pl.BlockSpec(memory_space=pltpu.SMEM)
    shape = jax.ShapeDtypeStruct
    dma = pltpu.SemaphoreType.DMA
    grant = pltpu.CompilerParams(
        collective_id=0, has_side_effects=True, vmem_limit_bytes=60 * 2**20
    )
    packed = pl.pallas_call(
        functools.partial(block_kernel, (n_batch, n_mp, channels, images)),
        out_shape=(
            shape((width, cell_count), F32),
            shape((9, width, channels), F32),
            shape((9, width, channels), F32),
            shape((16 + width, LANES), F32),
        ),
        in_specs=[any_space, in_smem] + [any_space] * 14,
        out_specs=(in_vmem,) * 4,
        scratch_shapes=[
            low(9, channels, channels),
            low(9, channels, channels),
            vmem(slots, classes),
            vmem(1, slots, dtype=jnp.int32),
            low(width, classes),
            vmem(1, classes),
            vmem(8, 1, width),
            low(n_mp, width, cells),
            vmem(n_mp, 8, LANES),
            vmem(n_batch, 8, LANES),
            low(n_mp, width, classes),
            vmem(4, everyone, 8, LANES),
            vmem(n_mp, 2 * images, LANES),
            vmem(everyone, 2 * images, LANES),
            vmem(cells, channels),
            vmem(cells, channels),
            vmem(cells, channels),
            vmem(cells, channels),
            vmem(cells, channels),
            low(3, padded, channels),
            low(3, padded, channels),
            low(3, padded, channels),
            low(seats, cells, channels),
            low(seats, cells, channels),
            low(seats, 3, padded, channels),
            low(seats, 3, padded, channels),
            low(2, seats, n_z * quarter, cells),
            low(2, seats, n_z * quarter, cells),
            vmem(2, n_z, tall, channels),
            low(2, n_z, tall, channels),
            low(2, n_z - 1, tall, channels),
            vmem(2, n_z, 8, LANES),
            vmem(2, n_z, quarter, LANES),
            vmem(2, n_z - 1, quarter, LANES),
            low(2, n_batch, tall, channels),
            low(n_mp, width, cells),
            low(n_mp, width, cells),
            dma((14,)),
            dma((128,)),
            dma((4,)),
            dma((4,)),
            dma,
            dma,
            dma((n_mp,)),
            dma((n_mp,)),
            dma((n_batch,)),
            dma((n_mp,)),
            dma((2, 17)),
            dma((2, 7)),
            dma((2, 7)),
            dma((2, n_z - 1)),
            dma((2, n_z - 1)),
            dma((2, n_z - 1)),
            dma((2, n_batch)),
            dma((n_mp,)),
        ],
        compiler_params=grant,
    )(
        features,
        counts,
        row(labels),
        teacher,
        taps_out(conv1_weight),
        taps_out(conv2_weight),
        head_weight,
        row(head_bias),
        row(bn1_gain),
        row(bn1_bias),
        row(bn2_gain),
        row(bn2_bias),
        row(run_mean1),
        row(run_var1),
        row(run_mean2),
        row(run_var2),
    )
    vector = shape((1, width), F32)
    results = pl.pallas_call(
        finish_kernel,
        out_shape=(
            shape((1,), F32),
            shape((width, cell_count), F32),
            shape((9, width, channels), F32),
            vector,
            vector,
            shape((9, width, channels), F32),
            vector,
            vector,
            shape((width, classes), F32),
            shape((1, classes), F32),
            vector,
            vector,
            vector,
            vector,
        ),
        in_specs=[in_vmem] * 4,
        out_specs=(in_smem,) + (in_vmem,) * 13,
        compiler_params=pltpu.CompilerParams(vmem_limit_bytes=60 * 2**20),
    )(*packed)
    loss, grad_features, conv1, gain1, bias1, conv2, gain2, bias2, head, *small = results
    return (
        loss.reshape(()),
        grad_features,
        taps_out(conv1),
        gain1.reshape(-1),
        bias1.reshape(-1),
        taps_out(conv2),
        gain2.reshape(-1),
        bias2.reshape(-1),
        head,
    ) + tuple(values.reshape(-1) for values in small)


def by_images(n_batch, n_mp, features, counts, *rest):
    width, cell_count = features.shape
    images = cell_count // (SIDE * SIDE) // n_mp
    fits = (
        n_batch == 4
        and n_mp == 8
        and width == 32
        and images == 4
        and head_fits(rest)
    )
    if not fits:
        return plain_device(features, counts, *rest)
    return block_device(n_batch, n_mp, features, counts, *rest)


def head_fits(rest):
    return rest[8].shape[1] < LANES


def solution(mesh):
    return jax.shard_map(
        functools.partial(by_images, mesh.shape["batch"], mesh.shape["mp"]),
        mesh=mesh,
        in_specs=(
            P("mp", "batch"),
            P("batch"),
            P("batch"),
            P("batch", None),
            P("mp", None, None),
            P("mp"),
            P("mp"),
            P("mp", None, None),
            P("mp"),
            P("mp"),
            P("mp", None),
            P(),
            P("mp"),
            P("mp"),
            P("mp"),
            P("mp"),
        ),
        out_specs=(
            P(),
            P("mp", "batch"),
            P("mp", None, None),
            P("mp"),
            P("mp"),
            P("mp", None, None),
            P("mp"),
            P("mp"),
            P("mp", None),
            P(),
            P("mp"),
            P("mp"),
            P("mp"),
            P("mp"),
        ),
        check_vma=False,
    )
```

```python
import functools

import jax
import jax.numpy as jnp
from jax import lax
from jax.experimental import pallas as pl
from jax.experimental.pallas import tpu as pltpu
from jax.sharding import PartitionSpec as P

SIDE = 8


epsilon = 1e-05
softening_heat = 4.0
target_weight = 1.0
other_weight = 8.0
loss_scale = 1024.0
momentum = 0.1
highest = lax.Precision.HIGHEST


def shifted_taps(field, sign):
    channels = field.shape[0]
    planes = field.reshape(channels, -1, SIDE, SIDE)
    padded = jnp.pad(planes, ((0, 0), (0, 0), (1, 1), (1, 1)))
    pieces = []
    for vertical in range(3):
        for lateral in range(3):
            row_start = 1 + sign * (vertical - 1)
            col_start = 1 + sign * (lateral - 1)
            pieces.append(
                padded[:, :, row_start : row_start + SIDE, col_start : col_start + SIDE].reshape(
                    channels, -1
                )
            )
    return jnp.stack(pieces)


def image_losses(class_logits, teacher, labels):
    onehot = (labels[:, None] == jnp.arange(class_logits.shape[1])[None, :]).astype(
        class_logits.dtype
    )
    cross = jax.nn.logsumexp(class_logits, axis=1) - jnp.sum(onehot * class_logits, axis=1)
    pupil_network = class_logits / softening_heat
    mentor_network = teacher / softening_heat
    student_rest = pupil_network - 1000.0 * onehot
    tutor_rest = mentor_network - 1000.0 * onehot
    student_all = jax.nn.logsumexp(pupil_network, axis=1)
    tutor_all = jax.nn.logsumexp(mentor_network, axis=1)
    student_other = jax.nn.logsumexp(student_rest, axis=1)
    tutor_other = jax.nn.logsumexp(tutor_rest, axis=1)
    student_hit = jnp.sum(onehot * pupil_network, axis=1) - student_all
    tutor_hit = jnp.sum(onehot * mentor_network, axis=1) - tutor_all
    student_miss = student_other - student_all
    tutor_miss = tutor_other - tutor_all
    binary = jnp.exp(tutor_hit) * (tutor_hit - student_hit) + jnp.exp(tutor_miss) * (
        tutor_miss - student_miss
    )
    tutor_log = tutor_rest - tutor_other[:, None]
    student_log = student_rest - student_other[:, None]
    spread = jnp.sum(jnp.exp(tutor_log) * (tutor_log - student_log), axis=1)
    squared_value = softening_heat * softening_heat
    return cross + squared_value * (target_weight * binary + other_weight * spread)


def silu_slope(values):
    sigma = jax.nn.sigmoid(values)
    return sigma * (1.0 + values * (1.0 - sigma))


def conv_piece(weight, piece):
    return jnp.einsum(
        "otc,tcn->on", weight, shifted_taps(piece, 1), preferred_element_type=jnp.float32
    )


def weight_piece(grad_low, piece):
    return jnp.einsum(
        "on,tcn->otc", grad_low, shifted_taps(piece, 1), preferred_element_type=jnp.float32
    )


def input_piece(weight, back_taps):
    return jnp.einsum("otc,ton->cn", weight, back_taps, preferred_element_type=jnp.float32)


def plain_device(
    features,
    counts,
    labels,
    teacher,
    conv1_weight,
    bn1_gain,
    bn1_bias,
    conv2_weight,
    bn2_gain,
    bn2_bias,
    head_weight,
    head_bias,
    run_mean1,
    run_var1,
    run_mean2,
    run_var2,
):
    channels, cell_count = features.shape
    image_area = SIDE * SIDE
    image_slots = cell_count // image_area
    image_present = (lax.broadcasted_iota(jnp.int32, (image_slots,), 0) < counts[0]).astype(
        jnp.float32
    )
    cell_live = jnp.broadcast_to(image_present[:, None], (image_slots, image_area)).reshape(-1)
    residual_in = features.astype(jnp.float32)
    first = conv_piece(conv1_weight, lax.all_gather(features, "mp", axis=0, tiled=True))
    first_sum, first_square, cells = lax.psum(
        (
            jnp.sum(first * cell_live[None, :], axis=1),
            jnp.sum(first * first * cell_live[None, :], axis=1),
            jnp.sum(cell_live),
        ),
        "batch",
    )
    mean1 = first_sum / cells
    var1 = first_square / cells - mean1 * mean1
    rstd1 = lax.rsqrt(var1 + epsilon)
    normed1 = (first - mean1[:, None]) * rstd1[:, None]
    pre1 = bn1_gain[:, None] * normed1 + bn1_bias[:, None]
    hidden = jax.nn.silu(pre1).astype(jnp.bfloat16)
    second = conv_piece(conv2_weight, lax.all_gather(hidden, "mp", axis=0, tiled=True))
    second_sum, second_square = lax.psum(
        (
            jnp.sum(second * cell_live[None, :], axis=1),
            jnp.sum(second * second * cell_live[None, :], axis=1),
        ),
        "batch",
    )
    mean2 = second_sum / cells
    var2 = second_square / cells - mean2 * mean2
    rstd2 = lax.rsqrt(var2 + epsilon)
    normed2 = (second - mean2[:, None]) * rstd2[:, None]
    pre2 = bn2_gain[:, None] * normed2 + bn2_bias[:, None] + residual_in
    block_out = jax.nn.silu(pre2)
    pooled = jnp.mean(block_out.reshape(channels, image_slots, image_area), axis=2)
    head_local = head_weight.astype(jnp.float32)
    partial_logits = jnp.einsum("cm,ck->mk", pooled, head_local, precision=highest)
    class_logits = lax.psum(partial_logits, "mp") + head_bias[None, :]
    image_batch = cells / image_area

    def losses_of(values):
        return image_losses(values, teacher, labels)

    per_image, pullback = jax.vjp(losses_of, class_logits)
    loss_part = jnp.sum(image_present * per_image)
    (grad_logits,) = pullback(image_present * (loss_scale / image_batch))
    head_grad = jnp.einsum("cm,mk->ck", pooled, grad_logits, precision=highest)
    head_bias_grad = jnp.sum(grad_logits, axis=0)
    grad_pooled = jnp.einsum("mk,ck->cm", grad_logits, head_local, precision=highest) / image_area
    grad_out = jnp.broadcast_to(
        grad_pooled[:, :, None], (channels, image_slots, image_area)
    ).reshape(channels, -1)
    grad_pre2 = grad_out * silu_slope(pre2)
    loss_total = lax.psum(loss_part, "batch")
    bias2_grad, gain2_grad = lax.psum(
        (jnp.sum(grad_pre2, axis=1), jnp.sum(grad_pre2 * normed2, axis=1)), "batch"
    )
    loss = loss_total / image_batch
    grad_second = (bn2_gain * rstd2)[:, None] * (
        grad_pre2
        - cell_live[None, :] * (bias2_grad[:, None] + normed2 * gain2_grad[:, None]) / cells
    )
    second_low = grad_second.astype(jnp.bfloat16)
    conv2_grad = weight_piece(second_low, lax.all_gather(hidden, "mp", axis=0, tiled=True))
    back_second = shifted_taps(second_low, -1)
    grad_hidden = lax.psum_scatter(
        input_piece(conv2_weight, back_second), "mp", scatter_dimension=0, tiled=True
    )
    grad_pre1 = grad_hidden * silu_slope(pre1)
    bias1_grad, gain1_grad = lax.psum(
        (jnp.sum(grad_pre1, axis=1), jnp.sum(grad_pre1 * normed1, axis=1)), "batch"
    )
    grad_first = (bn1_gain * rstd1)[:, None] * (
        grad_pre1
        - cell_live[None, :] * (bias1_grad[:, None] + normed1 * gain1_grad[:, None]) / cells
    )
    first_low = grad_first.astype(jnp.bfloat16)
    conv1_grad = weight_piece(first_low, lax.all_gather(features, "mp", axis=0, tiled=True))
    back_first = shifted_taps(first_low, -1)
    input_term = lax.psum_scatter(
        input_piece(conv1_weight, back_first), "mp", scatter_dimension=0, tiled=True
    )
    grad_features = input_term + grad_pre2
    conv1_grad, conv2_grad, head_grad, head_bias_grad = lax.psum(
        (conv1_grad, conv2_grad, head_grad, head_bias_grad), "batch"
    )
    bias_adjustment = cells / (cells - 1.0)
    new_mean1 = (1.0 - momentum) * run_mean1 + momentum * mean1
    new_var1 = (1.0 - momentum) * run_var1 + momentum * var1 * bias_adjustment
    new_mean2 = (1.0 - momentum) * run_mean2 + momentum * mean2
    new_var2 = (1.0 - momentum) * run_var2 + momentum * var2 * bias_adjustment
    return (
        loss,
        grad_features,
        conv1_grad,
        gain1_grad,
        bias1_grad,
        conv2_grad,
        gain2_grad,
        bias2_grad,
        head_grad,
        head_bias_grad,
        new_mean1,
        new_var1,
        new_mean2,
        new_var2,
    )


MESH = pl.DeviceIdType.MESH
F32 = jnp.float32
BF16 = jnp.bfloat16
LANES = 128
PLANE = 2


def nn(a, b, precision=None):
    return lax.dot_general(
        a, b, (((1,), (0,)), ((), ())), precision=precision, preferred_element_type=F32
    )


def nt(a, b, precision=None):
    return lax.dot_general(
        a, b, (((1,), (1,)), ((), ())), precision=precision, preferred_element_type=F32
    )


def tn(a, b, precision=None):
    return lax.dot_general(
        a, b, (((0,), (0,)), ((), ())), precision=precision, preferred_element_type=F32
    )


def rows_first(field, images):
    return jnp.concatenate(
        [
            field[(m * SIDE + i) * SIDE : (m * SIDE + i + 1) * SIDE]
            for i in range(SIDE)
            for m in range(images)
        ]
    )


def images_first(field, images):
    return jnp.concatenate(
        [
            field[(i * images + m) * SIDE : (i * images + m + 1) * SIDE]
            for m in range(images)
            for i in range(SIDE)
        ]
    )


def store_taps(put, field, block):
    cells, width = field.shape
    tiles = field.reshape(cells // SIDE, SIDE, width)
    column = lax.broadcasted_iota(jnp.int32, tiles.shape, 1)
    left = jnp.where(column == 0, 0.0, pltpu.roll(tiles, 1, 1)).reshape(cells, width)
    right = jnp.where(column == SIDE - 1, 0.0, pltpu.roll(tiles, SIDE - 1, 1)).reshape(
        cells, width
    )
    for lateral, shifted in enumerate((left, field, right)):
        put(lateral, pl.ds(block, cells), shifted.astype(BF16))


def row_sum(field):
    return jnp.sum(field, axis=0, keepdims=True)


def halves(row):
    return [row[:, at : at + LANES] for at in range(0, row.shape[1], LANES)]


def image_terms(logits, teacher, labels):
    def parts(values):
        top = jnp.max(values, axis=1, keepdims=True)
        weights = jnp.exp(values - top)
        total = jnp.sum(weights, axis=1, keepdims=True)
        return top + jnp.log(total), weights / total

    onehot = (
        labels == lax.broadcasted_iota(jnp.int32, logits.shape, 1)
    ).astype(F32)
    full_lse, full_soft = parts(logits)
    pupil = logits / softening_heat
    mentor = teacher / softening_heat
    pupil_rest = pupil - 1000.0 * onehot
    mentor_rest = mentor - 1000.0 * onehot
    pupil_all, pupil_soft = parts(pupil)
    mentor_all, _ = parts(mentor)
    pupil_other, pupil_rest_soft = parts(pupil_rest)
    mentor_other, mentor_rest_soft = parts(mentor_rest)

    def pick(values):
        return jnp.sum(onehot * values, axis=1, keepdims=True)

    pupil_hit = pick(pupil) - pupil_all
    mentor_hit = pick(mentor) - mentor_all
    pupil_miss = pupil_other - pupil_all
    mentor_miss = mentor_other - mentor_all
    hit_weight, miss_weight = jnp.exp(mentor_hit), jnp.exp(mentor_miss)
    binary = hit_weight * (mentor_hit - pupil_hit) + miss_weight * (
        mentor_miss - pupil_miss
    )
    gap = (mentor_rest - mentor_other) - (pupil_rest - pupil_other)
    spread = jnp.sum(mentor_rest_soft * gap, axis=1, keepdims=True)
    squared = softening_heat * softening_heat
    value = (
        full_lse
        - pick(logits)
        + squared * (target_weight * binary + other_weight * spread)
    )
    binary_slope = (
        (hit_weight + miss_weight) * pupil_soft
        - hit_weight * onehot
        - miss_weight * pupil_rest_soft
    )
    spread_slope = pupil_rest_soft - mentor_rest_soft
    slope = (
        full_soft
        - onehot
        + softening_heat
        * (target_weight * binary_slope + other_weight * spread_slope)
    )
    return value, slope


def block_kernel(
    sizes,
    features,
    counts,
    labels,
    teacher,
    conv1,
    conv2,
    head_weight,
    head_bias,
    *rest,
):
    params, rest = rest[:8], rest[8:]
    (
        out_features,
        out_conv1,
        out_conv2,
        out_small,
        weight1,
        weight2,
        teacher_here,
        labels_here,
        head_here,
        head_bias_here,
        params_here,
        cells_in,
        params_all,
        counts_all,
        head_all,
        sums_all,
        logit_stage,
        logit_all,
        head_part,
        field,
        normed1,
        slope1,
        normed2,
        grad_pre2,
        taps_x,
        taps_h,
        taps_g,
        raw_x,
        raw_h,
        strip_taps,
        live_taps,
        live_rows,
        norm_part,
        norm_edges,
        live_part,
        live_edges,
        columns,
        strip_stage,
        strip_all,
        column_part,
        column_stage,
        column_all,
        mean_all,
        edge_part,
        edge_all,
        quarter_all,
        cells_stage,
        cells_out,
        load_sem,
        send_sem,
        sums_send,
        sums_recv,
        logit_recv,
        head_part_recv,
        cells_recv,
        params_recv,
        counts_recv,
        head_recv,
        weight_recv,
        raw_recv,
        strip_recv,
        column_recv,
        mean_recv,
        edge_recv,
        quarter_recv,
        out_recv,
    ) = rest
    n_batch, n_mp, channels, images = sizes
    n_z = n_mp // PLANE
    width = channels // n_mp
    quarter = width // n_batch
    block = images * SIDE
    cells = block * SIDE
    everyone = n_batch * n_mp
    b, p = lax.axis_index("batch"), lax.axis_index("mp")
    x, c = b // PLANE, b % PLANE
    z, y = p // PLANE, p % PLANE
    me = b * n_mp + p
    seat = y * n_batch + b
    n_seats = PLANE * n_batch
    tall = column_part.shape[2]
    means_end_value = {}
    sent = []

    def send(src, dst, recv, to_b, to_p):
        copy = pltpu.make_async_remote_copy(
            src_ref=src,
            dst_ref=dst,
            send_sem=send_sem.at[len(sent)],
            recv_sem=recv,
            device_id=(to_b, to_p),
            device_id_type=MESH,
        )
        copy.start()
        sent.append(copy)

    def await_bytes(ref, sem):
        pltpu.make_async_copy(ref, ref, sem).wait()

    others = [
        ((b + j) % n_batch, (p + k) % n_mp)
        for k in range(n_mp)
        for j in range(n_batch)
        if j or k
    ]

    loads = [
        (conv1, weight1.at[:, pl.ds(pl.multiple_of(p * width, width), width), :]),
        (conv2, weight2.at[:, pl.ds(pl.multiple_of(p * width, width), width), :]),
        (teacher, teacher_here),
        (labels, labels_here),
        (head_weight, head_here),
        (head_bias, head_bias_here),
    ] + [(ref, params_here.at[i]) for i, ref in enumerate(params)]
    loads = [
        pltpu.make_async_copy(src, dst, load_sem.at[i])
        for i, (src, dst) in enumerate(loads)
    ]
    for load in loads:
        load.start()
    barrier = pltpu.get_barrier_semaphore()
    for to_b, to_p in others:
        pl.semaphore_signal(
            barrier, inc=1, device_id=(to_b, to_p), device_id_type=MESH
        )

    for taps in (taps_x, taps_h, taps_g):
        for lateral in range(3):
            taps[lateral, 0:block] = jnp.zeros((block, channels), BF16)
            taps[lateral, block + cells : 2 * block + cells] = jnp.zeros(
                (block, channels), BF16
            )
    for load in loads:
        load.wait()
    group = LANES // width
    place = pl.multiple_of((p % group) * width, width)
    own_params = jnp.concatenate(
        [params_here[i] for i in range(4)] + [jnp.zeros((4, width), F32)]
    )
    own_params = jnp.concatenate(
        [own_params, jnp.zeros((8, LANES - width), F32)], axis=1
    )
    params_all[p] = pltpu.roll(own_params, place, 1)
    count = counts[0]
    counts_all[b] = jnp.zeros((8, LANES), F32) + count.astype(F32)
    head_all[p] = jnp.concatenate(
        [
            head_here[...],
            jnp.zeros((width, LANES - head_here.shape[1]), BF16),
        ],
        axis=1,
    )

    pl.semaphore_wait(barrier, everyone - 1)

    half = pl.ds(pl.multiple_of(c * LANES, LANES), LANES)
    strip = width // PLANE

    def rows_of(at_z, at_y, at_x):
        start = (at_z * PLANE + at_y) * width + at_x * strip
        return pl.ds(pl.multiple_of(start, strip), strip)

    far = [
        lambda v: v + 1 - 2 * (v % 2),
        lambda v: (v + n_z // 2) % n_z,
        lambda v: n_z - 1 - v,
    ]
    mates = [(1, 1), (1, 0), (0, 1)]

    def column_start(which, weight):
        part = weight.at[:, rows_of(z, y, x), half]
        for k, other in enumerate(far):
            send(part, part, weight_recv.at[which, k], b, other(z) * PLANE + y)

    def shard_start(which, weight):
        part = weight.at[
            :, pl.ds(pl.multiple_of(p * width, width), width), half
        ]
        send(part, part, weight_recv.at[which, 3], b, z * PLANE + 1 - y)

    def layer_start(which, weight):
        for k, other in enumerate(far):
            part = weight.at[:, rows_of(other(z), y, x), half]
            await_bytes(part, weight_recv.at[which, k])
            for i, (dx, dy) in enumerate(mates):
                send(
                    part,
                    part,
                    weight_recv.at[which, 4 + 3 * k + i],
                    ((x + dx) % 2) * PLANE + c,
                    z * PLANE + (y + dy) % 2,
                )

    def core_start(which, weight):
        part = weight.at[
            :,
            pl.ds(
                pl.multiple_of((z * PLANE + 1 - y) * width, width), width
            ),
            half,
        ]
        await_bytes(part, weight_recv.at[which, 3])
        send(part, part, weight_recv.at[which, 13], x * PLANE + 1 - c, p)
        for k, other in enumerate(far):
            for i, (dx, dy) in enumerate(mates):
                part = weight.at[
                    :, rows_of(other(z), (y + dy) % 2, (x + dx) % 2), half
                ]
                await_bytes(part, weight_recv.at[which, 4 + 3 * k + i])
            part = weight.at[
                :,
                pl.ds(
                    pl.multiple_of(other(z) * PLANE * width, PLANE * width),
                    PLANE * width,
                ),
                half,
            ]
            send(part, part, weight_recv.at[which, 14 + k], x * PLANE + 1 - c, p)

    def core_end(which, weight):
        theirs = pl.ds(pl.multiple_of((1 - c) * LANES, LANES), LANES)
        part = weight.at[
            :,
            pl.ds(
                pl.multiple_of((z * PLANE + 1 - y) * width, width), width
            ),
            theirs,
        ]
        await_bytes(part, weight_recv.at[which, 13])
        for k, other in enumerate(far):
            part = weight.at[
                :,
                pl.ds(
                    pl.multiple_of(other(z) * PLANE * width, PLANE * width),
                    PLANE * width,
                ),
                theirs,
            ]
            await_bytes(part, weight_recv.at[which, 14 + k])

    column_start(0, weight1)
    shard_start(0, weight1)

    def cells_of(q):
        return pl.ds(pl.multiple_of(q * cells, cells), cells)

    own_cells = pltpu.make_async_copy(
        features.at[:, cells_of(p)], cells_in.at[p], load_sem.at[0]
    )
    own_cells.start()
    for k in range(1, n_mp):
        q = (p + k) % n_mp
        send(features.at[:, cells_of(q)], cells_in.at[p], cells_recv.at[k], b, q)
    column_start(1, weight2)
    for k in range(1, n_mp):
        q = (p + k) % n_mp
        send(params_all.at[p], params_all.at[p], params_recv.at[k], b, q)
        send(head_all.at[p], head_all.at[p], head_recv.at[k], b, q)
    for j in range(1, n_batch):
        send(
            counts_all.at[b],
            counts_all.at[b],
            counts_recv.at[j],
            (b + j) % n_batch,
            p,
        )

    layer_start(0, weight1)
    own_cells.wait()
    for k in range(1, n_mp):
        q = (p + n_mp - k) % n_mp
        await_bytes(cells_in.at[q], cells_recv.at[k])
    by_channel = cells_in[...].reshape(channels, cells).astype(F32)
    by_cell = rows_first(by_channel.T, images)
    field[...] = by_cell

    def put_x(lateral, where, value):
        taps_x[lateral, where] = value

    store_taps(put_x, by_cell, block)
    raw_x[seat] = by_cell.astype(BF16)

    shard_start(1, weight2)
    layer_start(1, weight2)
    core_start(0, weight1)

    for k in range(1, n_mp):
        q = (p + n_mp - k) % n_mp
        await_bytes(params_all.at[q], params_recv.at[k])
        await_bytes(head_all.at[q], head_recv.at[k])
    for j in range(1, n_batch):
        await_bytes(counts_all.at[(b + n_batch - j) % n_batch], counts_recv.at[j])
    full_params = jnp.concatenate(
        [
            sum(params_all[q] for q in range(at, at + group))
            for at in range(0, n_mp, group)
        ],
        axis=1,
    )
    gain1, bias1, gain2, bias2 = (full_params[i : i + 1] for i in range(4))
    live_images = sum(counts_all[i] for i in range(n_batch))[0:1, 0:1]
    live_cells = live_images * float(SIDE * SIDE)

    slot = (lax.broadcasted_iota(jnp.int32, (cells, channels), 0) // SIDE) % images
    live = (slot + p * images < count).astype(F32)

    shape = (cells, LANES)
    cell = lax.broadcasted_iota(jnp.int32, shape, 0)
    tap_at = lax.broadcasted_iota(jnp.int32, shape, 1)
    down = (tap_at >= 3).astype(jnp.int32) + (tap_at >= 6).astype(jnp.int32)
    across = tap_at - 3 * down
    at_row = cell // block + down - 1
    at_column = cell % SIDE + across - 1
    within = (at_row >= 0) & (at_row < SIDE) & (at_column >= 0) & (at_column < SIDE)
    inside = jnp.where(within & (tap_at < 9), 1.0, 0.0).astype(BF16)

    def conv(taps, weight):
        total = None
        for tap in range(9):
            vertical, lateral = divmod(tap, 3)
            term = nt(
                taps[lateral, block * vertical : block * vertical + cells],
                weight[tap],
            )
            total = term if total is None else total + term
        return total

    def conv_back(taps, weight):
        total = None
        for tap in range(9):
            vertical, lateral = divmod(tap, 3)
            up = block * (2 - vertical)
            term = nn(taps[2 - lateral, up : up + cells], weight[tap])
            total = term if total is None else total + term
        return total

    def sums_start(which, one, two):
        mine = sums_all.at[which, me, pl.ds(0, 4)]
        sums_all[which, me, 0:4] = jnp.concatenate(halves(one) + halves(two))
        for to_b, to_p in reversed(others):
            pltpu.make_async_remote_copy(
                src_ref=mine,
                dst_ref=mine,
                send_sem=sums_send.at[which],
                recv_sem=sums_recv.at[which],
                device_id=(to_b, to_p),
                device_id_type=MESH,
            ).start()

    def sums_end(which):
        everything = sums_all.at[which, pl.ds(0, everyone - 1), pl.ds(0, 4)]
        await_bytes(everything, sums_recv.at[which])
        total = jnp.sum(sums_all[which], axis=0)
        return (
            jnp.concatenate([total[0:1], total[1:2]], axis=1),
            jnp.concatenate([total[2:3], total[3:4]], axis=1),
        )

    def means_start(which, value):
        mean_all[which, z] = jnp.concatenate(
            halves(row_sum(value) / float(cells))
            + [jnp.zeros((8 - channels // LANES, LANES), F32)]
        )
        part = mean_all.at[which, z]
        for k, other in enumerate(far):
            send(part, part, mean_recv.at[which, k], b, other(z) * PLANE + y)

    def means_end(which):
        for k, other in enumerate(far):
            await_bytes(mean_all.at[which, other(z)], mean_recv.at[which, k])
        total = sum(mean_all[which, at_z] for at_z in range(n_z)) / float(n_z)
        return jnp.concatenate(
            [total[i : i + 1] for i in range(channels // LANES)], axis=1
        )

    def raw_start(which, raw):
        part = raw.at[seat]
        for i, (dx, dy) in enumerate(mates):
            send(
                part,
                part,
                raw_recv.at[which, i],
                ((x + dx) % 2) * PLANE + c,
                z * PLANE + (y + dy) % 2,
            )
        send(part, part, raw_recv.at[which, 3], x * PLANE + 1 - c, p)

    def seat_of(dx, dy, dc):
        return ((y + dy) % 2) * n_batch + ((x + dx) % 2) * PLANE + (c + dc) % 2

    def raw_forward(which, raw):
        for i, (dx, dy) in enumerate(mates):
            part = raw.at[seat_of(dx, dy, 0)]
            await_bytes(part, raw_recv.at[which, i])
            send(part, part, raw_recv.at[which, 4 + i], x * PLANE + 1 - c, p)

    def raw_end(which, raw):
        await_bytes(raw.at[seat_of(0, 0, 1)], raw_recv.at[which, 3])
        for i, (dx, dy) in enumerate(mates):
            await_bytes(raw.at[seat_of(dx, dy, 1)], raw_recv.at[which, 4 + i])

    seats = [
        (dx, dy, dc)
        for dy in (1, 0)
        for dx in (1, 0)
        for dc in (1, 0)
        if dx or dy or dc
    ]

    def strips_start(which, value):
        by_row = value.T
        for s in range(n_seats):
            at_y, at_b = divmod(s, n_batch)
            strip_stage[which, s] = jnp.concatenate(
                [
                    by_row[start : start + quarter]
                    for start in (
                        (at_z * PLANE + at_y) * width + at_b * quarter
                        for at_z in range(n_z)
                    )
                ]
            ).astype(BF16)
        for i, (dx, dy, dc) in enumerate(seats):
            send(
                strip_stage.at[which, seat_of(dx, dy, dc)],
                strip_all.at[which, seat],
                strip_recv.at[which, i],
                ((x + dx) % 2) * PLANE + (c + dc) % 2,
                z * PLANE + (y + dy) % 2,
            )
        strip_all[which, seat] = strip_stage[which, seat]

    shape = (9, 1, cells)
    cell = lax.broadcasted_iota(jnp.int32, shape, 2)
    tap_at = lax.broadcasted_iota(jnp.int32, shape, 0)
    down = (tap_at >= 3).astype(jnp.int32) + (tap_at >= 6).astype(jnp.int32)
    from_row = cell // block - down + 1
    from_column = cell % SIDE - (tap_at - 3 * down) + 1
    reach = jnp.where(
        (from_row >= 0)
        & (from_row < SIDE)
        & (from_column >= 0)
        & (from_column < SIDE),
        1.0,
        0.0,
    )

    def moved(value, tap):
        vertical, lateral = divmod(tap, 3)
        ahead = (vertical - 1) * block + lateral - 1
        return (pltpu.roll(value, ahead % cells, 1) if ahead else value) * reach[tap]

    strips = n_z * quarter

    def strips_product(which, raw):
        for i, (dx, dy, dc) in enumerate(seats):
            await_bytes(
                strip_all.at[which, seat_of(dx, dy, dc)], strip_recv.at[which, i]
            )
        for s in range(n_seats):
            value = strip_all[which, s].astype(F32)
            for tap in range(9):
                strip_taps[
                    tap * strips : (tap + 1) * strips, s * cells : (s + 1) * cells
                ] = moved(value, tap).astype(BF16)
        edges = sum(nn(strip_all[which, s], inside) for s in range(n_seats))
        return nn(strip_taps[...], raw[...].reshape(-1, channels)), edges

    def live_of(at_y, at_b):
        lane = lax.broadcasted_iota(jnp.int32, (8, cells), 1)
        image = (lane // SIDE) % images + (z * PLANE + at_y) * images
        return (image.astype(F32) < counts_all[at_b][:, 0:1]).astype(F32)

    def norm_product(raw):
        for s in range(n_seats):
            alive = live_of(*divmod(s, n_batch))
            live_rows[s : s + 1] = alive[0:1].astype(F32)
            for tap in range(9):
                live_taps[tap : tap + 1, s * cells : (s + 1) * cells] = moved(
                    alive, tap
                )[0:1]
        product, edges = strips_product(2, raw)
        norm_part[...] = product
        norm_edges[...] = edges
        live_part[...] = nn(
            live_taps[...].astype(BF16), raw[...].reshape(-1, channels)
        )
        live_edges[...] = nn(live_rows[...].astype(BF16), inside)

    def own_column(row):
        columns[...] = jnp.broadcast_to(row, (LANES, channels)).T
        return jnp.concatenate(
            [
                columns[
                    pl.ds(
                        pl.multiple_of(
                            (at_z * PLANE + y) * width + b * quarter, quarter
                        ),
                        quarter,
                    ),
                    :,
                ]
                for at_z in range(n_z)
            ]
        )[:, 0:1]

    def column_send(which, product, edges, sums=None):
        if sums is not None:
            bias_column, gain_column = (own_column(row / live_cells) for row in sums)
            edges = edges - (
                bias_column * row_sum(live_edges[...]) + gain_column * norm_edges[...]
            )
        mean = means_end(1 - which)
        means_end_value[which] = mean
        for at_z in range(n_z):
            edge_part[which, at_z] = edges[at_z * quarter : (at_z + 1) * quarter]
        for tap in range(9):
            rows = slice(tap * strips, (tap + 1) * strips)
            total = product[rows] - edges[:, tap : tap + 1] * mean
            if sums is not None:
                total = total - (
                    bias_column * live_part[tap : tap + 1]
                    + gain_column * norm_part[rows]
                )
            for at_z in range(n_z):
                column_part[which, at_z, tap * quarter : (tap + 1) * quarter] = total[
                    at_z * quarter : (at_z + 1) * quarter
                ]
        for at_z in range(n_z):
            column_stage[which, at_z] = column_part[which, at_z].astype(BF16)
        for k, other in enumerate(far):
            send(
                column_stage.at[which, other(z)],
                column_all.at[which, k],
                column_recv.at[which, k],
                b,
                other(z) * PLANE + y,
            )
            send(
                edge_part.at[which, other(z)],
                edge_all.at[which, k],
                edge_recv.at[which, k],
                b,
                other(z) * PLANE + y,
            )

    def quarters_start(which):
        for k in range(len(far)):
            await_bytes(column_all.at[which, k], column_recv.at[which, k])
            await_bytes(edge_all.at[which, k], edge_recv.at[which, k])
        mean = means_end_value[which]
        edges = edge_part[which, z]
        total = column_part[which, z]
        for k in range(len(far)):
            edges = edges + edge_all[which, k]
            total = total + column_all[which, k].astype(F32)
        back = jnp.concatenate(
            [edges[:, tap : tap + 1] * mean for tap in range(9)]
            + [jnp.zeros((tall - 9 * quarter, channels), F32)]
        )
        quarter_all[which, b] = (total + back).astype(BF16)
        for j in range(1, n_batch):
            part = quarter_all.at[which, b]
            send(part, part, quarter_recv.at[which, j], (b + j) % n_batch, p)

    def quarters_end(which, out):
        for j in range(1, n_batch):
            await_bytes(
                quarter_all.at[which, (b + n_batch - j) % n_batch],
                quarter_recv.at[which, j],
            )
        for at_b in range(n_batch):
            whole = quarter_all[which, at_b].astype(F32)
            for tap in range(9):
                out[tap, at_b * quarter : (at_b + 1) * quarter] = whole[
                    tap * quarter : (tap + 1) * quarter
                ]

    live_taps[...] = jnp.zeros_like(live_taps)
    for which in range(2):
        for at_z in range(n_z):
            column_part[which, at_z, 9 * quarter :] = jnp.zeros(
                (tall - 9 * quarter, channels), F32
            )

    means_start(0, by_cell)
    core_end(0, weight1)
    first = conv(taps_x, weight1)
    masked = first * live
    sums_start(0, row_sum(masked), row_sum(masked * first))
    raw_start(0, raw_x)
    core_start(1, weight2)
    total, square = sums_end(0)
    mean1 = total / live_cells
    var1 = square / live_cells - mean1 * mean1
    rstd1 = lax.rsqrt(var1 + epsilon)
    flat = (first - mean1) * rstd1
    normed1[...] = flat
    pre1 = gain1 * flat + bias1
    sigma1 = jax.nn.sigmoid(pre1)
    slope1[...] = sigma1 * (1.0 + pre1 * (1.0 - sigma1))
    hidden = pre1 * sigma1

    def put_h(lateral, where, value):
        taps_h[lateral, where] = value

    store_taps(put_h, hidden, block)
    raw_h[seat] = hidden.astype(BF16)
    means_start(1, hidden)
    core_end(1, weight2)

    second = conv(taps_h, weight2)
    masked = second * live
    sums_start(1, row_sum(masked), row_sum(masked * second))
    raw_start(1, raw_h)
    strips_start(2, normed1[...] * live)
    raw_forward(0, raw_x)
    total, square = sums_end(1)
    mean2 = total / live_cells
    var2 = square / live_cells - mean2 * mean2
    rstd2 = lax.rsqrt(var2 + epsilon)
    flat2 = (second - mean2) * rstd2
    normed2[...] = flat2
    pre2 = gain2 * flat2 + bias2 + field[...]
    sigma2 = jax.nn.sigmoid(pre2)
    block_out = pre2 * sigma2

    pooled = sum(block_out[i * block : (i + 1) * block] for i in range(SIDE))
    pooled = jnp.sum(pooled.reshape(images, SIDE, channels), axis=1) / float(
        SIDE * SIDE
    )
    head = head_all[...].reshape(channels, LANES).astype(F32)[:, 0 : head_here.shape[1]]
    logits = nn(pooled, head, highest) + head_bias_here[...]
    slots = labels_here.shape[1]
    image_at = lax.broadcasted_iota(jnp.int32, (images, slots), 0) + p * images
    picked = lax.broadcasted_iota(jnp.int32, (images, slots), 1) == image_at
    own_labels = jnp.sum(
        jnp.where(picked, labels_here[...], 0), axis=1, keepdims=True
    )
    own_teacher = nn(picked.astype(F32), teacher_here[...], highest)
    own_live = (image_at[:, 0:1] < count).astype(F32)
    per_image, slope = image_terms(logits, own_teacher, own_labels)
    grad_logits = slope * (own_live * (loss_scale / live_images))
    grad_pooled = nt(grad_logits, head, highest) / float(SIDE * SIDE)
    spread = jnp.concatenate(
        [
            jnp.broadcast_to(grad_pooled[m : m + 1], (SIDE, channels))
            for m in range(images)
        ]
    )
    spread = jnp.concatenate([spread] * SIDE)
    pre_grad2 = spread * (sigma2 * (1.0 + pre2 * (1.0 - sigma2)))
    grad_pre2[...] = pre_grad2
    sums_start(2, row_sum(pre_grad2), row_sum(pre_grad2 * flat2))

    classes = logits.shape[1]
    for q in range(n_mp):
        logit_stage[q] = jnp.zeros((2 * images, LANES), F32)
        logit_stage[q, 0:images, 0:classes] = grad_logits
        logit_stage[q, 0:images, classes : classes + 1] = own_live * per_image
        logit_stage[q, images : 2 * images, 0:width] = pooled[
            :, q * width : (q + 1) * width
        ]
    for k in range(1, n_mp):
        q = (p + k) % n_mp
        send(logit_stage.at[q], logit_all.at[p], logit_recv.at[k], b, q)
    logit_all[p] = logit_stage[p]
    raw_forward(1, raw_h)
    raw_end(1, raw_h)

    bias_grad2, gain_grad2 = sums_end(2)
    grad_second = (gain2 * rstd2) * (
        grad_pre2[...]
        - live * (bias_grad2 + normed2[...] * gain_grad2) / live_cells
    )
    strips_start(0, grad_second)

    def put_g(lateral, where, value):
        taps_g[lateral, where] = value

    store_taps(put_g, grad_second.astype(BF16).astype(F32), block)
    pre_grad1 = conv_back(taps_g, weight2) * slope1[...]
    sums_start(3, row_sum(pre_grad1), row_sum(pre_grad1 * normed1[...]))
    scale1 = gain1 * rstd1
    strips_start(1, scale1 * pre_grad1)
    product2, edges2 = strips_product(0, raw_h)
    column_send(0, product2, edges2)
    for k in range(1, n_mp):
        await_bytes(logit_all.at[(p + n_mp - k) % n_mp], logit_recv.at[k])
    both = logit_all[...]
    upper = lax.broadcasted_iota(jnp.int32, both.shape, 1) < images
    upper_logits = jnp.where(upper, both, 0.0).reshape(-1, LANES)
    lifted = jnp.where(upper, pltpu.roll(both, images, 1), 0.0).reshape(-1, LANES)
    head_part[b, 0:width] = tn(lifted, upper_logits, highest)[0:width]
    head_part[b, width : width + 8] = jnp.broadcast_to(
        row_sum(upper_logits), (8, LANES)
    )
    for j in range(1, n_batch):
        part = head_part.at[b]
        send(part, part, head_part_recv.at[j], (b + j) % n_batch, p)
    raw_end(0, raw_x)
    norm_product(raw_x)
    product1, edges1 = strips_product(1, raw_x)
    bias_grad1, gain_grad1 = sums_end(3)
    grad_first = (gain1 * rstd1) * (
        pre_grad1 - live * (bias_grad1 + normed1[...] * gain_grad1) / live_cells
    )
    column_send(1, product1, edges1, (scale1 * bias_grad1, scale1 * gain_grad1))
    quarters_start(0)
    store_taps(put_g, grad_first.astype(BF16).astype(F32), block)
    grad_in = conv_back(taps_g, weight1) + grad_pre2[...]
    cells_stage[...] = (
        images_first(grad_in, images).T.astype(BF16).reshape(n_mp, width, cells)
    )
    for k in range(1, n_mp):
        q = (p + k) % n_mp
        send(cells_stage.at[q], cells_out.at[p], out_recv.at[k], b, q)
    cells_out[p] = cells_stage[p]
    quarters_start(1)

    def own(row):
        pieces = halves(row)
        mine = pieces[0]
        for i in range(1, len(pieces)):
            mine = jnp.where(p // group == i, pieces[i], mine)
        return pltpu.roll(mine, (LANES - place) % LANES, 1)[:, 0:width]

    adjust = live_cells / (live_cells - 1.0)
    kept = 1.0 - momentum
    rows = [
        own(gain_grad1),
        own(bias_grad1),
        own(gain_grad2),
        own(bias_grad2),
        kept * params_here[4] + momentum * own(mean1),
        kept * params_here[5] + momentum * own(var1 * adjust),
        kept * params_here[6] + momentum * own(mean2),
        kept * params_here[7] + momentum * own(var2 * adjust),
    ]
    out_small[...] = jnp.zeros_like(out_small)
    for i, row in enumerate(rows):
        out_small[i : i + 1, 0:width] = row
    for j in range(1, n_batch):
        await_bytes(head_part.at[(b + n_batch - j) % n_batch], head_part_recv.at[j])
    head_sum = sum(head_part[at_b] for at_b in range(n_batch))
    out_small[16 : 16 + width] = head_sum[0:width]
    last = head_sum[width : width + 1]
    out_small[8:9] = last
    out_small[9:10] = jnp.broadcast_to(
        last[:, classes : classes + 1] / live_images, (1, LANES)
    )

    quarters_end(0, out_conv2)
    for k in range(1, n_mp):
        q = (p + n_mp - k) % n_mp
        await_bytes(cells_out.at[q], out_recv.at[k])
    for q in range(n_mp):
        out_features[:, q * cells : (q + 1) * cells] = cells_out[q].astype(F32)
    quarters_end(1, out_conv1)

    for copy in sent:
        copy.wait_send()
    for which in range(4):
        await_bytes(
            sums_all.at[which, pl.ds(0, everyone - 1), pl.ds(0, 4)],
            sums_send.at[which],
        )


def finish_kernel(
    features_in,
    conv1_in,
    conv2_in,
    small,
    loss,
    features_out,
    conv1_out,
    gain1_out,
    bias1_out,
    conv2_out,
    gain2_out,
    bias2_out,
    head_out,
    head_bias_out,
    *stats_out,
):
    features_out[...] = features_in[...]
    conv1_out[...] = conv1_in[...]
    conv2_out[...] = conv2_in[...]
    vectors = (gain1_out, bias1_out, gain2_out, bias2_out) + stats_out
    for i, out in enumerate(vectors):
        out[...] = small[i : i + 1, 0 : out.shape[1]]
    head_bias_out[...] = small[8:9, 0 : head_bias_out.shape[1]]
    loss[0] = small[9, 0]
    head_out[...] = small[16 : 16 + head_out.shape[0], 0 : head_out.shape[1]]


def block_device(
    n_batch,
    n_mp,
    features,
    counts,
    labels,
    teacher,
    conv1_weight,
    bn1_gain,
    bn1_bias,
    conv2_weight,
    bn2_gain,
    bn2_bias,
    head_weight,
    head_bias,
    run_mean1,
    run_var1,
    run_mean2,
    run_var2,
):
    width, cell_count = features.shape
    channels = width * n_mp
    classes = head_weight.shape[1]
    slots = cell_count // (SIDE * SIDE)
    images = slots // n_mp
    block = images * SIDE
    cells = block * SIDE
    n_z = n_mp // PLANE
    quarter = width // n_batch
    seats = n_batch * PLANE
    everyone = n_batch * n_mp
    tall = -(-9 * quarter // 16) * 16
    padded = cells + 2 * block

    def row(values):
        return values.reshape(1, -1)

    def taps_out(values):
        return values.transpose(1, 0, 2)

    def vmem(*shape, dtype=F32):
        return pltpu.VMEM(shape, dtype)

    def low(*shape):
        return pltpu.VMEM(shape, BF16)

    any_space = pl.BlockSpec(memory_space=pl.ANY)
    in_vmem = pl.BlockSpec(memory_space=pltpu.VMEM)
    in_smem = pl.BlockSpec(memory_space=pltpu.SMEM)
    shape = jax.ShapeDtypeStruct
    dma = pltpu.SemaphoreType.DMA
    grant = pltpu.CompilerParams(
        collective_id=0, has_side_effects=True, vmem_limit_bytes=60 * 2**20
    )
    packed = pl.pallas_call(
        functools.partial(block_kernel, (n_batch, n_mp, channels, images)),
        out_shape=(
            shape((width, cell_count), F32),
            shape((9, width, channels), F32),
            shape((9, width, channels), F32),
            shape((16 + width, LANES), F32),
        ),
        in_specs=[any_space, in_smem] + [any_space] * 14,
        out_specs=(in_vmem,) * 4,
        scratch_shapes=[
            low(9, channels, channels),
            low(9, channels, channels),
            vmem(slots, classes),
            vmem(1, slots, dtype=jnp.int32),
            low(width, classes),
            vmem(1, classes),
            vmem(8, 1, width),
            low(n_mp, width, cells),
            vmem(n_mp, 8, LANES),
            vmem(n_batch, 8, LANES),
            low(n_mp, width, LANES),
            vmem(4, everyone, 8, LANES),
            vmem(n_mp, 2 * images, LANES),
            vmem(n_mp, 2 * images, LANES),
            vmem(n_batch, width + 8, LANES),
            vmem(cells, channels),
            vmem(cells, channels),
            vmem(cells, channels),
            vmem(cells, channels),
            vmem(cells, channels),
            low(3, padded, channels),
            low(3, padded, channels),
            low(3, padded, channels),
            low(seats, cells, channels),
            low(seats, cells, channels),
            low(9 * n_z * quarter, seats * cells),
            vmem(16, seats * cells),
            vmem(8, cells),
            vmem(9 * n_z * quarter, channels),
            vmem(n_z * quarter, LANES),
            vmem(16, channels),
            vmem(8, LANES),
            vmem(channels, LANES),
            low(3, seats, n_z * quarter, cells),
            low(3, seats, n_z * quarter, cells),
            vmem(2, n_z, tall, channels),
            low(2, n_z, tall, channels),
            low(2, n_z - 1, tall, channels),
            vmem(2, n_z, 8, LANES),
            vmem(2, n_z, quarter, LANES),
            vmem(2, n_z - 1, quarter, LANES),
            low(2, n_batch, tall, channels),
            low(n_mp, width, cells),
            low(n_mp, width, cells),
            dma((14,)),
            dma((160,)),
            dma((4,)),
            dma((4,)),
            dma((n_mp,)),
            dma((n_batch,)),
            dma((n_mp,)),
            dma((n_mp,)),
            dma((n_batch,)),
            dma((n_mp,)),
            dma((2, 17)),
            dma((2, 7)),
            dma((3, 7)),
            dma((2, n_z - 1)),
            dma((2, n_z - 1)),
            dma((2, n_z - 1)),
            dma((2, n_batch)),
            dma((n_mp,)),
        ],
        compiler_params=grant,
    )(
        features,
        counts,
        row(labels),
        teacher,
        taps_out(conv1_weight),
        taps_out(conv2_weight),
        head_weight,
        row(head_bias),
        row(bn1_gain),
        row(bn1_bias),
        row(bn2_gain),
        row(bn2_bias),
        row(run_mean1),
        row(run_var1),
        row(run_mean2),
        row(run_var2),
    )
    vector = shape((1, width), F32)
    results = pl.pallas_call(
        finish_kernel,
        out_shape=(
            shape((1,), F32),
            shape((width, cell_count), F32),
            shape((9, width, channels), F32),
            vector,
            vector,
            shape((9, width, channels), F32),
            vector,
            vector,
            shape((width, classes), F32),
            shape((1, classes), F32),
            vector,
            vector,
            vector,
            vector,
        ),
        in_specs=[in_vmem] * 4,
        out_specs=(in_smem,) + (in_vmem,) * 13,
        compiler_params=pltpu.CompilerParams(vmem_limit_bytes=60 * 2**20),
    )(*packed)
    loss, grad_features, conv1, gain1, bias1, conv2, gain2, bias2, head, *small = results
    return (
        loss.reshape(()),
        grad_features,
        taps_out(conv1),
        gain1.reshape(-1),
        bias1.reshape(-1),
        taps_out(conv2),
        gain2.reshape(-1),
        bias2.reshape(-1),
        head,
    ) + tuple(values.reshape(-1) for values in small)


def by_images(n_batch, n_mp, features, counts, *rest):
    width, cell_count = features.shape
    images = cell_count // (SIDE * SIDE) // n_mp
    fits = (
        n_batch == 4
        and n_mp == 8
        and width == 32
        and images == 4
        and head_fits(rest)
    )
    if not fits:
        return plain_device(features, counts, *rest)
    return block_device(n_batch, n_mp, features, counts, *rest)


def head_fits(rest):
    return rest[8].shape[1] < LANES


def solution(mesh):
    return jax.shard_map(
        functools.partial(by_images, mesh.shape["batch"], mesh.shape["mp"]),
        mesh=mesh,
        in_specs=(
            P("mp", "batch"),
            P("batch"),
            P("batch"),
            P("batch", None),
            P("mp", None, None),
            P("mp"),
            P("mp"),
            P("mp", None, None),
            P("mp"),
            P("mp"),
            P("mp", None),
            P(),
            P("mp"),
            P("mp"),
            P("mp"),
            P("mp"),
        ),
        out_specs=(
            P(),
            P("mp", "batch"),
            P("mp", None, None),
            P("mp"),
            P("mp"),
            P("mp", None, None),
            P("mp"),
            P("mp"),
            P("mp", None),
            P(),
            P("mp"),
            P("mp"),
            P("mp"),
            P("mp"),
        ),
        check_vma=False,
    )
```

```python
import functools

import jax
import jax.numpy as jnp
from jax import lax
from jax.experimental import pallas as pl
from jax.experimental.pallas import tpu as pltpu
from jax.sharding import PartitionSpec as P

SIDE = 8


epsilon = 1e-05
softening_heat = 4.0
target_weight = 1.0
other_weight = 8.0
loss_scale = 1024.0
momentum = 0.1
highest = lax.Precision.HIGHEST


def shifted_taps(field, sign):
    channels = field.shape[0]
    planes = field.reshape(channels, -1, SIDE, SIDE)
    padded = jnp.pad(planes, ((0, 0), (0, 0), (1, 1), (1, 1)))
    pieces = []
    for vertical in range(3):
        for lateral in range(3):
            row_start = 1 + sign * (vertical - 1)
            col_start = 1 + sign * (lateral - 1)
            pieces.append(
                padded[:, :, row_start : row_start + SIDE, col_start : col_start + SIDE].reshape(
                    channels, -1
                )
            )
    return jnp.stack(pieces)


def image_losses(class_logits, teacher, labels):
    onehot = (labels[:, None] == jnp.arange(class_logits.shape[1])[None, :]).astype(
        class_logits.dtype
    )
    cross = jax.nn.logsumexp(class_logits, axis=1) - jnp.sum(onehot * class_logits, axis=1)
    pupil_network = class_logits / softening_heat
    mentor_network = teacher / softening_heat
    student_rest = pupil_network - 1000.0 * onehot
    tutor_rest = mentor_network - 1000.0 * onehot
    student_all = jax.nn.logsumexp(pupil_network, axis=1)
    tutor_all = jax.nn.logsumexp(mentor_network, axis=1)
    student_other = jax.nn.logsumexp(student_rest, axis=1)
    tutor_other = jax.nn.logsumexp(tutor_rest, axis=1)
    student_hit = jnp.sum(onehot * pupil_network, axis=1) - student_all
    tutor_hit = jnp.sum(onehot * mentor_network, axis=1) - tutor_all
    student_miss = student_other - student_all
    tutor_miss = tutor_other - tutor_all
    binary = jnp.exp(tutor_hit) * (tutor_hit - student_hit) + jnp.exp(tutor_miss) * (
        tutor_miss - student_miss
    )
    tutor_log = tutor_rest - tutor_other[:, None]
    student_log = student_rest - student_other[:, None]
    spread = jnp.sum(jnp.exp(tutor_log) * (tutor_log - student_log), axis=1)
    squared_value = softening_heat * softening_heat
    return cross + squared_value * (target_weight * binary + other_weight * spread)


def silu_slope(values):
    sigma = jax.nn.sigmoid(values)
    return sigma * (1.0 + values * (1.0 - sigma))


def conv_piece(weight, piece):
    return jnp.einsum(
        "otc,tcn->on", weight, shifted_taps(piece, 1), preferred_element_type=jnp.float32
    )


def weight_piece(grad_low, piece):
    return jnp.einsum(
        "on,tcn->otc", grad_low, shifted_taps(piece, 1), preferred_element_type=jnp.float32
    )


def input_piece(weight, back_taps):
    return jnp.einsum("otc,ton->cn", weight, back_taps, preferred_element_type=jnp.float32)


def plain_device(
    features,
    counts,
    labels,
    teacher,
    conv1_weight,
    bn1_gain,
    bn1_bias,
    conv2_weight,
    bn2_gain,
    bn2_bias,
    head_weight,
    head_bias,
    run_mean1,
    run_var1,
    run_mean2,
    run_var2,
):
    channels, cell_count = features.shape
    image_area = SIDE * SIDE
    image_slots = cell_count // image_area
    image_present = (lax.broadcasted_iota(jnp.int32, (image_slots,), 0) < counts[0]).astype(
        jnp.float32
    )
    cell_live = jnp.broadcast_to(image_present[:, None], (image_slots, image_area)).reshape(-1)
    residual_in = features.astype(jnp.float32)
    first = conv_piece(conv1_weight, lax.all_gather(features, "mp", axis=0, tiled=True))
    first_sum, first_square, cells = lax.psum(
        (
            jnp.sum(first * cell_live[None, :], axis=1),
            jnp.sum(first * first * cell_live[None, :], axis=1),
            jnp.sum(cell_live),
        ),
        "batch",
    )
    mean1 = first_sum / cells
    var1 = first_square / cells - mean1 * mean1
    rstd1 = lax.rsqrt(var1 + epsilon)
    normed1 = (first - mean1[:, None]) * rstd1[:, None]
    pre1 = bn1_gain[:, None] * normed1 + bn1_bias[:, None]
    hidden = jax.nn.silu(pre1).astype(jnp.bfloat16)
    second = conv_piece(conv2_weight, lax.all_gather(hidden, "mp", axis=0, tiled=True))
    second_sum, second_square = lax.psum(
        (
            jnp.sum(second * cell_live[None, :], axis=1),
            jnp.sum(second * second * cell_live[None, :], axis=1),
        ),
        "batch",
    )
    mean2 = second_sum / cells
    var2 = second_square / cells - mean2 * mean2
    rstd2 = lax.rsqrt(var2 + epsilon)
    normed2 = (second - mean2[:, None]) * rstd2[:, None]
    pre2 = bn2_gain[:, None] * normed2 + bn2_bias[:, None] + residual_in
    block_out = jax.nn.silu(pre2)
    pooled = jnp.mean(block_out.reshape(channels, image_slots, image_area), axis=2)
    head_local = head_weight.astype(jnp.float32)
    partial_logits = jnp.einsum("cm,ck->mk", pooled, head_local, precision=highest)
    class_logits = lax.psum(partial_logits, "mp") + head_bias[None, :]
    image_batch = cells / image_area

    def losses_of(values):
        return image_losses(values, teacher, labels)

    per_image, pullback = jax.vjp(losses_of, class_logits)
    loss_part = jnp.sum(image_present * per_image)
    (grad_logits,) = pullback(image_present * (loss_scale / image_batch))
    head_grad = jnp.einsum("cm,mk->ck", pooled, grad_logits, precision=highest)
    head_bias_grad = jnp.sum(grad_logits, axis=0)
    grad_pooled = jnp.einsum("mk,ck->cm", grad_logits, head_local, precision=highest) / image_area
    grad_out = jnp.broadcast_to(
        grad_pooled[:, :, None], (channels, image_slots, image_area)
    ).reshape(channels, -1)
    grad_pre2 = grad_out * silu_slope(pre2)
    loss_total = lax.psum(loss_part, "batch")
    bias2_grad, gain2_grad = lax.psum(
        (jnp.sum(grad_pre2, axis=1), jnp.sum(grad_pre2 * normed2, axis=1)), "batch"
    )
    loss = loss_total / image_batch
    grad_second = (bn2_gain * rstd2)[:, None] * (
        grad_pre2
        - cell_live[None, :] * (bias2_grad[:, None] + normed2 * gain2_grad[:, None]) / cells
    )
    second_low = grad_second.astype(jnp.bfloat16)
    conv2_grad = weight_piece(second_low, lax.all_gather(hidden, "mp", axis=0, tiled=True))
    back_second = shifted_taps(second_low, -1)
    grad_hidden = lax.psum_scatter(
        input_piece(conv2_weight, back_second), "mp", scatter_dimension=0, tiled=True
    )
    grad_pre1 = grad_hidden * silu_slope(pre1)
    bias1_grad, gain1_grad = lax.psum(
        (jnp.sum(grad_pre1, axis=1), jnp.sum(grad_pre1 * normed1, axis=1)), "batch"
    )
    grad_first = (bn1_gain * rstd1)[:, None] * (
        grad_pre1
        - cell_live[None, :] * (bias1_grad[:, None] + normed1 * gain1_grad[:, None]) / cells
    )
    first_low = grad_first.astype(jnp.bfloat16)
    conv1_grad = weight_piece(first_low, lax.all_gather(features, "mp", axis=0, tiled=True))
    back_first = shifted_taps(first_low, -1)
    input_term = lax.psum_scatter(
        input_piece(conv1_weight, back_first), "mp", scatter_dimension=0, tiled=True
    )
    grad_features = input_term + grad_pre2
    conv1_grad, conv2_grad, head_grad, head_bias_grad = lax.psum(
        (conv1_grad, conv2_grad, head_grad, head_bias_grad), "batch"
    )
    bias_adjustment = cells / (cells - 1.0)
    new_mean1 = (1.0 - momentum) * run_mean1 + momentum * mean1
    new_var1 = (1.0 - momentum) * run_var1 + momentum * var1 * bias_adjustment
    new_mean2 = (1.0 - momentum) * run_mean2 + momentum * mean2
    new_var2 = (1.0 - momentum) * run_var2 + momentum * var2 * bias_adjustment
    return (
        loss,
        grad_features,
        conv1_grad,
        gain1_grad,
        bias1_grad,
        conv2_grad,
        gain2_grad,
        bias2_grad,
        head_grad,
        head_bias_grad,
        new_mean1,
        new_var1,
        new_mean2,
        new_var2,
    )


MESH = pl.DeviceIdType.MESH
F32 = jnp.float32
BF16 = jnp.bfloat16
LANES = 128
PLANE = 2


def nn(a, b, precision=None):
    return lax.dot_general(
        a, b, (((1,), (0,)), ((), ())), precision=precision, preferred_element_type=F32
    )


def nt(a, b, precision=None):
    return lax.dot_general(
        a, b, (((1,), (1,)), ((), ())), precision=precision, preferred_element_type=F32
    )


def tn(a, b, precision=None):
    return lax.dot_general(
        a, b, (((0,), (0,)), ((), ())), precision=precision, preferred_element_type=F32
    )


def rows_first(field, images):
    return jnp.concatenate(
        [
            field[(m * SIDE + i) * SIDE : (m * SIDE + i + 1) * SIDE]
            for i in range(SIDE)
            for m in range(images)
        ]
    )


def images_first(field, images):
    return jnp.concatenate(
        [
            field[(i * images + m) * SIDE : (i * images + m + 1) * SIDE]
            for m in range(images)
            for i in range(SIDE)
        ]
    )


def store_taps(put, field, block):
    cells, width = field.shape
    tiles = field.reshape(cells // SIDE, SIDE, width)
    column = lax.broadcasted_iota(jnp.int32, tiles.shape, 1)
    left = jnp.where(column == 0, 0.0, pltpu.roll(tiles, 1, 1)).reshape(cells, width)
    right = jnp.where(column == SIDE - 1, 0.0, pltpu.roll(tiles, SIDE - 1, 1)).reshape(
        cells, width
    )
    for lateral, shifted in enumerate((left, field, right)):
        put(lateral, pl.ds(block, cells), shifted.astype(BF16))


def row_sum(field):
    return jnp.sum(field, axis=0, keepdims=True)


def halves(row):
    return [row[:, at : at + LANES] for at in range(0, row.shape[1], LANES)]


def image_terms(logits, teacher, labels):
    def parts(values):
        top = jnp.max(values, axis=1, keepdims=True)
        weights = jnp.exp(values - top)
        total = jnp.sum(weights, axis=1, keepdims=True)
        return top + jnp.log(total), weights / total

    onehot = (
        labels == lax.broadcasted_iota(jnp.int32, logits.shape, 1)
    ).astype(F32)
    full_lse, full_soft = parts(logits)
    pupil = logits / softening_heat
    mentor = teacher / softening_heat
    pupil_rest = pupil - 1000.0 * onehot
    mentor_rest = mentor - 1000.0 * onehot
    pupil_all, pupil_soft = parts(pupil)
    mentor_all, _ = parts(mentor)
    pupil_other, pupil_rest_soft = parts(pupil_rest)
    mentor_other, mentor_rest_soft = parts(mentor_rest)

    def pick(values):
        return jnp.sum(onehot * values, axis=1, keepdims=True)

    pupil_hit = pick(pupil) - pupil_all
    mentor_hit = pick(mentor) - mentor_all
    pupil_miss = pupil_other - pupil_all
    mentor_miss = mentor_other - mentor_all
    hit_weight, miss_weight = jnp.exp(mentor_hit), jnp.exp(mentor_miss)
    binary = hit_weight * (mentor_hit - pupil_hit) + miss_weight * (
        mentor_miss - pupil_miss
    )
    gap = (mentor_rest - mentor_other) - (pupil_rest - pupil_other)
    spread = jnp.sum(mentor_rest_soft * gap, axis=1, keepdims=True)
    squared = softening_heat * softening_heat
    value = (
        full_lse
        - pick(logits)
        + squared * (target_weight * binary + other_weight * spread)
    )
    binary_slope = (
        (hit_weight + miss_weight) * pupil_soft
        - hit_weight * onehot
        - miss_weight * pupil_rest_soft
    )
    spread_slope = pupil_rest_soft - mentor_rest_soft
    slope = (
        full_soft
        - onehot
        + softening_heat
        * (target_weight * binary_slope + other_weight * spread_slope)
    )
    return value, slope


def block_kernel(
    sizes,
    features,
    counts,
    labels,
    teacher,
    conv1,
    conv2,
    head_weight,
    head_bias,
    *rest,
):
    params, rest = rest[:8], rest[8:]
    (
        out_cells,
        out_quarters,
        out_small,
        weight1,
        weight2,
        teacher_here,
        labels_here,
        head_here,
        head_bias_here,
        params_here,
        cells_in,
        params_all,
        counts_all,
        head_all,
        sums_all,
        logit_stage,
        logit_all,
        head_part,
        field,
        normed1,
        slope1,
        normed2,
        grad_pre2,
        taps_x,
        taps_h,
        taps_g,
        raw_x,
        raw_h,
        strip_taps,
        live_taps,
        live_rows,
        norm_part,
        norm_edges,
        live_part,
        live_edges,
        columns,
        strip_stage,
        strip_all,
        column_part,
        column_stage,
        column_all,
        mean_all,
        edge_part,
        edge_all,
        quarter_all,
        cells_stage,
        cells_out,
        load_sem,
        send_sem,
        sums_send,
        sums_recv,
        logit_recv,
        head_part_recv,
        cells_recv,
        params_recv,
        counts_recv,
        head_recv,
        weight_recv,
        raw_recv,
        strip_recv,
        column_recv,
        mean_recv,
        edge_recv,
        quarter_recv,
        out_recv,
    ) = rest
    n_batch, n_mp, channels, images = sizes
    n_z = n_mp // PLANE
    width = channels // n_mp
    quarter = width // n_batch
    block = images * SIDE
    cells = block * SIDE
    everyone = n_batch * n_mp
    b, p = lax.axis_index("batch"), lax.axis_index("mp")
    x, c = b // PLANE, b % PLANE
    z, y = p // PLANE, p % PLANE
    me = b * n_mp + p
    seat = y * n_batch + b
    n_seats = PLANE * n_batch
    means_end_value = {}
    sent = []

    def send(src, dst, recv, to_b, to_p):
        copy = pltpu.make_async_remote_copy(
            src_ref=src,
            dst_ref=dst,
            send_sem=send_sem.at[len(sent)],
            recv_sem=recv,
            device_id=(to_b, to_p),
            device_id_type=MESH,
        )
        copy.start()
        sent.append(copy)

    def await_bytes(ref, sem):
        pltpu.make_async_copy(ref, ref, sem).wait()

    far = [
        lambda v: v + 1 - 2 * (v % 2),
        lambda v: (v + n_z // 2) % n_z,
        lambda v: n_z - 1 - v,
    ]
    others = [
        (((x + dx) % 2) * PLANE + (c + dc) % 2, at_z * PLANE + (y + dy) % 2)
        for at_z in [other(z) for other in reversed(far)] + [z]
        for dy in (1, 0)
        for dx in (1, 0)
        for dc in (1, 0)
    ][:-1]

    loads = [
        (conv1, weight1.at[:, pl.ds(pl.multiple_of(p * width, width), width), :]),
        (conv2, weight2.at[:, pl.ds(pl.multiple_of(p * width, width), width), :]),
        (teacher, teacher_here),
        (labels, labels_here),
        (head_weight, head_here),
        (head_bias, head_bias_here),
    ] + [(ref, params_here.at[i]) for i, ref in enumerate(params)]
    loads = [
        pltpu.make_async_copy(src, dst, load_sem.at[i])
        for i, (src, dst) in enumerate(loads)
    ]
    for load in loads:
        load.start()
    barrier = pltpu.get_barrier_semaphore()
    for to_b, to_p in others:
        pl.semaphore_signal(
            barrier, inc=1, device_id=(to_b, to_p), device_id_type=MESH
        )

    for taps in (taps_x, taps_h, taps_g):
        for lateral in range(3):
            taps[lateral, 0:block] = jnp.zeros((block, channels), BF16)
            taps[lateral, block + cells : 2 * block + cells] = jnp.zeros(
                (block, channels), BF16
            )
    for load in loads:
        load.wait()
    group = LANES // width
    place = pl.multiple_of((p % group) * width, width)
    own_params = jnp.concatenate(
        [params_here[i] for i in range(4)] + [jnp.zeros((4, width), F32)]
    )
    own_params = jnp.concatenate(
        [own_params, jnp.zeros((8, LANES - width), F32)], axis=1
    )
    params_all[p] = pltpu.roll(own_params, place, 1)
    count = counts[0]
    counts_all[b] = jnp.zeros((8, LANES), F32) + count.astype(F32)
    head_all[p] = jnp.concatenate(
        [
            head_here[...],
            jnp.zeros((width, LANES - head_here.shape[1]), BF16),
        ],
        axis=1,
    )

    pl.semaphore_wait(barrier, everyone - 1)

    half = pl.ds(pl.multiple_of(c * LANES, LANES), LANES)
    strip = width // PLANE

    def rows_of(at_z, at_y, at_x):
        start = (at_z * PLANE + at_y) * width + at_x * strip
        return pl.ds(pl.multiple_of(start, strip), strip)

    mates = [(1, 0), (0, 1), (1, 1)]

    def column_start(which, weight):
        part = weight.at[:, rows_of(z, y, x), half]
        for k, other in enumerate(far):
            send(part, part, weight_recv.at[which, k], b, other(z) * PLANE + y)

    def shard_start(which, weight):
        part = weight.at[
            :, pl.ds(pl.multiple_of(p * width, width), width), half
        ]
        send(part, part, weight_recv.at[which, 3], b, z * PLANE + 1 - y)

    def layer_start(which, weight):
        for k, other in enumerate(far):
            part = weight.at[:, rows_of(other(z), y, x), half]
            await_bytes(part, weight_recv.at[which, k])
            for i, (dx, dy) in enumerate(mates):
                send(
                    part,
                    part,
                    weight_recv.at[which, 4 + 3 * k + i],
                    ((x + dx) % 2) * PLANE + c,
                    z * PLANE + (y + dy) % 2,
                )

    def core_start(which, weight):
        part = weight.at[
            :,
            pl.ds(
                pl.multiple_of((z * PLANE + 1 - y) * width, width), width
            ),
            half,
        ]
        await_bytes(part, weight_recv.at[which, 3])
        send(part, part, weight_recv.at[which, 13], x * PLANE + 1 - c, p)
        for k, other in enumerate(far):
            for i, (dx, dy) in enumerate(mates):
                part = weight.at[
                    :, rows_of(other(z), (y + dy) % 2, (x + dx) % 2), half
                ]
                await_bytes(part, weight_recv.at[which, 4 + 3 * k + i])
            part = weight.at[
                :,
                pl.ds(
                    pl.multiple_of(other(z) * PLANE * width, PLANE * width),
                    PLANE * width,
                ),
                half,
            ]
            send(part, part, weight_recv.at[which, 14 + k], x * PLANE + 1 - c, p)

    def core_end(which, weight):
        theirs = pl.ds(pl.multiple_of((1 - c) * LANES, LANES), LANES)
        part = weight.at[
            :,
            pl.ds(
                pl.multiple_of((z * PLANE + 1 - y) * width, width), width
            ),
            theirs,
        ]
        await_bytes(part, weight_recv.at[which, 13])
        for k, other in enumerate(far):
            part = weight.at[
                :,
                pl.ds(
                    pl.multiple_of(other(z) * PLANE * width, PLANE * width),
                    PLANE * width,
                ),
                theirs,
            ]
            await_bytes(part, weight_recv.at[which, 14 + k])

    column_start(0, weight1)
    shard_start(0, weight1)

    def cells_of(q):
        return pl.ds(pl.multiple_of(q * cells, cells), cells)

    own_cells = pltpu.make_async_copy(
        features.at[:, cells_of(p)], cells_in.at[p], load_sem.at[0]
    )
    own_cells.start()
    for k in range(1, n_mp):
        q = (p + k) % n_mp
        send(features.at[:, cells_of(q)], cells_in.at[p], cells_recv.at[k], b, q)
    column_start(1, weight2)
    for k in range(1, n_mp):
        q = (p + k) % n_mp
        send(params_all.at[p], params_all.at[p], params_recv.at[k], b, q)
        send(head_all.at[p], head_all.at[p], head_recv.at[k], b, q)
    for j in range(1, n_batch):
        send(
            counts_all.at[b],
            counts_all.at[b],
            counts_recv.at[j],
            (b + j) % n_batch,
            p,
        )

    layer_start(0, weight1)
    own_cells.wait()
    for k in range(1, n_mp):
        q = (p + n_mp - k) % n_mp
        await_bytes(cells_in.at[q], cells_recv.at[k])
    by_channel = cells_in[...].reshape(channels, cells).astype(F32)
    by_cell = rows_first(by_channel.T, images)
    field[...] = by_cell

    def put_x(lateral, where, value):
        taps_x[lateral, where] = value

    store_taps(put_x, by_cell, block)
    raw_x[seat] = by_cell.astype(BF16)

    shard_start(1, weight2)
    layer_start(1, weight2)
    core_start(0, weight1)

    for k in range(1, n_mp):
        q = (p + n_mp - k) % n_mp
        await_bytes(params_all.at[q], params_recv.at[k])
        await_bytes(head_all.at[q], head_recv.at[k])
    for j in range(1, n_batch):
        await_bytes(counts_all.at[(b + n_batch - j) % n_batch], counts_recv.at[j])
    full_params = jnp.concatenate(
        [
            sum(params_all[q] for q in range(at, at + group))
            for at in range(0, n_mp, group)
        ],
        axis=1,
    )
    gain1, bias1, gain2, bias2 = (full_params[i : i + 1] for i in range(4))
    live_images = sum(counts_all[i] for i in range(n_batch))[0:1, 0:1]
    live_cells = live_images * float(SIDE * SIDE)

    slot = (lax.broadcasted_iota(jnp.int32, (cells, channels), 0) // SIDE) % images
    live = (slot + p * images < count).astype(F32)

    shape = (cells, LANES)
    cell = lax.broadcasted_iota(jnp.int32, shape, 0)
    tap_at = lax.broadcasted_iota(jnp.int32, shape, 1)
    down = (tap_at >= 3).astype(jnp.int32) + (tap_at >= 6).astype(jnp.int32)
    across = tap_at - 3 * down
    at_row = cell // block + down - 1
    at_column = cell % SIDE + across - 1
    within = (at_row >= 0) & (at_row < SIDE) & (at_column >= 0) & (at_column < SIDE)
    inside = jnp.where(within & (tap_at < 9), 1.0, 0.0).astype(BF16)

    def conv(taps, weight):
        total = None
        for tap in range(9):
            vertical, lateral = divmod(tap, 3)
            term = nt(
                taps[lateral, block * vertical : block * vertical + cells],
                weight[tap],
            )
            total = term if total is None else total + term
        return total

    def conv_back(taps, weight):
        total = None
        for tap in range(9):
            vertical, lateral = divmod(tap, 3)
            up = block * (2 - vertical)
            term = nn(taps[2 - lateral, up : up + cells], weight[tap])
            total = term if total is None else total + term
        return total

    def sums_start(which, one, two):
        mine = sums_all.at[which, me, pl.ds(0, 4)]
        sums_all[which, me, 0:4] = jnp.concatenate(halves(one) + halves(two))
        for to_b, to_p in others:
            pltpu.make_async_remote_copy(
                src_ref=mine,
                dst_ref=mine,
                send_sem=sums_send.at[which],
                recv_sem=sums_recv.at[which],
                device_id=(to_b, to_p),
                device_id_type=MESH,
            ).start()

    def sums_end(which):
        everything = sums_all.at[which, pl.ds(0, everyone - 1), pl.ds(0, 4)]
        await_bytes(everything, sums_recv.at[which])
        total = jnp.sum(sums_all[which], axis=0)
        return (
            jnp.concatenate([total[0:1], total[1:2]], axis=1),
            jnp.concatenate([total[2:3], total[3:4]], axis=1),
        )

    def means_start(which, value):
        mean_all[which, z] = jnp.concatenate(
            halves(row_sum(value) / float(cells))
            + [jnp.zeros((8 - channels // LANES, LANES), F32)]
        )
        part = mean_all.at[which, z]
        for k, other in enumerate(far):
            send(part, part, mean_recv.at[which, k], b, other(z) * PLANE + y)

    def means_end(which):
        for k, other in enumerate(far):
            await_bytes(mean_all.at[which, other(z)], mean_recv.at[which, k])
        total = sum(mean_all[which, at_z] for at_z in range(n_z)) / float(n_z)
        return jnp.concatenate(
            [total[i : i + 1] for i in range(channels // LANES)], axis=1
        )

    def raw_start(which, raw):
        part = raw.at[seat]
        for i, (dx, dy) in enumerate(mates):
            send(
                part,
                part,
                raw_recv.at[which, i],
                ((x + dx) % 2) * PLANE + c,
                z * PLANE + (y + dy) % 2,
            )
        send(part, part, raw_recv.at[which, 3], x * PLANE + 1 - c, p)

    def seat_of(dx, dy, dc):
        return ((y + dy) % 2) * n_batch + ((x + dx) % 2) * PLANE + (c + dc) % 2

    def raw_forward(which, raw):
        for i, (dx, dy) in enumerate(mates):
            part = raw.at[seat_of(dx, dy, 0)]
            await_bytes(part, raw_recv.at[which, i])
            send(part, part, raw_recv.at[which, 4 + i], x * PLANE + 1 - c, p)

    def raw_end(which, raw):
        await_bytes(raw.at[seat_of(0, 0, 1)], raw_recv.at[which, 3])
        for i, (dx, dy) in enumerate(mates):
            await_bytes(raw.at[seat_of(dx, dy, 1)], raw_recv.at[which, 4 + i])

    seats = [
        (dx, dy, dc)
        for dy in (1, 0)
        for dx in (1, 0)
        for dc in (1, 0)
        if dx or dy or dc
    ]

    def strips_start(which, value):
        by_row = value.T
        for s in range(n_seats):
            at_y, at_b = divmod(s, n_batch)
            strip_stage[which, s] = jnp.concatenate(
                [
                    by_row[start : start + quarter]
                    for start in (
                        (at_z * PLANE + at_y) * width + at_b * quarter
                        for at_z in range(n_z)
                    )
                ]
            ).astype(BF16)
        for i, (dx, dy, dc) in enumerate(seats):
            send(
                strip_stage.at[which, seat_of(dx, dy, dc)],
                strip_all.at[which, seat],
                strip_recv.at[which, i],
                ((x + dx) % 2) * PLANE + (c + dc) % 2,
                z * PLANE + (y + dy) % 2,
            )
        strip_all[which, seat] = strip_stage[which, seat]

    shape = (9, 1, cells)
    cell = lax.broadcasted_iota(jnp.int32, shape, 2)
    tap_at = lax.broadcasted_iota(jnp.int32, shape, 0)
    down = (tap_at >= 3).astype(jnp.int32) + (tap_at >= 6).astype(jnp.int32)
    from_row = cell // block - down + 1
    from_column = cell % SIDE - (tap_at - 3 * down) + 1
    reach = jnp.where(
        (from_row >= 0)
        & (from_row < SIDE)
        & (from_column >= 0)
        & (from_column < SIDE),
        1.0,
        0.0,
    )

    def moved(value, tap):
        vertical, lateral = divmod(tap, 3)
        ahead = (vertical - 1) * block + lateral - 1
        return (pltpu.roll(value, ahead % cells, 1) if ahead else value) * reach[tap]

    strips = n_z * quarter

    def strips_product(which, raw):
        for i, (dx, dy, dc) in enumerate(seats):
            await_bytes(
                strip_all.at[which, seat_of(dx, dy, dc)], strip_recv.at[which, i]
            )
        for s in range(n_seats):
            value = strip_all[which, s].astype(F32)
            for tap in range(9):
                strip_taps[
                    tap * strips : (tap + 1) * strips, s * cells : (s + 1) * cells
                ] = moved(value, tap).astype(BF16)
        edges = sum(nn(strip_all[which, s], inside) for s in range(n_seats))
        return nn(strip_taps[...], raw[...].reshape(-1, channels)), edges

    def live_of(at_y, at_b):
        lane = lax.broadcasted_iota(jnp.int32, (8, cells), 1)
        image = (lane // SIDE) % images + (z * PLANE + at_y) * images
        return (image.astype(F32) < counts_all[at_b][:, 0:1]).astype(F32)

    def norm_product(raw):
        for s in range(n_seats):
            alive = live_of(*divmod(s, n_batch))
            live_rows[s : s + 1] = alive[0:1].astype(F32)
            for tap in range(9):
                live_taps[tap : tap + 1, s * cells : (s + 1) * cells] = moved(
                    alive, tap
                )[0:1]
        product, edges = strips_product(2, raw)
        norm_part[...] = product
        norm_edges[...] = edges
        live_part[...] = nn(
            live_taps[...].astype(BF16), raw[...].reshape(-1, channels)
        )
        live_edges[...] = nn(live_rows[...].astype(BF16), inside)

    def own_column(row):
        columns[...] = jnp.broadcast_to(row, (LANES, channels)).T
        return jnp.concatenate(
            [
                columns[
                    pl.ds(
                        pl.multiple_of(
                            (at_z * PLANE + y) * width + b * quarter, quarter
                        ),
                        quarter,
                    ),
                    :,
                ]
                for at_z in range(n_z)
            ]
        )[:, 0:1]

    def column_send(which, product, edges, sums=None):
        if sums is not None:
            bias_column, gain_column = (own_column(row / live_cells) for row in sums)
            edges = edges - (
                bias_column * row_sum(live_edges[...]) + gain_column * norm_edges[...]
            )
        mean = means_end(1 - which)
        means_end_value[which] = mean
        for at_z in range(n_z):
            edge_part[which, at_z] = edges[at_z * quarter : (at_z + 1) * quarter]
        for tap in range(9):
            rows = slice(tap * strips, (tap + 1) * strips)
            total = product[rows] - edges[:, tap : tap + 1] * mean
            if sums is not None:
                total = total - (
                    bias_column * live_part[tap : tap + 1]
                    + gain_column * norm_part[rows]
                )
            for at_z in range(n_z):
                column_part[which, at_z, tap * quarter : (tap + 1) * quarter] = total[
                    at_z * quarter : (at_z + 1) * quarter
                ]
        for at_z in range(n_z):
            column_stage[which, at_z] = jnp.concatenate(
                halves(column_part[which, at_z])
            ).astype(BF16)
        for k, other in enumerate(far):
            send(
                column_stage.at[which, other(z)],
                column_all.at[which, k],
                column_recv.at[which, k],
                b,
                other(z) * PLANE + y,
            )
            send(
                edge_part.at[which, other(z)],
                edge_all.at[which, k],
                edge_recv.at[which, k],
                b,
                other(z) * PLANE + y,
            )

    def unfold(piece):
        return jnp.concatenate(
            [
                piece[at : at + 9 * quarter]
                for at in range(0, piece.shape[0], 9 * quarter)
            ],
            axis=1,
        )

    def quarters_start(which):
        for k in range(len(far)):
            await_bytes(column_all.at[which, k], column_recv.at[which, k])
            await_bytes(edge_all.at[which, k], edge_recv.at[which, k])
        mean = means_end_value[which]
        edges = edge_part[which, z]
        total = column_part[which, z]
        for k in range(len(far)):
            edges = edges + edge_all[which, k]
            total = total + unfold(column_all[which, k].astype(F32))
        back = jnp.concatenate([edges[:, tap : tap + 1] * mean for tap in range(9)])
        quarter_all[which, b] = jnp.concatenate(halves(total + back)).astype(BF16)
        for j in range(1, n_batch):
            part = quarter_all.at[which, b]
            send(part, part, quarter_recv.at[which, j], (b + j) % n_batch, p)

    def quarters_end(which):
        for j in range(1, n_batch):
            await_bytes(
                quarter_all.at[which, (b + n_batch - j) % n_batch],
                quarter_recv.at[which, j],
            )
        out_quarters[which] = quarter_all[which]

    live_taps[...] = jnp.zeros_like(live_taps)
    means_start(0, by_cell)
    core_end(0, weight1)
    first = conv(taps_x, weight1)
    masked = first * live
    sums_start(0, row_sum(masked), row_sum(masked * first))
    raw_start(0, raw_x)
    core_start(1, weight2)
    total, square = sums_end(0)
    mean1 = total / live_cells
    var1 = square / live_cells - mean1 * mean1
    rstd1 = lax.rsqrt(var1 + epsilon)
    flat = (first - mean1) * rstd1
    normed1[...] = flat
    pre1 = gain1 * flat + bias1
    sigma1 = jax.nn.sigmoid(pre1)
    slope1[...] = sigma1 * (1.0 + pre1 * (1.0 - sigma1))
    hidden = pre1 * sigma1

    def put_h(lateral, where, value):
        taps_h[lateral, where] = value

    store_taps(put_h, hidden, block)
    raw_h[seat] = hidden.astype(BF16)
    means_start(1, hidden)
    core_end(1, weight2)

    second = conv(taps_h, weight2)
    masked = second * live
    sums_start(1, row_sum(masked), row_sum(masked * second))
    raw_start(1, raw_h)
    strips_start(2, normed1[...] * live)
    raw_forward(0, raw_x)
    total, square = sums_end(1)
    mean2 = total / live_cells
    var2 = square / live_cells - mean2 * mean2
    rstd2 = lax.rsqrt(var2 + epsilon)
    flat2 = (second - mean2) * rstd2
    normed2[...] = flat2
    pre2 = gain2 * flat2 + bias2 + field[...]
    sigma2 = jax.nn.sigmoid(pre2)
    block_out = pre2 * sigma2

    pooled = sum(block_out[i * block : (i + 1) * block] for i in range(SIDE))
    pooled = jnp.sum(pooled.reshape(images, SIDE, channels), axis=1) / float(
        SIDE * SIDE
    )
    head = head_all[...].reshape(channels, LANES).astype(F32)[:, 0 : head_here.shape[1]]
    logits = nn(pooled, head, highest) + head_bias_here[...]
    slots = labels_here.shape[1]
    image_at = lax.broadcasted_iota(jnp.int32, (images, slots), 0) + p * images
    picked = lax.broadcasted_iota(jnp.int32, (images, slots), 1) == image_at
    own_labels = jnp.sum(
        jnp.where(picked, labels_here[...], 0), axis=1, keepdims=True
    )
    own_teacher = nn(picked.astype(F32), teacher_here[...], highest)
    own_live = (image_at[:, 0:1] < count).astype(F32)
    per_image, slope = image_terms(logits, own_teacher, own_labels)
    grad_logits = slope * (own_live * (loss_scale / live_images))
    grad_pooled = nt(grad_logits, head, highest) / float(SIDE * SIDE)
    spread = jnp.concatenate(
        [
            jnp.broadcast_to(grad_pooled[m : m + 1], (SIDE, channels))
            for m in range(images)
        ]
    )
    spread = jnp.concatenate([spread] * SIDE)
    pre_grad2 = spread * (sigma2 * (1.0 + pre2 * (1.0 - sigma2)))
    grad_pre2[...] = pre_grad2
    sums_start(2, row_sum(pre_grad2), row_sum(pre_grad2 * flat2))

    classes = logits.shape[1]
    for q in range(n_mp):
        logit_stage[q] = jnp.zeros((2 * images, LANES), F32)
        logit_stage[q, 0:images, 0:classes] = grad_logits
        logit_stage[q, 0:images, classes : classes + 1] = own_live * per_image
        logit_stage[q, images : 2 * images, 0:width] = pooled[
            :, q * width : (q + 1) * width
        ]
    for k in range(1, n_mp):
        q = (p + k) % n_mp
        send(logit_stage.at[q], logit_all.at[p], logit_recv.at[k], b, q)
    logit_all[p] = logit_stage[p]
    raw_forward(1, raw_h)
    raw_end(1, raw_h)

    bias_grad2, gain_grad2 = sums_end(2)
    grad_second = (gain2 * rstd2) * (
        grad_pre2[...]
        - live * (bias_grad2 + normed2[...] * gain_grad2) / live_cells
    )
    strips_start(0, grad_second)

    def put_g(lateral, where, value):
        taps_g[lateral, where] = value

    store_taps(put_g, grad_second.astype(BF16).astype(F32), block)
    pre_grad1 = conv_back(taps_g, weight2) * slope1[...]
    sums_start(3, row_sum(pre_grad1), row_sum(pre_grad1 * normed1[...]))
    scale1 = gain1 * rstd1
    strips_start(1, scale1 * pre_grad1)
    raw_end(0, raw_x)
    norm_product(raw_x)
    product2, edges2 = strips_product(0, raw_h)
    column_send(0, product2, edges2)
    product1, edges1 = strips_product(1, raw_x)
    bias_grad1, gain_grad1 = sums_end(3)
    grad_first = (gain1 * rstd1) * (
        pre_grad1 - live * (bias_grad1 + normed1[...] * gain_grad1) / live_cells
    )
    column_send(1, product1, edges1, (scale1 * bias_grad1, scale1 * gain_grad1))
    store_taps(put_g, grad_first.astype(BF16).astype(F32), block)
    grad_in = conv_back(taps_g, weight1) + grad_pre2[...]
    cells_stage[...] = (
        images_first(grad_in, images).T.astype(BF16).reshape(n_mp, width, cells)
    )
    for k in range(1, n_mp):
        q = (p + k) % n_mp
        send(cells_stage.at[q], cells_out.at[p], out_recv.at[k], b, q)
    cells_out[p] = cells_stage[p]
    for k in range(1, n_mp):
        await_bytes(logit_all.at[(p + n_mp - k) % n_mp], logit_recv.at[k])
    both = logit_all[...]
    upper = lax.broadcasted_iota(jnp.int32, both.shape, 1) < images
    upper_logits = jnp.where(upper, both, 0.0).reshape(-1, LANES)
    lifted = jnp.where(upper, pltpu.roll(both, images, 1), 0.0).reshape(-1, LANES)
    head_part[b, 0:width] = tn(lifted, upper_logits, highest)[0:width]
    head_part[b, width : width + 8] = jnp.broadcast_to(
        row_sum(upper_logits), (8, LANES)
    )
    for j in range(1, n_batch):
        part = head_part.at[b]
        send(part, part, head_part_recv.at[j], (b + j) % n_batch, p)
    quarters_start(0)
    quarters_start(1)

    def own(row):
        pieces = halves(row)
        mine = pieces[0]
        for i in range(1, len(pieces)):
            mine = jnp.where(p // group == i, pieces[i], mine)
        return pltpu.roll(mine, (LANES - place) % LANES, 1)[:, 0:width]

    adjust = live_cells / (live_cells - 1.0)
    kept = 1.0 - momentum
    rows = [
        own(gain_grad1),
        own(bias_grad1),
        own(gain_grad2),
        own(bias_grad2),
        kept * params_here[4] + momentum * own(mean1),
        kept * params_here[5] + momentum * own(var1 * adjust),
        kept * params_here[6] + momentum * own(mean2),
        kept * params_here[7] + momentum * own(var2 * adjust),
    ]
    out_small[...] = jnp.zeros_like(out_small)
    for i, row in enumerate(rows):
        out_small[i : i + 1, 0:width] = row
    for j in range(1, n_batch):
        await_bytes(head_part.at[(b + n_batch - j) % n_batch], head_part_recv.at[j])
    head_sum = sum(head_part[at_b] for at_b in range(n_batch))
    out_small[16 : 16 + width] = head_sum[0:width]
    last = head_sum[width : width + 1]
    out_small[8:9] = last
    out_small[9:10] = jnp.broadcast_to(
        last[:, classes : classes + 1] / live_images, (1, LANES)
    )

    quarters_end(0)
    for k in range(1, n_mp):
        q = (p + n_mp - k) % n_mp
        await_bytes(cells_out.at[q], out_recv.at[k])
    out_cells[...] = cells_out[...]
    quarters_end(1)

    for copy in sent:
        copy.wait_send()
    for which in range(4):
        await_bytes(
            sums_all.at[which, pl.ds(0, everyone - 1), pl.ds(0, 4)],
            sums_send.at[which],
        )


def finish_kernel(
    cells_in,
    quarters_in,
    small,
    loss,
    features_out,
    conv1_out,
    gain1_out,
    bias1_out,
    conv2_out,
    gain2_out,
    bias2_out,
    head_out,
    head_bias_out,
    *stats_out,
):
    n_mp, _, cells = cells_in.shape
    for q in range(n_mp):
        features_out[:, q * cells : (q + 1) * cells] = cells_in[q].astype(F32)
    n_batch = quarters_in.shape[1]
    quarter = conv1_out.shape[1] // n_batch
    for which, out in enumerate((conv2_out, conv1_out)):
        for at_b in range(n_batch):
            whole = quarters_in[which, at_b].astype(F32)
            for start in range(0, whole.shape[0], quarter):
                tap, lanes = start // quarter % 9, start // quarter // 9 * LANES
                out[
                    tap, at_b * quarter : (at_b + 1) * quarter, lanes : lanes + LANES
                ] = whole[start : start + quarter]
    vectors = (gain1_out, bias1_out, gain2_out, bias2_out) + stats_out
    for i, out in enumerate(vectors):
        out[...] = small[i : i + 1, 0 : out.shape[1]]
    head_bias_out[...] = small[8:9, 0 : head_bias_out.shape[1]]
    loss[0] = small[9, 0]
    head_out[...] = small[16 : 16 + head_out.shape[0], 0 : head_out.shape[1]]


def block_device(
    n_batch,
    n_mp,
    features,
    counts,
    labels,
    teacher,
    conv1_weight,
    bn1_gain,
    bn1_bias,
    conv2_weight,
    bn2_gain,
    bn2_bias,
    head_weight,
    head_bias,
    run_mean1,
    run_var1,
    run_mean2,
    run_var2,
):
    width, cell_count = features.shape
    channels = width * n_mp
    classes = head_weight.shape[1]
    slots = cell_count // (SIDE * SIDE)
    images = slots // n_mp
    block = images * SIDE
    cells = block * SIDE
    n_z = n_mp // PLANE
    quarter = width // n_batch
    seats = n_batch * PLANE
    everyone = n_batch * n_mp
    tall = 9 * quarter * (channels // LANES)
    padded = cells + 2 * block

    def row(values):
        return values.reshape(1, -1)

    def taps_out(values):
        return values.transpose(1, 0, 2)

    def vmem(*shape, dtype=F32):
        return pltpu.VMEM(shape, dtype)

    def low(*shape):
        return pltpu.VMEM(shape, BF16)

    any_space = pl.BlockSpec(memory_space=pl.ANY)
    in_vmem = pl.BlockSpec(memory_space=pltpu.VMEM)
    in_smem = pl.BlockSpec(memory_space=pltpu.SMEM)
    shape = jax.ShapeDtypeStruct
    dma = pltpu.SemaphoreType.DMA
    grant = pltpu.CompilerParams(
        collective_id=0, has_side_effects=True, vmem_limit_bytes=60 * 2**20
    )
    packed = pl.pallas_call(
        functools.partial(block_kernel, (n_batch, n_mp, channels, images)),
        out_shape=(
            shape((n_mp, width, cells), BF16),
            shape((2, n_batch, tall, LANES), BF16),
            shape((16 + width, LANES), F32),
        ),
        in_specs=[any_space, in_smem] + [any_space] * 14,
        out_specs=(in_vmem,) * 3,
        scratch_shapes=[
            low(9, channels, channels),
            low(9, channels, channels),
            vmem(slots, classes),
            vmem(1, slots, dtype=jnp.int32),
            low(width, classes),
            vmem(1, classes),
            vmem(8, 1, width),
            low(n_mp, width, cells),
            vmem(n_mp, 8, LANES),
            vmem(n_batch, 8, LANES),
            low(n_mp, width, LANES),
            vmem(4, everyone, 8, LANES),
            vmem(n_mp, 2 * images, LANES),
            vmem(n_mp, 2 * images, LANES),
            vmem(n_batch, width + 8, LANES),
            vmem(cells, channels),
            vmem(cells, channels),
            vmem(cells, channels),
            vmem(cells, channels),
            vmem(cells, channels),
            low(3, padded, channels),
            low(3, padded, channels),
            low(3, padded, channels),
            low(seats, cells, channels),
            low(seats, cells, channels),
            low(9 * n_z * quarter, seats * cells),
            vmem(16, seats * cells),
            vmem(8, cells),
            vmem(9 * n_z * quarter, channels),
            vmem(n_z * quarter, LANES),
            vmem(16, channels),
            vmem(8, LANES),
            vmem(channels, LANES),
            low(3, seats, n_z * quarter, cells),
            low(3, seats, n_z * quarter, cells),
            vmem(2, n_z, 9 * quarter, channels),
            low(2, n_z, tall, LANES),
            low(2, n_z - 1, tall, LANES),
            vmem(2, n_z, 8, LANES),
            vmem(2, n_z, quarter, LANES),
            vmem(2, n_z - 1, quarter, LANES),
            low(2, n_batch, tall, LANES),
            low(n_mp, width, cells),
            low(n_mp, width, cells),
            dma((14,)),
            dma((160,)),
            dma((4,)),
            dma((4,)),
            dma((n_mp,)),
            dma((n_batch,)),
            dma((n_mp,)),
            dma((n_mp,)),
            dma((n_batch,)),
            dma((n_mp,)),
            dma((2, 17)),
            dma((2, 7)),
            dma((3, 7)),
            dma((2, n_z - 1)),
            dma((2, n_z - 1)),
            dma((2, n_z - 1)),
            dma((2, n_batch)),
            dma((n_mp,)),
        ],
        compiler_params=grant,
    )(
        features,
        counts,
        row(labels),
        teacher,
        taps_out(conv1_weight),
        taps_out(conv2_weight),
        head_weight,
        row(head_bias),
        row(bn1_gain),
        row(bn1_bias),
        row(bn2_gain),
        row(bn2_bias),
        row(run_mean1),
        row(run_var1),
        row(run_mean2),
        row(run_var2),
    )
    vector = shape((1, width), F32)
    results = pl.pallas_call(
        finish_kernel,
        out_shape=(
            shape((1,), F32),
            shape((width, cell_count), F32),
            shape((9, width, channels), F32),
            vector,
            vector,
            shape((9, width, channels), F32),
            vector,
            vector,
            shape((width, classes), F32),
            shape((1, classes), F32),
            vector,
            vector,
            vector,
            vector,
        ),
        in_specs=[in_vmem] * 3,
        out_specs=(in_smem,) + (in_vmem,) * 13,
        compiler_params=pltpu.CompilerParams(vmem_limit_bytes=60 * 2**20),
    )(*packed)
    loss, grad_features, conv1, gain1, bias1, conv2, gain2, bias2, head, *small = results
    return (
        loss.reshape(()),
        grad_features,
        taps_out(conv1),
        gain1.reshape(-1),
        bias1.reshape(-1),
        taps_out(conv2),
        gain2.reshape(-1),
        bias2.reshape(-1),
        head,
    ) + tuple(values.reshape(-1) for values in small)


def by_images(n_batch, n_mp, features, counts, *rest):
    width, cell_count = features.shape
    images = cell_count // (SIDE * SIDE) // n_mp
    fits = (
        n_batch == 4
        and n_mp == 8
        and width == 32
        and images == 4
        and head_fits(rest)
    )
    if not fits:
        return plain_device(features, counts, *rest)
    return block_device(n_batch, n_mp, features, counts, *rest)


def head_fits(rest):
    return rest[8].shape[1] < LANES


def solution(mesh):
    return jax.shard_map(
        functools.partial(by_images, mesh.shape["batch"], mesh.shape["mp"]),
        mesh=mesh,
        in_specs=(
            P("mp", "batch"),
            P("batch"),
            P("batch"),
            P("batch", None),
            P("mp", None, None),
            P("mp"),
            P("mp"),
            P("mp", None, None),
            P("mp"),
            P("mp"),
            P("mp", None),
            P(),
            P("mp"),
            P("mp"),
            P("mp"),
            P("mp"),
        ),
        out_specs=(
            P(),
            P("mp", "batch"),
            P("mp", None, None),
            P("mp"),
            P("mp"),
            P("mp", None, None),
            P("mp"),
            P("mp"),
            P("mp", None),
            P(),
            P("mp"),
            P("mp"),
            P("mp"),
            P("mp"),
        ),
        check_vma=False,
    )
```

```python
import functools

import jax
import jax.numpy as jnp
from jax import lax
from jax.experimental import pallas as pl
from jax.experimental.pallas import tpu as pltpu
from jax.sharding import PartitionSpec as P

SIDE = 8


epsilon = 1e-05
softening_heat = 4.0
target_weight = 1.0
other_weight = 8.0
loss_scale = 1024.0
momentum = 0.1
highest = lax.Precision.HIGHEST


def shifted_taps(field, sign):
    channels = field.shape[0]
    planes = field.reshape(channels, -1, SIDE, SIDE)
    padded = jnp.pad(planes, ((0, 0), (0, 0), (1, 1), (1, 1)))
    pieces = []
    for vertical in range(3):
        for lateral in range(3):
            row_start = 1 + sign * (vertical - 1)
            col_start = 1 + sign * (lateral - 1)
            pieces.append(
                padded[:, :, row_start : row_start + SIDE, col_start : col_start + SIDE].reshape(
                    channels, -1
                )
            )
    return jnp.stack(pieces)


def image_losses(class_logits, teacher, labels):
    onehot = (labels[:, None] == jnp.arange(class_logits.shape[1])[None, :]).astype(
        class_logits.dtype
    )
    cross = jax.nn.logsumexp(class_logits, axis=1) - jnp.sum(onehot * class_logits, axis=1)
    pupil_network = class_logits / softening_heat
    mentor_network = teacher / softening_heat
    student_rest = pupil_network - 1000.0 * onehot
    tutor_rest = mentor_network - 1000.0 * onehot
    student_all = jax.nn.logsumexp(pupil_network, axis=1)
    tutor_all = jax.nn.logsumexp(mentor_network, axis=1)
    student_other = jax.nn.logsumexp(student_rest, axis=1)
    tutor_other = jax.nn.logsumexp(tutor_rest, axis=1)
    student_hit = jnp.sum(onehot * pupil_network, axis=1) - student_all
    tutor_hit = jnp.sum(onehot * mentor_network, axis=1) - tutor_all
    student_miss = student_other - student_all
    tutor_miss = tutor_other - tutor_all
    binary = jnp.exp(tutor_hit) * (tutor_hit - student_hit) + jnp.exp(tutor_miss) * (
        tutor_miss - student_miss
    )
    tutor_log = tutor_rest - tutor_other[:, None]
    student_log = student_rest - student_other[:, None]
    spread = jnp.sum(jnp.exp(tutor_log) * (tutor_log - student_log), axis=1)
    squared_value = softening_heat * softening_heat
    return cross + squared_value * (target_weight * binary + other_weight * spread)


def silu_slope(values):
    sigma = jax.nn.sigmoid(values)
    return sigma * (1.0 + values * (1.0 - sigma))


def conv_piece(weight, piece):
    return jnp.einsum(
        "otc,tcn->on", weight, shifted_taps(piece, 1), preferred_element_type=jnp.float32
    )


def weight_piece(grad_low, piece):
    return jnp.einsum(
        "on,tcn->otc", grad_low, shifted_taps(piece, 1), preferred_element_type=jnp.float32
    )


def input_piece(weight, back_taps):
    return jnp.einsum("otc,ton->cn", weight, back_taps, preferred_element_type=jnp.float32)


def plain_device(
    features,
    counts,
    labels,
    teacher,
    conv1_weight,
    bn1_gain,
    bn1_bias,
    conv2_weight,
    bn2_gain,
    bn2_bias,
    head_weight,
    head_bias,
    run_mean1,
    run_var1,
    run_mean2,
    run_var2,
):
    channels, cell_count = features.shape
    image_area = SIDE * SIDE
    image_slots = cell_count // image_area
    image_present = (lax.broadcasted_iota(jnp.int32, (image_slots,), 0) < counts[0]).astype(
        jnp.float32
    )
    cell_live = jnp.broadcast_to(image_present[:, None], (image_slots, image_area)).reshape(-1)
    residual_in = features.astype(jnp.float32)
    first = conv_piece(conv1_weight, lax.all_gather(features, "mp", axis=0, tiled=True))
    first_sum, first_square, cells = lax.psum(
        (
            jnp.sum(first * cell_live[None, :], axis=1),
            jnp.sum(first * first * cell_live[None, :], axis=1),
            jnp.sum(cell_live),
        ),
        "batch",
    )
    mean1 = first_sum / cells
    var1 = first_square / cells - mean1 * mean1
    rstd1 = lax.rsqrt(var1 + epsilon)
    normed1 = (first - mean1[:, None]) * rstd1[:, None]
    pre1 = bn1_gain[:, None] * normed1 + bn1_bias[:, None]
    hidden = jax.nn.silu(pre1).astype(jnp.bfloat16)
    second = conv_piece(conv2_weight, lax.all_gather(hidden, "mp", axis=0, tiled=True))
    second_sum, second_square = lax.psum(
        (
            jnp.sum(second * cell_live[None, :], axis=1),
            jnp.sum(second * second * cell_live[None, :], axis=1),
        ),
        "batch",
    )
    mean2 = second_sum / cells
    var2 = second_square / cells - mean2 * mean2
    rstd2 = lax.rsqrt(var2 + epsilon)
    normed2 = (second - mean2[:, None]) * rstd2[:, None]
    pre2 = bn2_gain[:, None] * normed2 + bn2_bias[:, None] + residual_in
    block_out = jax.nn.silu(pre2)
    pooled = jnp.mean(block_out.reshape(channels, image_slots, image_area), axis=2)
    head_local = head_weight.astype(jnp.float32)
    partial_logits = jnp.einsum("cm,ck->mk", pooled, head_local, precision=highest)
    class_logits = lax.psum(partial_logits, "mp") + head_bias[None, :]
    image_batch = cells / image_area

    def losses_of(values):
        return image_losses(values, teacher, labels)

    per_image, pullback = jax.vjp(losses_of, class_logits)
    loss_part = jnp.sum(image_present * per_image)
    (grad_logits,) = pullback(image_present * (loss_scale / image_batch))
    head_grad = jnp.einsum("cm,mk->ck", pooled, grad_logits, precision=highest)
    head_bias_grad = jnp.sum(grad_logits, axis=0)
    grad_pooled = jnp.einsum("mk,ck->cm", grad_logits, head_local, precision=highest) / image_area
    grad_out = jnp.broadcast_to(
        grad_pooled[:, :, None], (channels, image_slots, image_area)
    ).reshape(channels, -1)
    grad_pre2 = grad_out * silu_slope(pre2)
    loss_total = lax.psum(loss_part, "batch")
    bias2_grad, gain2_grad = lax.psum(
        (jnp.sum(grad_pre2, axis=1), jnp.sum(grad_pre2 * normed2, axis=1)), "batch"
    )
    loss = loss_total / image_batch
    grad_second = (bn2_gain * rstd2)[:, None] * (
        grad_pre2
        - cell_live[None, :] * (bias2_grad[:, None] + normed2 * gain2_grad[:, None]) / cells
    )
    second_low = grad_second.astype(jnp.bfloat16)
    conv2_grad = weight_piece(second_low, lax.all_gather(hidden, "mp", axis=0, tiled=True))
    back_second = shifted_taps(second_low, -1)
    grad_hidden = lax.psum_scatter(
        input_piece(conv2_weight, back_second), "mp", scatter_dimension=0, tiled=True
    )
    grad_pre1 = grad_hidden * silu_slope(pre1)
    bias1_grad, gain1_grad = lax.psum(
        (jnp.sum(grad_pre1, axis=1), jnp.sum(grad_pre1 * normed1, axis=1)), "batch"
    )
    grad_first = (bn1_gain * rstd1)[:, None] * (
        grad_pre1
        - cell_live[None, :] * (bias1_grad[:, None] + normed1 * gain1_grad[:, None]) / cells
    )
    first_low = grad_first.astype(jnp.bfloat16)
    conv1_grad = weight_piece(first_low, lax.all_gather(features, "mp", axis=0, tiled=True))
    back_first = shifted_taps(first_low, -1)
    input_term = lax.psum_scatter(
        input_piece(conv1_weight, back_first), "mp", scatter_dimension=0, tiled=True
    )
    grad_features = input_term + grad_pre2
    conv1_grad, conv2_grad, head_grad, head_bias_grad = lax.psum(
        (conv1_grad, conv2_grad, head_grad, head_bias_grad), "batch"
    )
    bias_adjustment = cells / (cells - 1.0)
    new_mean1 = (1.0 - momentum) * run_mean1 + momentum * mean1
    new_var1 = (1.0 - momentum) * run_var1 + momentum * var1 * bias_adjustment
    new_mean2 = (1.0 - momentum) * run_mean2 + momentum * mean2
    new_var2 = (1.0 - momentum) * run_var2 + momentum * var2 * bias_adjustment
    return (
        loss,
        grad_features,
        conv1_grad,
        gain1_grad,
        bias1_grad,
        conv2_grad,
        gain2_grad,
        bias2_grad,
        head_grad,
        head_bias_grad,
        new_mean1,
        new_var1,
        new_mean2,
        new_var2,
    )


MESH = pl.DeviceIdType.MESH
F32 = jnp.float32
BF16 = jnp.bfloat16
LANES = 128
PLANE = 2


def nn(a, b, precision=None):
    return lax.dot_general(
        a, b, (((1,), (0,)), ((), ())), precision=precision, preferred_element_type=F32
    )


def nt(a, b, precision=None):
    return lax.dot_general(
        a, b, (((1,), (1,)), ((), ())), precision=precision, preferred_element_type=F32
    )


def tn(a, b, precision=None):
    return lax.dot_general(
        a, b, (((0,), (0,)), ((), ())), precision=precision, preferred_element_type=F32
    )


def rows_first(field, images):
    return jnp.concatenate(
        [
            field[(m * SIDE + i) * SIDE : (m * SIDE + i + 1) * SIDE]
            for i in range(SIDE)
            for m in range(images)
        ]
    )


def images_first(field, images):
    return jnp.concatenate(
        [
            field[(i * images + m) * SIDE : (i * images + m + 1) * SIDE]
            for m in range(images)
            for i in range(SIDE)
        ]
    )


def store_taps(put, field, block):
    cells, width = field.shape
    tiles = field.reshape(cells // SIDE, SIDE, width)
    column = lax.broadcasted_iota(jnp.int32, tiles.shape, 1)
    left = jnp.where(column == 0, 0.0, pltpu.roll(tiles, 1, 1)).reshape(cells, width)
    right = jnp.where(column == SIDE - 1, 0.0, pltpu.roll(tiles, SIDE - 1, 1)).reshape(
        cells, width
    )
    for lateral, shifted in enumerate((left, field, right)):
        put(lateral, pl.ds(block, cells), shifted.astype(BF16))


def row_sum(field):
    return jnp.sum(field, axis=0, keepdims=True)


def halves(row):
    return [row[:, at : at + LANES] for at in range(0, row.shape[1], LANES)]


def image_terms(logits, teacher, labels):
    def parts(values):
        top = jnp.max(values, axis=1, keepdims=True)
        weights = jnp.exp(values - top)
        total = jnp.sum(weights, axis=1, keepdims=True)
        return top + jnp.log(total), weights / total

    onehot = (
        labels == lax.broadcasted_iota(jnp.int32, logits.shape, 1)
    ).astype(F32)
    full_lse, full_soft = parts(logits)
    pupil = logits / softening_heat
    mentor = teacher / softening_heat
    pupil_rest = pupil - 1000.0 * onehot
    mentor_rest = mentor - 1000.0 * onehot
    pupil_all, pupil_soft = parts(pupil)
    mentor_all, _ = parts(mentor)
    pupil_other, pupil_rest_soft = parts(pupil_rest)
    mentor_other, mentor_rest_soft = parts(mentor_rest)

    def pick(values):
        return jnp.sum(onehot * values, axis=1, keepdims=True)

    pupil_hit = pick(pupil) - pupil_all
    mentor_hit = pick(mentor) - mentor_all
    pupil_miss = pupil_other - pupil_all
    mentor_miss = mentor_other - mentor_all
    hit_weight, miss_weight = jnp.exp(mentor_hit), jnp.exp(mentor_miss)
    binary = hit_weight * (mentor_hit - pupil_hit) + miss_weight * (
        mentor_miss - pupil_miss
    )
    gap = (mentor_rest - mentor_other) - (pupil_rest - pupil_other)
    spread = jnp.sum(mentor_rest_soft * gap, axis=1, keepdims=True)
    squared = softening_heat * softening_heat
    value = (
        full_lse
        - pick(logits)
        + squared * (target_weight * binary + other_weight * spread)
    )
    binary_slope = (
        (hit_weight + miss_weight) * pupil_soft
        - hit_weight * onehot
        - miss_weight * pupil_rest_soft
    )
    spread_slope = pupil_rest_soft - mentor_rest_soft
    slope = (
        full_soft
        - onehot
        + softening_heat
        * (target_weight * binary_slope + other_weight * spread_slope)
    )
    return value, slope


def block_kernel(
    sizes,
    features,
    counts,
    labels,
    teacher,
    conv1,
    conv2,
    head_weight,
    head_bias,
    *rest,
):
    params, rest = rest[:8], rest[8:]
    (
        out_cells,
        out_quarters,
        out_small,
        weight1,
        weight2,
        teacher_here,
        labels_here,
        head_here,
        head_bias_here,
        params_here,
        cells_in,
        params_all,
        counts_all,
        head_all,
        sums_all,
        logit_stage,
        logit_all,
        head_part,
        field,
        normed1,
        slope1,
        normed2,
        grad_pre2,
        taps_x,
        taps_h,
        taps_g,
        raw_x,
        raw_h,
        strip_taps,
        live_taps,
        live_rows,
        norm_part,
        norm_edges,
        live_part,
        live_edges,
        columns,
        strip_stage,
        strip_all,
        column_part,
        column_stage,
        column_all,
        mean_all,
        edge_part,
        edge_all,
        quarter_all,
        cells_stage,
        cells_out,
        load_sem,
        send_sem,
        sums_send,
        sums_recv,
        logit_recv,
        head_part_recv,
        cells_recv,
        params_recv,
        counts_recv,
        head_recv,
        weight_recv,
        raw_recv,
        strip_recv,
        column_recv,
        mean_recv,
        edge_recv,
        quarter_recv,
        out_recv,
    ) = rest
    n_batch, n_mp, channels, images = sizes
    n_z = n_mp // PLANE
    width = channels // n_mp
    quarter = width // n_batch
    block = images * SIDE
    cells = block * SIDE
    everyone = n_batch * n_mp
    b, p = lax.axis_index("batch"), lax.axis_index("mp")
    x, c = b // PLANE, b % PLANE
    z, y = p // PLANE, p % PLANE
    me = b * n_mp + p
    seat = y * n_batch + b
    n_seats = PLANE * n_batch
    means_end_value = {}
    sent = []

    def send(src, dst, recv, to_b, to_p):
        copy = pltpu.make_async_remote_copy(
            src_ref=src,
            dst_ref=dst,
            send_sem=send_sem.at[len(sent)],
            recv_sem=recv,
            device_id=(to_b, to_p),
            device_id_type=MESH,
        )
        copy.start()
        sent.append(copy)

    def await_bytes(ref, sem):
        pltpu.make_async_copy(ref, ref, sem).wait()

    far = [
        lambda v: v + 1 - 2 * (v % 2),
        lambda v: (v + n_z // 2) % n_z,
        lambda v: n_z - 1 - v,
    ]
    others = [
        (((x + dx) % 2) * PLANE + (c + dc) % 2, at_z * PLANE + (y + dy) % 2)
        for at_z in [other(z) for other in reversed(far)] + [z]
        for dy in (1, 0)
        for dx in (1, 0)
        for dc in (1, 0)
    ][:-1]

    loads = [
        (conv1, weight1.at[:, pl.ds(pl.multiple_of(p * width, width), width), :]),
        (conv2, weight2.at[:, pl.ds(pl.multiple_of(p * width, width), width), :]),
        (teacher, teacher_here),
        (labels, labels_here),
        (head_weight, head_here),
        (head_bias, head_bias_here),
    ] + [(ref, params_here.at[i]) for i, ref in enumerate(params)]
    loads = [
        pltpu.make_async_copy(src, dst, load_sem.at[i])
        for i, (src, dst) in enumerate(loads)
    ]
    for load in loads:
        load.start()
    barrier = pltpu.get_barrier_semaphore()
    for to_b, to_p in others:
        pl.semaphore_signal(
            barrier, inc=1, device_id=(to_b, to_p), device_id_type=MESH
        )

    for taps in (taps_x, taps_h, taps_g):
        for lateral in range(3):
            taps[lateral, 0:block] = jnp.zeros((block, channels), BF16)
            taps[lateral, block + cells : 2 * block + cells] = jnp.zeros(
                (block, channels), BF16
            )
    for load in loads:
        load.wait()
    group = LANES // width
    place = pl.multiple_of((p % group) * width, width)
    own_params = jnp.concatenate(
        [params_here[i] for i in range(4)] + [jnp.zeros((4, width), F32)]
    )
    own_params = jnp.concatenate(
        [own_params, jnp.zeros((8, LANES - width), F32)], axis=1
    )
    params_all[p] = pltpu.roll(own_params, place, 1)
    count = counts[0]
    counts_all[b] = jnp.zeros((8, LANES), F32) + count.astype(F32)
    head_all[p] = jnp.concatenate(
        [
            head_here[...],
            jnp.zeros((width, LANES - head_here.shape[1]), BF16),
        ],
        axis=1,
    )

    pl.semaphore_wait(barrier, everyone - 1)

    half = pl.ds(pl.multiple_of(c * LANES, LANES), LANES)
    strip = width // PLANE

    def rows_of(at_z, at_y, at_x):
        start = (at_z * PLANE + at_y) * width + at_x * strip
        return pl.ds(pl.multiple_of(start, strip), strip)

    mates = [(1, 0), (0, 1), (1, 1)]

    def column_start(which, weight):
        part = weight.at[:, rows_of(z, y, x), half]
        for k, other in enumerate(far):
            send(part, part, weight_recv.at[which, k], b, other(z) * PLANE + y)

    def shard_start(which, weight):
        part = weight.at[
            :, pl.ds(pl.multiple_of(p * width, width), width), half
        ]
        send(part, part, weight_recv.at[which, 3], b, z * PLANE + 1 - y)

    def layer_start(which, weight):
        for k, other in enumerate(far):
            part = weight.at[:, rows_of(other(z), y, x), half]
            await_bytes(part, weight_recv.at[which, k])
            for i, (dx, dy) in enumerate(mates):
                send(
                    part,
                    part,
                    weight_recv.at[which, 4 + 3 * k + i],
                    ((x + dx) % 2) * PLANE + c,
                    z * PLANE + (y + dy) % 2,
                )

    def core_start(which, weight):
        part = weight.at[
            :,
            pl.ds(
                pl.multiple_of((z * PLANE + 1 - y) * width, width), width
            ),
            half,
        ]
        await_bytes(part, weight_recv.at[which, 3])
        send(part, part, weight_recv.at[which, 13], x * PLANE + 1 - c, p)
        for k, other in enumerate(far):
            for i, (dx, dy) in enumerate(mates):
                part = weight.at[
                    :, rows_of(other(z), (y + dy) % 2, (x + dx) % 2), half
                ]
                await_bytes(part, weight_recv.at[which, 4 + 3 * k + i])
            part = weight.at[
                :,
                pl.ds(
                    pl.multiple_of(other(z) * PLANE * width, PLANE * width),
                    PLANE * width,
                ),
                half,
            ]
            send(part, part, weight_recv.at[which, 14 + k], x * PLANE + 1 - c, p)

    def core_end(which, weight):
        theirs = pl.ds(pl.multiple_of((1 - c) * LANES, LANES), LANES)
        part = weight.at[
            :,
            pl.ds(
                pl.multiple_of((z * PLANE + 1 - y) * width, width), width
            ),
            theirs,
        ]
        await_bytes(part, weight_recv.at[which, 13])
        for k, other in enumerate(far):
            part = weight.at[
                :,
                pl.ds(
                    pl.multiple_of(other(z) * PLANE * width, PLANE * width),
                    PLANE * width,
                ),
                theirs,
            ]
            await_bytes(part, weight_recv.at[which, 14 + k])

    column_start(0, weight1)
    shard_start(0, weight1)

    def cells_of(q):
        return pl.ds(pl.multiple_of(q * cells, cells), cells)

    own_cells = pltpu.make_async_copy(
        features.at[:, cells_of(p)], cells_in.at[p], load_sem.at[0]
    )
    own_cells.start()
    for k in range(1, n_mp):
        q = (p + k) % n_mp
        send(features.at[:, cells_of(q)], cells_in.at[p], cells_recv.at[k], b, q)
    column_start(1, weight2)
    for k in range(1, n_mp):
        q = (p + k) % n_mp
        send(params_all.at[p], params_all.at[p], params_recv.at[k], b, q)
        send(head_all.at[p], head_all.at[p], head_recv.at[k], b, q)
    for j in range(1, n_batch):
        send(
            counts_all.at[b],
            counts_all.at[b],
            counts_recv.at[j],
            (b + j) % n_batch,
            p,
        )

    layer_start(0, weight1)
    own_cells.wait()
    for k in range(1, n_mp):
        q = (p + n_mp - k) % n_mp
        await_bytes(cells_in.at[q], cells_recv.at[k])
    by_channel = cells_in[...].reshape(channels, cells).astype(F32)
    by_cell = rows_first(by_channel.T, images)
    field[...] = by_cell

    def put_x(lateral, where, value):
        taps_x[lateral, where] = value

    store_taps(put_x, by_cell, block)
    raw_x[seat] = by_cell.astype(BF16)

    shard_start(1, weight2)
    layer_start(1, weight2)
    core_start(0, weight1)

    for k in range(1, n_mp):
        q = (p + n_mp - k) % n_mp
        await_bytes(params_all.at[q], params_recv.at[k])
        await_bytes(head_all.at[q], head_recv.at[k])
    for j in range(1, n_batch):
        await_bytes(counts_all.at[(b + n_batch - j) % n_batch], counts_recv.at[j])
    full_params = jnp.concatenate(
        [
            sum(params_all[q] for q in range(at, at + group))
            for at in range(0, n_mp, group)
        ],
        axis=1,
    )
    gain1, bias1, gain2, bias2 = (full_params[i : i + 1] for i in range(4))
    live_images = sum(counts_all[i] for i in range(n_batch))[0:1, 0:1]
    live_cells = live_images * float(SIDE * SIDE)

    slot = (lax.broadcasted_iota(jnp.int32, (cells, channels), 0) // SIDE) % images
    live = (slot + p * images < count).astype(F32)

    shape = (cells, LANES)
    cell = lax.broadcasted_iota(jnp.int32, shape, 0)
    tap_at = lax.broadcasted_iota(jnp.int32, shape, 1)
    down = (tap_at >= 3).astype(jnp.int32) + (tap_at >= 6).astype(jnp.int32)
    across = tap_at - 3 * down
    at_row = cell // block + down - 1
    at_column = cell % SIDE + across - 1
    within = (at_row >= 0) & (at_row < SIDE) & (at_column >= 0) & (at_column < SIDE)
    inside = jnp.where(within & (tap_at < 9), 1.0, 0.0).astype(BF16)

    def conv(taps, weight):
        total = None
        for tap in range(9):
            vertical, lateral = divmod(tap, 3)
            term = nt(
                taps[lateral, block * vertical : block * vertical + cells],
                weight[tap],
            )
            total = term if total is None else total + term
        return total

    def conv_back(taps, weight):
        total = None
        for tap in range(9):
            vertical, lateral = divmod(tap, 3)
            up = block * (2 - vertical)
            term = nn(taps[2 - lateral, up : up + cells], weight[tap])
            total = term if total is None else total + term
        return total

    def sums_start(which, one, two):
        mine = sums_all.at[which, me, pl.ds(0, 4)]
        sums_all[which, me, 0:4] = jnp.concatenate(halves(one) + halves(two))
        for to_b, to_p in others:
            pltpu.make_async_remote_copy(
                src_ref=mine,
                dst_ref=mine,
                send_sem=sums_send.at[which],
                recv_sem=sums_recv.at[which],
                device_id=(to_b, to_p),
                device_id_type=MESH,
            ).start()

    def sums_end(which):
        everything = sums_all.at[which, pl.ds(0, everyone - 1), pl.ds(0, 4)]
        await_bytes(everything, sums_recv.at[which])
        total = jnp.sum(sums_all[which], axis=0)
        return (
            jnp.concatenate([total[0:1], total[1:2]], axis=1),
            jnp.concatenate([total[2:3], total[3:4]], axis=1),
        )

    def means_start(which, value):
        mean_all[which, z] = jnp.concatenate(
            halves(row_sum(value) / float(cells))
            + [jnp.zeros((8 - channels // LANES, LANES), F32)]
        )
        part = mean_all.at[which, z]
        for k, other in enumerate(far):
            send(part, part, mean_recv.at[which, k], b, other(z) * PLANE + y)

    def means_end(which):
        for k, other in enumerate(far):
            await_bytes(mean_all.at[which, other(z)], mean_recv.at[which, k])
        total = sum(mean_all[which, at_z] for at_z in range(n_z)) / float(n_z)
        return jnp.concatenate(
            [total[i : i + 1] for i in range(channels // LANES)], axis=1
        )

    def raw_start(which, raw):
        part = raw.at[seat]
        for i, (dx, dy) in enumerate(mates):
            send(
                part,
                part,
                raw_recv.at[which, i],
                ((x + dx) % 2) * PLANE + c,
                z * PLANE + (y + dy) % 2,
            )
        send(part, part, raw_recv.at[which, 3], x * PLANE + 1 - c, p)

    def seat_of(dx, dy, dc):
        return ((y + dy) % 2) * n_batch + ((x + dx) % 2) * PLANE + (c + dc) % 2

    def raw_forward(which, raw):
        for i, (dx, dy) in enumerate(mates):
            part = raw.at[seat_of(dx, dy, 0)]
            await_bytes(part, raw_recv.at[which, i])
            send(part, part, raw_recv.at[which, 4 + i], x * PLANE + 1 - c, p)

    def raw_end(which, raw):
        await_bytes(raw.at[seat_of(0, 0, 1)], raw_recv.at[which, 3])
        for i, (dx, dy) in enumerate(mates):
            await_bytes(raw.at[seat_of(dx, dy, 1)], raw_recv.at[which, 4 + i])

    seats = [
        (dx, dy, dc)
        for dy in (1, 0)
        for dx in (1, 0)
        for dc in (1, 0)
        if dx or dy or dc
    ]

    def strips_start(which, value):
        by_row = value.T
        for s in range(n_seats):
            at_y, at_b = divmod(s, n_batch)
            strip_stage[which, s] = jnp.concatenate(
                [
                    by_row[start : start + quarter]
                    for start in (
                        (at_z * PLANE + at_y) * width + at_b * quarter
                        for at_z in range(n_z)
                    )
                ]
            ).astype(BF16)
        for i, (dx, dy, dc) in enumerate(seats):
            send(
                strip_stage.at[which, seat_of(dx, dy, dc)],
                strip_all.at[which, seat],
                strip_recv.at[which, i],
                ((x + dx) % 2) * PLANE + (c + dc) % 2,
                z * PLANE + (y + dy) % 2,
            )
        strip_all[which, seat] = strip_stage[which, seat]

    shape = (9, 1, cells)
    cell = lax.broadcasted_iota(jnp.int32, shape, 2)
    tap_at = lax.broadcasted_iota(jnp.int32, shape, 0)
    down = (tap_at >= 3).astype(jnp.int32) + (tap_at >= 6).astype(jnp.int32)
    from_row = cell // block - down + 1
    from_column = cell % SIDE - (tap_at - 3 * down) + 1
    reach = jnp.where(
        (from_row >= 0)
        & (from_row < SIDE)
        & (from_column >= 0)
        & (from_column < SIDE),
        1.0,
        0.0,
    )

    def moved(value, tap):
        vertical, lateral = divmod(tap, 3)
        ahead = (vertical - 1) * block + lateral - 1
        return (pltpu.roll(value, ahead % cells, 1) if ahead else value) * reach[tap]

    strips = n_z * quarter

    def strips_product(which, raw):
        for i, (dx, dy, dc) in enumerate(seats):
            await_bytes(
                strip_all.at[which, seat_of(dx, dy, dc)], strip_recv.at[which, i]
            )
        for s in range(n_seats):
            value = strip_all[which, s].astype(F32)
            for tap in range(9):
                strip_taps[
                    tap * strips : (tap + 1) * strips, s * cells : (s + 1) * cells
                ] = moved(value, tap).astype(BF16)
        edges = sum(nn(strip_all[which, s], inside) for s in range(n_seats))
        return nn(strip_taps[...], raw[...].reshape(-1, channels)), edges

    def live_of(at_y, at_b):
        lane = lax.broadcasted_iota(jnp.int32, (8, cells), 1)
        image = (lane // SIDE) % images + (z * PLANE + at_y) * images
        return (image.astype(F32) < counts_all[at_b][:, 0:1]).astype(F32)

    def norm_product(raw):
        product, edges = strips_product(2, raw)
        norm_part[...] = product
        norm_edges[...] = edges
        live_part[...] = nn(
            live_taps[...].astype(BF16), raw[...].reshape(-1, channels)
        )
        live_edges[...] = nn(live_rows[...].astype(BF16), inside)

    def own_column(row):
        columns[...] = jnp.broadcast_to(row, (LANES, channels)).T
        return jnp.concatenate(
            [
                columns[
                    pl.ds(
                        pl.multiple_of(
                            (at_z * PLANE + y) * width + b * quarter, quarter
                        ),
                        quarter,
                    ),
                    :,
                ]
                for at_z in range(n_z)
            ]
        )[:, 0:1]

    def column_send(which, product, edges, sums=None):
        if sums is not None:
            bias_column, gain_column = (own_column(row / live_cells) for row in sums)
            edges = edges - (
                bias_column * row_sum(live_edges[...]) + gain_column * norm_edges[...]
            )
        mean = means_end(1 - which)
        means_end_value[which] = mean
        for at_z in range(n_z):
            edge_part[which, at_z] = edges[at_z * quarter : (at_z + 1) * quarter]
        for tap in range(9):
            rows = slice(tap * strips, (tap + 1) * strips)
            total = product[rows] - edges[:, tap : tap + 1] * mean
            if sums is not None:
                total = total - (
                    bias_column * live_part[tap : tap + 1]
                    + gain_column * norm_part[rows]
                )
            for at_z in range(n_z):
                column_part[which, at_z, tap * quarter : (tap + 1) * quarter] = total[
                    at_z * quarter : (at_z + 1) * quarter
                ]
        for at_z in range(n_z):
            column_stage[which, at_z] = jnp.concatenate(
                halves(column_part[which, at_z])
            ).astype(BF16)
        for k, other in enumerate(far):
            send(
                column_stage.at[which, other(z)],
                column_all.at[which, k],
                column_recv.at[which, k],
                b,
                other(z) * PLANE + y,
            )
            send(
                edge_part.at[which, other(z)],
                edge_all.at[which, k],
                edge_recv.at[which, k],
                b,
                other(z) * PLANE + y,
            )

    def unfold(piece):
        return jnp.concatenate(
            [
                piece[at : at + 9 * quarter]
                for at in range(0, piece.shape[0], 9 * quarter)
            ],
            axis=1,
        )

    def quarters_start(which):
        for k in range(len(far)):
            await_bytes(column_all.at[which, k], column_recv.at[which, k])
            await_bytes(edge_all.at[which, k], edge_recv.at[which, k])
        mean = means_end_value[which]
        edges = edge_part[which, z]
        total = column_part[which, z]
        for k in range(len(far)):
            edges = edges + edge_all[which, k]
            total = total + unfold(column_all[which, k].astype(F32))
        back = jnp.concatenate([edges[:, tap : tap + 1] * mean for tap in range(9)])
        quarter_all[which, b] = jnp.concatenate(halves(total + back)).astype(BF16)
        for j in range(1, n_batch):
            part = quarter_all.at[which, b]
            send(part, part, quarter_recv.at[which, j], (b + j) % n_batch, p)

    def quarters_end(which):
        for j in range(1, n_batch):
            await_bytes(
                quarter_all.at[which, (b + n_batch - j) % n_batch],
                quarter_recv.at[which, j],
            )
        out_quarters[which] = quarter_all[which]

    live_taps[...] = jnp.zeros_like(live_taps)
    means_start(0, by_cell)
    core_end(0, weight1)
    first = conv(taps_x, weight1)
    masked = first * live
    sums_start(0, row_sum(masked), row_sum(masked * first))
    raw_start(0, raw_x)
    for s in range(n_seats):
        alive = live_of(*divmod(s, n_batch))
        live_rows[s : s + 1] = alive[0:1].astype(F32)
        for tap in range(9):
            live_taps[tap : tap + 1, s * cells : (s + 1) * cells] = moved(
                alive, tap
            )[0:1]
    core_start(1, weight2)
    total, square = sums_end(0)
    mean1 = total / live_cells
    var1 = square / live_cells - mean1 * mean1
    rstd1 = lax.rsqrt(var1 + epsilon)
    flat = (first - mean1) * rstd1
    normed1[...] = flat
    pre1 = gain1 * flat + bias1
    sigma1 = jax.nn.sigmoid(pre1)
    slope1[...] = sigma1 * (1.0 + pre1 * (1.0 - sigma1))
    hidden = pre1 * sigma1

    def put_h(lateral, where, value):
        taps_h[lateral, where] = value

    store_taps(put_h, hidden, block)
    raw_h[seat] = hidden.astype(BF16)
    means_start(1, hidden)
    core_end(1, weight2)

    second = conv(taps_h, weight2)
    masked = second * live
    sums_start(1, row_sum(masked), row_sum(masked * second))
    raw_start(1, raw_h)
    strips_start(2, normed1[...] * live)
    raw_forward(0, raw_x)
    total, square = sums_end(1)
    mean2 = total / live_cells
    var2 = square / live_cells - mean2 * mean2
    rstd2 = lax.rsqrt(var2 + epsilon)
    flat2 = (second - mean2) * rstd2
    normed2[...] = flat2
    pre2 = gain2 * flat2 + bias2 + field[...]
    sigma2 = jax.nn.sigmoid(pre2)
    block_out = pre2 * sigma2

    pooled = sum(block_out[i * block : (i + 1) * block] for i in range(SIDE))
    pooled = jnp.sum(pooled.reshape(images, SIDE, channels), axis=1) / float(
        SIDE * SIDE
    )
    head = head_all[...].reshape(channels, LANES).astype(F32)[:, 0 : head_here.shape[1]]
    logits = nn(pooled, head, highest) + head_bias_here[...]
    slots = labels_here.shape[1]
    image_at = lax.broadcasted_iota(jnp.int32, (images, slots), 0) + p * images
    picked = lax.broadcasted_iota(jnp.int32, (images, slots), 1) == image_at
    own_labels = jnp.sum(
        jnp.where(picked, labels_here[...], 0), axis=1, keepdims=True
    )
    own_teacher = nn(picked.astype(F32), teacher_here[...], highest)
    own_live = (image_at[:, 0:1] < count).astype(F32)
    per_image, slope = image_terms(logits, own_teacher, own_labels)
    grad_logits = slope * (own_live * (loss_scale / live_images))
    grad_pooled = nt(grad_logits, head, highest) / float(SIDE * SIDE)
    spread = jnp.concatenate(
        [
            jnp.broadcast_to(grad_pooled[m : m + 1], (SIDE, channels))
            for m in range(images)
        ]
    )
    spread = jnp.concatenate([spread] * SIDE)
    pre_grad2 = spread * (sigma2 * (1.0 + pre2 * (1.0 - sigma2)))
    grad_pre2[...] = pre_grad2
    sums_start(2, row_sum(pre_grad2), row_sum(pre_grad2 * flat2))

    raw_forward(1, raw_h)

    bias_grad2, gain_grad2 = sums_end(2)
    grad_second = (gain2 * rstd2) * (
        grad_pre2[...]
        - live * (bias_grad2 + normed2[...] * gain_grad2) / live_cells
    )
    strips_start(0, grad_second)

    def put_g(lateral, where, value):
        taps_g[lateral, where] = value

    store_taps(put_g, grad_second.astype(BF16).astype(F32), block)
    pre_grad1 = conv_back(taps_g, weight2) * slope1[...]
    sums_start(3, row_sum(pre_grad1), row_sum(pre_grad1 * normed1[...]))
    scale1 = gain1 * rstd1
    strips_start(1, scale1 * pre_grad1)
    classes = logits.shape[1]
    for q in range(n_mp):
        logit_stage[q] = jnp.zeros((2 * images, LANES), F32)
        logit_stage[q, 0:images, 0:classes] = grad_logits
        logit_stage[q, 0:images, classes : classes + 1] = own_live * per_image
        logit_stage[q, images : 2 * images, 0:width] = pooled[
            :, q * width : (q + 1) * width
        ]
    for k in range(1, n_mp):
        q = (p + k) % n_mp
        send(logit_stage.at[q], logit_all.at[p], logit_recv.at[k], b, q)
    logit_all[p] = logit_stage[p]
    raw_end(0, raw_x)
    norm_product(raw_x)
    raw_end(1, raw_h)
    product2, edges2 = strips_product(0, raw_h)
    column_send(0, product2, edges2)
    product1, edges1 = strips_product(1, raw_x)
    bias_grad1, gain_grad1 = sums_end(3)
    grad_first = (gain1 * rstd1) * (
        pre_grad1 - live * (bias_grad1 + normed1[...] * gain_grad1) / live_cells
    )
    column_send(1, product1, edges1, (scale1 * bias_grad1, scale1 * gain_grad1))
    store_taps(put_g, grad_first.astype(BF16).astype(F32), block)
    grad_in = conv_back(taps_g, weight1) + grad_pre2[...]
    cells_stage[...] = (
        images_first(grad_in, images).T.astype(BF16).reshape(n_mp, width, cells)
    )
    for k in range(1, n_mp):
        q = (p + k) % n_mp
        send(cells_stage.at[q], cells_out.at[p], out_recv.at[k], b, q)
    cells_out[p] = cells_stage[p]
    for k in range(1, n_mp):
        await_bytes(logit_all.at[(p + n_mp - k) % n_mp], logit_recv.at[k])
    both = logit_all[...]
    upper = lax.broadcasted_iota(jnp.int32, both.shape, 1) < images
    upper_logits = jnp.where(upper, both, 0.0).reshape(-1, LANES)
    lifted = jnp.where(upper, pltpu.roll(both, images, 1), 0.0).reshape(-1, LANES)
    head_part[b, 0:width] = tn(lifted, upper_logits, highest)[0:width]
    head_part[b, width : width + 8] = jnp.broadcast_to(
        row_sum(upper_logits), (8, LANES)
    )
    for j in range(1, n_batch):
        part = head_part.at[b]
        send(part, part, head_part_recv.at[j], (b + j) % n_batch, p)
    quarters_start(0)
    quarters_start(1)

    def own(row):
        pieces = halves(row)
        mine = pieces[0]
        for i in range(1, len(pieces)):
            mine = jnp.where(p // group == i, pieces[i], mine)
        return pltpu.roll(mine, (LANES - place) % LANES, 1)[:, 0:width]

    adjust = live_cells / (live_cells - 1.0)
    kept = 1.0 - momentum
    rows = [
        own(gain_grad1),
        own(bias_grad1),
        own(gain_grad2),
        own(bias_grad2),
        kept * params_here[4] + momentum * own(mean1),
        kept * params_here[5] + momentum * own(var1 * adjust),
        kept * params_here[6] + momentum * own(mean2),
        kept * params_here[7] + momentum * own(var2 * adjust),
    ]
    out_small[...] = jnp.zeros_like(out_small)
    for i, row in enumerate(rows):
        out_small[i : i + 1, 0:width] = row
    for j in range(1, n_batch):
        await_bytes(head_part.at[(b + n_batch - j) % n_batch], head_part_recv.at[j])
    head_sum = sum(head_part[at_b] for at_b in range(n_batch))
    out_small[16 : 16 + width] = head_sum[0:width]
    last = head_sum[width : width + 1]
    out_small[8:9] = last
    out_small[9:10] = jnp.broadcast_to(
        last[:, classes : classes + 1] / live_images, (1, LANES)
    )

    quarters_end(0)
    for k in range(1, n_mp):
        q = (p + n_mp - k) % n_mp
        await_bytes(cells_out.at[q], out_recv.at[k])
    out_cells[...] = cells_out[...]
    quarters_end(1)

    for copy in sent:
        copy.wait_send()
    for which in range(4):
        await_bytes(
            sums_all.at[which, pl.ds(0, everyone - 1), pl.ds(0, 4)],
            sums_send.at[which],
        )


def finish_kernel(
    cells_in,
    quarters_in,
    small,
    loss,
    features_out,
    conv1_out,
    gain1_out,
    bias1_out,
    conv2_out,
    gain2_out,
    bias2_out,
    head_out,
    head_bias_out,
    *stats_out,
):
    n_mp, _, cells = cells_in.shape
    for q in range(n_mp):
        features_out[:, q * cells : (q + 1) * cells] = cells_in[q].astype(F32)
    n_batch = quarters_in.shape[1]
    quarter = conv1_out.shape[1] // n_batch
    for which, out in enumerate((conv2_out, conv1_out)):
        for at_b in range(n_batch):
            whole = quarters_in[which, at_b].astype(F32)
            for start in range(0, whole.shape[0], quarter):
                tap, lanes = start // quarter % 9, start // quarter // 9 * LANES
                out[
                    tap, at_b * quarter : (at_b + 1) * quarter, lanes : lanes + LANES
                ] = whole[start : start + quarter]
    vectors = (gain1_out, bias1_out, gain2_out, bias2_out) + stats_out
    for i, out in enumerate(vectors):
        out[...] = small[i : i + 1, 0 : out.shape[1]]
    head_bias_out[...] = small[8:9, 0 : head_bias_out.shape[1]]
    loss[0] = small[9, 0]
    head_out[...] = small[16 : 16 + head_out.shape[0], 0 : head_out.shape[1]]


def block_device(
    n_batch,
    n_mp,
    features,
    counts,
    labels,
    teacher,
    conv1_weight,
    bn1_gain,
    bn1_bias,
    conv2_weight,
    bn2_gain,
    bn2_bias,
    head_weight,
    head_bias,
    run_mean1,
    run_var1,
    run_mean2,
    run_var2,
):
    width, cell_count = features.shape
    channels = width * n_mp
    classes = head_weight.shape[1]
    slots = cell_count // (SIDE * SIDE)
    images = slots // n_mp
    block = images * SIDE
    cells = block * SIDE
    n_z = n_mp // PLANE
    quarter = width // n_batch
    seats = n_batch * PLANE
    everyone = n_batch * n_mp
    tall = 9 * quarter * (channels // LANES)
    padded = cells + 2 * block

    def row(values):
        return values.reshape(1, -1)

    def taps_out(values):
        return values.transpose(1, 0, 2)

    def vmem(*shape, dtype=F32):
        return pltpu.VMEM(shape, dtype)

    def low(*shape):
        return pltpu.VMEM(shape, BF16)

    any_space = pl.BlockSpec(memory_space=pl.ANY)
    in_vmem = pl.BlockSpec(memory_space=pltpu.VMEM)
    in_smem = pl.BlockSpec(memory_space=pltpu.SMEM)
    shape = jax.ShapeDtypeStruct
    dma = pltpu.SemaphoreType.DMA
    grant = pltpu.CompilerParams(
        collective_id=0, has_side_effects=True, vmem_limit_bytes=60 * 2**20
    )
    packed = pl.pallas_call(
        functools.partial(block_kernel, (n_batch, n_mp, channels, images)),
        out_shape=(
            shape((n_mp, width, cells), BF16),
            shape((2, n_batch, tall, LANES), BF16),
            shape((16 + width, LANES), F32),
        ),
        in_specs=[any_space, in_smem] + [any_space] * 14,
        out_specs=(in_vmem,) * 3,
        scratch_shapes=[
            low(9, channels, channels),
            low(9, channels, channels),
            vmem(slots, classes),
            vmem(1, slots, dtype=jnp.int32),
            low(width, classes),
            vmem(1, classes),
            vmem(8, 1, width),
            low(n_mp, width, cells),
            vmem(n_mp, 8, LANES),
            vmem(n_batch, 8, LANES),
            low(n_mp, width, LANES),
            vmem(4, everyone, 8, LANES),
            vmem(n_mp, 2 * images, LANES),
            vmem(n_mp, 2 * images, LANES),
            vmem(n_batch, width + 8, LANES),
            vmem(cells, channels),
            vmem(cells, channels),
            vmem(cells, channels),
            vmem(cells, channels),
            vmem(cells, channels),
            low(3, padded, channels),
            low(3, padded, channels),
            low(3, padded, channels),
            low(seats, cells, channels),
            low(seats, cells, channels),
            low(9 * n_z * quarter, seats * cells),
            vmem(16, seats * cells),
            vmem(8, cells),
            vmem(9 * n_z * quarter, channels),
            vmem(n_z * quarter, LANES),
            vmem(16, channels),
            vmem(8, LANES),
            vmem(channels, LANES),
            low(3, seats, n_z * quarter, cells),
            low(3, seats, n_z * quarter, cells),
            vmem(2, n_z, 9 * quarter, channels),
            low(2, n_z, tall, LANES),
            low(2, n_z - 1, tall, LANES),
            vmem(2, n_z, 8, LANES),
            vmem(2, n_z, quarter, LANES),
            vmem(2, n_z - 1, quarter, LANES),
            low(2, n_batch, tall, LANES),
            low(n_mp, width, cells),
            low(n_mp, width, cells),
            dma((14,)),
            dma((160,)),
            dma((4,)),
            dma((4,)),
            dma((n_mp,)),
            dma((n_batch,)),
            dma((n_mp,)),
            dma((n_mp,)),
            dma((n_batch,)),
            dma((n_mp,)),
            dma((2, 17)),
            dma((2, 7)),
            dma((3, 7)),
            dma((2, n_z - 1)),
            dma((2, n_z - 1)),
            dma((2, n_z - 1)),
            dma((2, n_batch)),
            dma((n_mp,)),
        ],
        compiler_params=grant,
    )(
        features,
        counts,
        row(labels),
        teacher,
        taps_out(conv1_weight),
        taps_out(conv2_weight),
        head_weight,
        row(head_bias),
        row(bn1_gain),
        row(bn1_bias),
        row(bn2_gain),
        row(bn2_bias),
        row(run_mean1),
        row(run_var1),
        row(run_mean2),
        row(run_var2),
    )
    vector = shape((1, width), F32)
    results = pl.pallas_call(
        finish_kernel,
        out_shape=(
            shape((1,), F32),
            shape((width, cell_count), F32),
            shape((9, width, channels), F32),
            vector,
            vector,
            shape((9, width, channels), F32),
            vector,
            vector,
            shape((width, classes), F32),
            shape((1, classes), F32),
            vector,
            vector,
            vector,
            vector,
        ),
        in_specs=[in_vmem] * 3,
        out_specs=(in_smem,) + (in_vmem,) * 13,
        compiler_params=pltpu.CompilerParams(vmem_limit_bytes=60 * 2**20),
    )(*packed)
    loss, grad_features, conv1, gain1, bias1, conv2, gain2, bias2, head, *small = results
    return (
        loss.reshape(()),
        grad_features,
        taps_out(conv1),
        gain1.reshape(-1),
        bias1.reshape(-1),
        taps_out(conv2),
        gain2.reshape(-1),
        bias2.reshape(-1),
        head,
    ) + tuple(values.reshape(-1) for values in small)


def by_images(n_batch, n_mp, features, counts, *rest):
    width, cell_count = features.shape
    images = cell_count // (SIDE * SIDE) // n_mp
    fits = (
        n_batch == 4
        and n_mp == 8
        and width == 32
        and images == 4
        and head_fits(rest)
    )
    if not fits:
        return plain_device(features, counts, *rest)
    return block_device(n_batch, n_mp, features, counts, *rest)


def head_fits(rest):
    return rest[8].shape[1] < LANES


def solution(mesh):
    return jax.shard_map(
        functools.partial(by_images, mesh.shape["batch"], mesh.shape["mp"]),
        mesh=mesh,
        in_specs=(
            P("mp", "batch"),
            P("batch"),
            P("batch"),
            P("batch", None),
            P("mp", None, None),
            P("mp"),
            P("mp"),
            P("mp", None, None),
            P("mp"),
            P("mp"),
            P("mp", None),
            P(),
            P("mp"),
            P("mp"),
            P("mp"),
            P("mp"),
        ),
        out_specs=(
            P(),
            P("mp", "batch"),
            P("mp", None, None),
            P("mp"),
            P("mp"),
            P("mp", None, None),
            P("mp"),
            P("mp"),
            P("mp", None),
            P(),
            P("mp"),
            P("mp"),
            P("mp"),
            P("mp"),
        ),
        check_vma=False,
    )
```

```python
import functools

import jax
import jax.numpy as jnp
from jax import lax
from jax.experimental import pallas as pl
from jax.experimental.pallas import tpu as pltpu
from jax.sharding import PartitionSpec as P

SIDE = 8


epsilon = 1e-05
softening_heat = 4.0
target_weight = 1.0
other_weight = 8.0
loss_scale = 1024.0
momentum = 0.1
highest = lax.Precision.HIGHEST


def shifted_taps(field, sign):
    channels = field.shape[0]
    planes = field.reshape(channels, -1, SIDE, SIDE)
    padded = jnp.pad(planes, ((0, 0), (0, 0), (1, 1), (1, 1)))
    pieces = []
    for vertical in range(3):
        for lateral in range(3):
            row_start = 1 + sign * (vertical - 1)
            col_start = 1 + sign * (lateral - 1)
            pieces.append(
                padded[:, :, row_start : row_start + SIDE, col_start : col_start + SIDE].reshape(
                    channels, -1
                )
            )
    return jnp.stack(pieces)


def image_losses(class_logits, teacher, labels):
    onehot = (labels[:, None] == jnp.arange(class_logits.shape[1])[None, :]).astype(
        class_logits.dtype
    )
    cross = jax.nn.logsumexp(class_logits, axis=1) - jnp.sum(onehot * class_logits, axis=1)
    pupil_network = class_logits / softening_heat
    mentor_network = teacher / softening_heat
    student_rest = pupil_network - 1000.0 * onehot
    tutor_rest = mentor_network - 1000.0 * onehot
    student_all = jax.nn.logsumexp(pupil_network, axis=1)
    tutor_all = jax.nn.logsumexp(mentor_network, axis=1)
    student_other = jax.nn.logsumexp(student_rest, axis=1)
    tutor_other = jax.nn.logsumexp(tutor_rest, axis=1)
    student_hit = jnp.sum(onehot * pupil_network, axis=1) - student_all
    tutor_hit = jnp.sum(onehot * mentor_network, axis=1) - tutor_all
    student_miss = student_other - student_all
    tutor_miss = tutor_other - tutor_all
    binary = jnp.exp(tutor_hit) * (tutor_hit - student_hit) + jnp.exp(tutor_miss) * (
        tutor_miss - student_miss
    )
    tutor_log = tutor_rest - tutor_other[:, None]
    student_log = student_rest - student_other[:, None]
    spread = jnp.sum(jnp.exp(tutor_log) * (tutor_log - student_log), axis=1)
    squared_value = softening_heat * softening_heat
    return cross + squared_value * (target_weight * binary + other_weight * spread)


def silu_slope(values):
    sigma = jax.nn.sigmoid(values)
    return sigma * (1.0 + values * (1.0 - sigma))


def conv_piece(weight, piece):
    return jnp.einsum(
        "otc,tcn->on", weight, shifted_taps(piece, 1), preferred_element_type=jnp.float32
    )


def weight_piece(grad_low, piece):
    return jnp.einsum(
        "on,tcn->otc", grad_low, shifted_taps(piece, 1), preferred_element_type=jnp.float32
    )


def input_piece(weight, back_taps):
    return jnp.einsum("otc,ton->cn", weight, back_taps, preferred_element_type=jnp.float32)


def plain_device(
    features,
    counts,
    labels,
    teacher,
    conv1_weight,
    bn1_gain,
    bn1_bias,
    conv2_weight,
    bn2_gain,
    bn2_bias,
    head_weight,
    head_bias,
    run_mean1,
    run_var1,
    run_mean2,
    run_var2,
):
    channels, cell_count = features.shape
    image_area = SIDE * SIDE
    image_slots = cell_count // image_area
    image_present = (lax.broadcasted_iota(jnp.int32, (image_slots,), 0) < counts[0]).astype(
        jnp.float32
    )
    cell_live = jnp.broadcast_to(image_present[:, None], (image_slots, image_area)).reshape(-1)
    residual_in = features.astype(jnp.float32)
    first = conv_piece(conv1_weight, lax.all_gather(features, "mp", axis=0, tiled=True))
    first_sum, first_square, cells = lax.psum(
        (
            jnp.sum(first * cell_live[None, :], axis=1),
            jnp.sum(first * first * cell_live[None, :], axis=1),
            jnp.sum(cell_live),
        ),
        "batch",
    )
    mean1 = first_sum / cells
    var1 = first_square / cells - mean1 * mean1
    rstd1 = lax.rsqrt(var1 + epsilon)
    normed1 = (first - mean1[:, None]) * rstd1[:, None]
    pre1 = bn1_gain[:, None] * normed1 + bn1_bias[:, None]
    hidden = jax.nn.silu(pre1).astype(jnp.bfloat16)
    second = conv_piece(conv2_weight, lax.all_gather(hidden, "mp", axis=0, tiled=True))
    second_sum, second_square = lax.psum(
        (
            jnp.sum(second * cell_live[None, :], axis=1),
            jnp.sum(second * second * cell_live[None, :], axis=1),
        ),
        "batch",
    )
    mean2 = second_sum / cells
    var2 = second_square / cells - mean2 * mean2
    rstd2 = lax.rsqrt(var2 + epsilon)
    normed2 = (second - mean2[:, None]) * rstd2[:, None]
    pre2 = bn2_gain[:, None] * normed2 + bn2_bias[:, None] + residual_in
    block_out = jax.nn.silu(pre2)
    pooled = jnp.mean(block_out.reshape(channels, image_slots, image_area), axis=2)
    head_local = head_weight.astype(jnp.float32)
    partial_logits = jnp.einsum("cm,ck->mk", pooled, head_local, precision=highest)
    class_logits = lax.psum(partial_logits, "mp") + head_bias[None, :]
    image_batch = cells / image_area

    def losses_of(values):
        return image_losses(values, teacher, labels)

    per_image, pullback = jax.vjp(losses_of, class_logits)
    loss_part = jnp.sum(image_present * per_image)
    (grad_logits,) = pullback(image_present * (loss_scale / image_batch))
    head_grad = jnp.einsum("cm,mk->ck", pooled, grad_logits, precision=highest)
    head_bias_grad = jnp.sum(grad_logits, axis=0)
    grad_pooled = jnp.einsum("mk,ck->cm", grad_logits, head_local, precision=highest) / image_area
    grad_out = jnp.broadcast_to(
        grad_pooled[:, :, None], (channels, image_slots, image_area)
    ).reshape(channels, -1)
    grad_pre2 = grad_out * silu_slope(pre2)
    loss_total = lax.psum(loss_part, "batch")
    bias2_grad, gain2_grad = lax.psum(
        (jnp.sum(grad_pre2, axis=1), jnp.sum(grad_pre2 * normed2, axis=1)), "batch"
    )
    loss = loss_total / image_batch
    grad_second = (bn2_gain * rstd2)[:, None] * (
        grad_pre2
        - cell_live[None, :] * (bias2_grad[:, None] + normed2 * gain2_grad[:, None]) / cells
    )
    second_low = grad_second.astype(jnp.bfloat16)
    conv2_grad = weight_piece(second_low, lax.all_gather(hidden, "mp", axis=0, tiled=True))
    back_second = shifted_taps(second_low, -1)
    grad_hidden = lax.psum_scatter(
        input_piece(conv2_weight, back_second), "mp", scatter_dimension=0, tiled=True
    )
    grad_pre1 = grad_hidden * silu_slope(pre1)
    bias1_grad, gain1_grad = lax.psum(
        (jnp.sum(grad_pre1, axis=1), jnp.sum(grad_pre1 * normed1, axis=1)), "batch"
    )
    grad_first = (bn1_gain * rstd1)[:, None] * (
        grad_pre1
        - cell_live[None, :] * (bias1_grad[:, None] + normed1 * gain1_grad[:, None]) / cells
    )
    first_low = grad_first.astype(jnp.bfloat16)
    conv1_grad = weight_piece(first_low, lax.all_gather(features, "mp", axis=0, tiled=True))
    back_first = shifted_taps(first_low, -1)
    input_term = lax.psum_scatter(
        input_piece(conv1_weight, back_first), "mp", scatter_dimension=0, tiled=True
    )
    grad_features = input_term + grad_pre2
    conv1_grad, conv2_grad, head_grad, head_bias_grad = lax.psum(
        (conv1_grad, conv2_grad, head_grad, head_bias_grad), "batch"
    )
    bias_adjustment = cells / (cells - 1.0)
    new_mean1 = (1.0 - momentum) * run_mean1 + momentum * mean1
    new_var1 = (1.0 - momentum) * run_var1 + momentum * var1 * bias_adjustment
    new_mean2 = (1.0 - momentum) * run_mean2 + momentum * mean2
    new_var2 = (1.0 - momentum) * run_var2 + momentum * var2 * bias_adjustment
    return (
        loss,
        grad_features,
        conv1_grad,
        gain1_grad,
        bias1_grad,
        conv2_grad,
        gain2_grad,
        bias2_grad,
        head_grad,
        head_bias_grad,
        new_mean1,
        new_var1,
        new_mean2,
        new_var2,
    )


MESH = pl.DeviceIdType.MESH
F32 = jnp.float32
BF16 = jnp.bfloat16
LANES = 128
PLANE = 2


def nn(a, b, precision=None):
    return lax.dot_general(
        a, b, (((1,), (0,)), ((), ())), precision=precision, preferred_element_type=F32
    )


def nt(a, b, precision=None):
    return lax.dot_general(
        a, b, (((1,), (1,)), ((), ())), precision=precision, preferred_element_type=F32
    )


def tn(a, b, precision=None):
    return lax.dot_general(
        a, b, (((0,), (0,)), ((), ())), precision=precision, preferred_element_type=F32
    )


def rows_first(field, images):
    return jnp.concatenate(
        [
            field[(m * SIDE + i) * SIDE : (m * SIDE + i + 1) * SIDE]
            for i in range(SIDE)
            for m in range(images)
        ]
    )


def images_first(field, images):
    return jnp.concatenate(
        [
            field[(i * images + m) * SIDE : (i * images + m + 1) * SIDE]
            for m in range(images)
            for i in range(SIDE)
        ]
    )


def store_taps(put, field, block):
    cells, width = field.shape
    tiles = field.reshape(cells // SIDE, SIDE, width)
    column = lax.broadcasted_iota(jnp.int32, tiles.shape, 1)
    left = jnp.where(column == 0, 0.0, pltpu.roll(tiles, 1, 1)).reshape(cells, width)
    right = jnp.where(column == SIDE - 1, 0.0, pltpu.roll(tiles, SIDE - 1, 1)).reshape(
        cells, width
    )
    for lateral, shifted in enumerate((left, field, right)):
        put(lateral, pl.ds(block, cells), shifted.astype(BF16))


def row_sum(field):
    return jnp.sum(field, axis=0, keepdims=True)


def halves(row):
    return [row[:, at : at + LANES] for at in range(0, row.shape[1], LANES)]


def image_terms(logits, teacher, labels):
    def parts(values):
        top = jnp.max(values, axis=1, keepdims=True)
        weights = jnp.exp(values - top)
        total = jnp.sum(weights, axis=1, keepdims=True)
        return top + jnp.log(total), weights / total

    onehot = (
        labels == lax.broadcasted_iota(jnp.int32, logits.shape, 1)
    ).astype(F32)
    full_lse, full_soft = parts(logits)
    pupil = logits / softening_heat
    mentor = teacher / softening_heat
    pupil_rest = pupil - 1000.0 * onehot
    mentor_rest = mentor - 1000.0 * onehot
    pupil_all, pupil_soft = parts(pupil)
    mentor_all, _ = parts(mentor)
    pupil_other, pupil_rest_soft = parts(pupil_rest)
    mentor_other, mentor_rest_soft = parts(mentor_rest)

    def pick(values):
        return jnp.sum(onehot * values, axis=1, keepdims=True)

    pupil_hit = pick(pupil) - pupil_all
    mentor_hit = pick(mentor) - mentor_all
    pupil_miss = pupil_other - pupil_all
    mentor_miss = mentor_other - mentor_all
    hit_weight, miss_weight = jnp.exp(mentor_hit), jnp.exp(mentor_miss)
    binary = hit_weight * (mentor_hit - pupil_hit) + miss_weight * (
        mentor_miss - pupil_miss
    )
    gap = (mentor_rest - mentor_other) - (pupil_rest - pupil_other)
    spread = jnp.sum(mentor_rest_soft * gap, axis=1, keepdims=True)
    squared = softening_heat * softening_heat
    value = (
        full_lse
        - pick(logits)
        + squared * (target_weight * binary + other_weight * spread)
    )
    binary_slope = (
        (hit_weight + miss_weight) * pupil_soft
        - hit_weight * onehot
        - miss_weight * pupil_rest_soft
    )
    spread_slope = pupil_rest_soft - mentor_rest_soft
    slope = (
        full_soft
        - onehot
        + softening_heat
        * (target_weight * binary_slope + other_weight * spread_slope)
    )
    return value, slope


def block_kernel(
    sizes,
    features,
    counts,
    labels,
    teacher,
    conv1,
    conv2,
    head_weight,
    head_bias,
    *rest,
):
    params, rest = rest[:8], rest[8:]
    (
        out_cells,
        out_quarters,
        out_small,
        weight1,
        weight2,
        teacher_here,
        labels_here,
        head_here,
        head_bias_here,
        params_here,
        cells_in,
        params_all,
        counts_all,
        head_all,
        sums_all,
        logit_stage,
        logit_all,
        head_part,
        field,
        normed1,
        slope1,
        normed2,
        grad_pre2,
        taps_x,
        taps_h,
        taps_g,
        raw_x,
        raw_h,
        strip_taps,
        live_taps,
        live_rows,
        norm_part,
        norm_edges,
        live_part,
        live_edges,
        columns,
        strip_stage,
        strip_all,
        column_part,
        column_stage,
        column_all,
        mean_all,
        edge_part,
        edge_all,
        quarter_all,
        cells_stage,
        cells_out,
        load_sem,
        send_sem,
        sums_send,
        sums_recv,
        logit_recv,
        head_part_recv,
        cells_recv,
        params_recv,
        counts_recv,
        head_recv,
        weight_recv,
        raw_recv,
        strip_recv,
        column_recv,
        mean_recv,
        edge_recv,
        quarter_recv,
        out_recv,
    ) = rest
    n_batch, n_mp, channels, images = sizes
    n_z = n_mp // PLANE
    width = channels // n_mp
    quarter = width // n_batch
    block = images * SIDE
    cells = block * SIDE
    everyone = n_batch * n_mp
    b, p = lax.axis_index("batch"), lax.axis_index("mp")
    x, c = b // PLANE, b % PLANE
    z, y = p // PLANE, p % PLANE
    me = b * n_mp + p
    seat = y * n_batch + b
    n_seats = PLANE * n_batch
    means_end_value = {}
    sent = []

    def send(src, dst, recv, to_b, to_p):
        copy = pltpu.make_async_remote_copy(
            src_ref=src,
            dst_ref=dst,
            send_sem=send_sem.at[len(sent)],
            recv_sem=recv,
            device_id=(to_b, to_p),
            device_id_type=MESH,
        )
        copy.start()
        sent.append(copy)

    def await_bytes(ref, sem):
        pltpu.make_async_copy(ref, ref, sem).wait()

    far = [
        lambda v: v + 1 - 2 * (v % 2),
        lambda v: (v + n_z // 2) % n_z,
        lambda v: n_z - 1 - v,
    ]
    others = [
        (((x + dx) % 2) * PLANE + (c + dc) % 2, at_z * PLANE + (y + dy) % 2)
        for at_z in [other(z) for other in reversed(far)] + [z]
        for dy in (1, 0)
        for dx in (1, 0)
        for dc in (1, 0)
    ][:-1]

    barrier = pltpu.get_barrier_semaphore()
    for to_b, to_p in others:
        pl.semaphore_signal(
            barrier, inc=1, device_id=(to_b, to_p), device_id_type=MESH
        )

    loads = [
        (conv1, weight1.at[:, pl.ds(pl.multiple_of(p * width, width), width), :]),
        (conv2, weight2.at[:, pl.ds(pl.multiple_of(p * width, width), width), :]),
        (teacher, teacher_here),
        (labels, labels_here),
        (head_weight, head_here),
        (head_bias, head_bias_here),
    ] + [(ref, params_here.at[i]) for i, ref in enumerate(params)]
    loads = [
        pltpu.make_async_copy(src, dst, load_sem.at[i])
        for i, (src, dst) in enumerate(loads)
    ]
    for load in loads:
        load.start()
    for taps in (taps_x, taps_h, taps_g):
        for lateral in range(3):
            taps[lateral, 0:block] = jnp.zeros((block, channels), BF16)
            taps[lateral, block + cells : 2 * block + cells] = jnp.zeros(
                (block, channels), BF16
            )
    for load in loads:
        load.wait()
    group = LANES // width
    place = pl.multiple_of((p % group) * width, width)
    own_params = jnp.concatenate(
        [params_here[i] for i in range(4)] + [jnp.zeros((4, width), F32)]
    )
    own_params = jnp.concatenate(
        [own_params, jnp.zeros((8, LANES - width), F32)], axis=1
    )
    params_all[p] = pltpu.roll(own_params, place, 1)
    count = counts[0]
    counts_all[b] = jnp.zeros((8, LANES), F32) + count.astype(F32)
    head_all[p] = jnp.concatenate(
        [
            head_here[...],
            jnp.zeros((width, LANES - head_here.shape[1]), BF16),
        ],
        axis=1,
    )

    pl.semaphore_wait(barrier, everyone - 1)

    half = pl.ds(pl.multiple_of(c * LANES, LANES), LANES)
    strip = width // PLANE

    def rows_of(at_z, at_y, at_x):
        start = (at_z * PLANE + at_y) * width + at_x * strip
        return pl.ds(pl.multiple_of(start, strip), strip)

    mates = [(1, 0), (0, 1), (1, 1)]

    def column_start(which, weight):
        part = weight.at[:, rows_of(z, y, x), half]
        for k, other in enumerate(far):
            send(part, part, weight_recv.at[which, k], b, other(z) * PLANE + y)

    def shard_start(which, weight):
        part = weight.at[
            :, pl.ds(pl.multiple_of(p * width, width), width), half
        ]
        send(part, part, weight_recv.at[which, 3], b, z * PLANE + 1 - y)

    def layer_start(which, weight):
        for k, other in enumerate(far):
            part = weight.at[:, rows_of(other(z), y, x), half]
            await_bytes(part, weight_recv.at[which, k])
            for i, (dx, dy) in enumerate(mates):
                send(
                    part,
                    part,
                    weight_recv.at[which, 4 + 3 * k + i],
                    ((x + dx) % 2) * PLANE + c,
                    z * PLANE + (y + dy) % 2,
                )

    def core_start(which, weight):
        part = weight.at[
            :,
            pl.ds(
                pl.multiple_of((z * PLANE + 1 - y) * width, width), width
            ),
            half,
        ]
        await_bytes(part, weight_recv.at[which, 3])
        send(part, part, weight_recv.at[which, 13], x * PLANE + 1 - c, p)
        for k, other in enumerate(far):
            for i, (dx, dy) in enumerate(mates):
                part = weight.at[
                    :, rows_of(other(z), (y + dy) % 2, (x + dx) % 2), half
                ]
                await_bytes(part, weight_recv.at[which, 4 + 3 * k + i])
            part = weight.at[
                :,
                pl.ds(
                    pl.multiple_of(other(z) * PLANE * width, PLANE * width),
                    PLANE * width,
                ),
                half,
            ]
            send(part, part, weight_recv.at[which, 14 + k], x * PLANE + 1 - c, p)

    def core_end(which, weight):
        theirs = pl.ds(pl.multiple_of((1 - c) * LANES, LANES), LANES)
        part = weight.at[
            :,
            pl.ds(
                pl.multiple_of((z * PLANE + 1 - y) * width, width), width
            ),
            theirs,
        ]
        await_bytes(part, weight_recv.at[which, 13])
        for k, other in enumerate(far):
            part = weight.at[
                :,
                pl.ds(
                    pl.multiple_of(other(z) * PLANE * width, PLANE * width),
                    PLANE * width,
                ),
                theirs,
            ]
            await_bytes(part, weight_recv.at[which, 14 + k])

    column_start(0, weight1)
    shard_start(0, weight1)

    def cells_of(q):
        return pl.ds(pl.multiple_of(q * cells, cells), cells)

    own_cells = pltpu.make_async_copy(
        features.at[:, cells_of(p)], cells_in.at[p], load_sem.at[0]
    )
    own_cells.start()
    for k in range(1, n_mp):
        q = (p + k) % n_mp
        send(features.at[:, cells_of(q)], cells_in.at[p], cells_recv.at[k], b, q)
    column_start(1, weight2)
    for k in range(1, n_mp):
        q = (p + k) % n_mp
        send(params_all.at[p], params_all.at[p], params_recv.at[k], b, q)
        send(head_all.at[p], head_all.at[p], head_recv.at[k], b, q)
    for j in range(1, n_batch):
        send(
            counts_all.at[b],
            counts_all.at[b],
            counts_recv.at[j],
            (b + j) % n_batch,
            p,
        )

    layer_start(0, weight1)
    own_cells.wait()
    for k in range(1, n_mp):
        q = (p + n_mp - k) % n_mp
        await_bytes(cells_in.at[q], cells_recv.at[k])
    by_channel = cells_in[...].reshape(channels, cells).astype(F32)
    by_cell = rows_first(by_channel.T, images)
    field[...] = by_cell

    def put_x(lateral, where, value):
        taps_x[lateral, where] = value

    store_taps(put_x, by_cell, block)
    raw_x[seat] = by_cell.astype(BF16)

    shard_start(1, weight2)
    layer_start(1, weight2)
    core_start(0, weight1)

    for k in range(1, n_mp):
        q = (p + n_mp - k) % n_mp
        await_bytes(params_all.at[q], params_recv.at[k])
        await_bytes(head_all.at[q], head_recv.at[k])
    for j in range(1, n_batch):
        await_bytes(counts_all.at[(b + n_batch - j) % n_batch], counts_recv.at[j])
    full_params = jnp.concatenate(
        [
            sum(params_all[q] for q in range(at, at + group))
            for at in range(0, n_mp, group)
        ],
        axis=1,
    )
    gain1, bias1, gain2, bias2 = (full_params[i : i + 1] for i in range(4))
    live_images = sum(counts_all[i] for i in range(n_batch))[0:1, 0:1]
    live_cells = live_images * float(SIDE * SIDE)

    slot = (lax.broadcasted_iota(jnp.int32, (cells, channels), 0) // SIDE) % images
    live = (slot + p * images < count).astype(F32)

    shape = (cells, LANES)
    cell = lax.broadcasted_iota(jnp.int32, shape, 0)
    tap_at = lax.broadcasted_iota(jnp.int32, shape, 1)
    down = (tap_at >= 3).astype(jnp.int32) + (tap_at >= 6).astype(jnp.int32)
    across = tap_at - 3 * down
    at_row = cell // block + down - 1
    at_column = cell % SIDE + across - 1
    within = (at_row >= 0) & (at_row < SIDE) & (at_column >= 0) & (at_column < SIDE)
    inside = jnp.where(within & (tap_at < 9), 1.0, 0.0).astype(BF16)

    def conv(taps, weight):
        total = None
        for tap in range(9):
            vertical, lateral = divmod(tap, 3)
            term = nt(
                taps[lateral, block * vertical : block * vertical + cells],
                weight[tap],
            )
            total = term if total is None else total + term
        return total

    def conv_back(taps, weight):
        total = None
        for tap in range(9):
            vertical, lateral = divmod(tap, 3)
            up = block * (2 - vertical)
            term = nn(taps[2 - lateral, up : up + cells], weight[tap])
            total = term if total is None else total + term
        return total

    def sums_start(which, one, two):
        mine = sums_all.at[which, me, pl.ds(0, 4)]
        sums_all[which, me, 0:4] = jnp.concatenate(halves(one) + halves(two))
        for to_b, to_p in others:
            pltpu.make_async_remote_copy(
                src_ref=mine,
                dst_ref=mine,
                send_sem=sums_send.at[which],
                recv_sem=sums_recv.at[which],
                device_id=(to_b, to_p),
                device_id_type=MESH,
            ).start()

    def sums_end(which):
        everything = sums_all.at[which, pl.ds(0, everyone - 1), pl.ds(0, 4)]
        await_bytes(everything, sums_recv.at[which])
        total = jnp.sum(sums_all[which], axis=0)
        return (
            jnp.concatenate([total[0:1], total[1:2]], axis=1),
            jnp.concatenate([total[2:3], total[3:4]], axis=1),
        )

    def means_start(which, value):
        mean_all[which, z] = jnp.concatenate(
            halves(row_sum(value) / float(cells))
            + [jnp.zeros((8 - channels // LANES, LANES), F32)]
        )
        part = mean_all.at[which, z]
        for k, other in enumerate(far):
            send(part, part, mean_recv.at[which, k], b, other(z) * PLANE + y)

    def means_end(which):
        for k, other in enumerate(far):
            await_bytes(mean_all.at[which, other(z)], mean_recv.at[which, k])
        total = sum(mean_all[which, at_z] for at_z in range(n_z)) / float(n_z)
        return jnp.concatenate(
            [total[i : i + 1] for i in range(channels // LANES)], axis=1
        )

    def raw_start(which, raw):
        part = raw.at[seat]
        for i, (dx, dy) in enumerate(mates):
            send(
                part,
                part,
                raw_recv.at[which, i],
                ((x + dx) % 2) * PLANE + c,
                z * PLANE + (y + dy) % 2,
            )
        send(part, part, raw_recv.at[which, 3], x * PLANE + 1 - c, p)

    def seat_of(dx, dy, dc):
        return ((y + dy) % 2) * n_batch + ((x + dx) % 2) * PLANE + (c + dc) % 2

    def raw_forward(which, raw):
        for i, (dx, dy) in enumerate(mates):
            part = raw.at[seat_of(dx, dy, 0)]
            await_bytes(part, raw_recv.at[which, i])
            send(part, part, raw_recv.at[which, 4 + i], x * PLANE + 1 - c, p)

    def raw_end(which, raw):
        await_bytes(raw.at[seat_of(0, 0, 1)], raw_recv.at[which, 3])
        for i, (dx, dy) in enumerate(mates):
            await_bytes(raw.at[seat_of(dx, dy, 1)], raw_recv.at[which, 4 + i])

    seats = [
        (dx, dy, dc)
        for dy in (1, 0)
        for dx in (1, 0)
        for dc in (1, 0)
        if dx or dy or dc
    ]

    def strips_start(which, value):
        by_row = value.T
        for s in range(n_seats):
            at_y, at_b = divmod(s, n_batch)
            strip_stage[which, s] = jnp.concatenate(
                [
                    by_row[start : start + quarter]
                    for start in (
                        (at_z * PLANE + at_y) * width + at_b * quarter
                        for at_z in range(n_z)
                    )
                ]
            ).astype(BF16)
        for i, (dx, dy, dc) in enumerate(seats):
            send(
                strip_stage.at[which, seat_of(dx, dy, dc)],
                strip_all.at[which, seat],
                strip_recv.at[which, i],
                ((x + dx) % 2) * PLANE + (c + dc) % 2,
                z * PLANE + (y + dy) % 2,
            )
        strip_all[which, seat] = strip_stage[which, seat]

    shape = (9, 1, cells)
    cell = lax.broadcasted_iota(jnp.int32, shape, 2)
    tap_at = lax.broadcasted_iota(jnp.int32, shape, 0)
    down = (tap_at >= 3).astype(jnp.int32) + (tap_at >= 6).astype(jnp.int32)
    from_row = cell // block - down + 1
    from_column = cell % SIDE - (tap_at - 3 * down) + 1
    reach = jnp.where(
        (from_row >= 0)
        & (from_row < SIDE)
        & (from_column >= 0)
        & (from_column < SIDE),
        1.0,
        0.0,
    )

    def moved(value, tap):
        vertical, lateral = divmod(tap, 3)
        ahead = (vertical - 1) * block + lateral - 1
        return (pltpu.roll(value, ahead % cells, 1) if ahead else value) * reach[tap]

    strips = n_z * quarter

    def strips_product(which, raw):
        for i, (dx, dy, dc) in enumerate(seats):
            await_bytes(
                strip_all.at[which, seat_of(dx, dy, dc)], strip_recv.at[which, i]
            )
        for s in range(n_seats):
            value = strip_all[which, s].astype(F32)
            for tap in range(9):
                strip_taps[
                    tap * strips : (tap + 1) * strips, s * cells : (s + 1) * cells
                ] = moved(value, tap).astype(BF16)
        edges = sum(nn(strip_all[which, s], inside) for s in range(n_seats))
        return nn(strip_taps[...], raw[...].reshape(-1, channels)), edges

    def live_of(at_y, at_b):
        lane = lax.broadcasted_iota(jnp.int32, (8, cells), 1)
        image = (lane // SIDE) % images + (z * PLANE + at_y) * images
        return (image.astype(F32) < counts_all[at_b][:, 0:1]).astype(F32)

    def norm_product(raw):
        product, edges = strips_product(2, raw)
        norm_part[...] = product
        norm_edges[...] = edges
        live_part[...] = nn(
            live_taps[...].astype(BF16), raw[...].reshape(-1, channels)
        )
        live_edges[...] = nn(live_rows[...].astype(BF16), inside)

    def own_column(row):
        columns[...] = jnp.broadcast_to(row, (LANES, channels)).T
        return jnp.concatenate(
            [
                columns[
                    pl.ds(
                        pl.multiple_of(
                            (at_z * PLANE + y) * width + b * quarter, quarter
                        ),
                        quarter,
                    ),
                    :,
                ]
                for at_z in range(n_z)
            ]
        )[:, 0:1]

    def column_send(which, product, edges, sums=None):
        if sums is not None:
            bias_column, gain_column = (own_column(row / live_cells) for row in sums)
            edges = edges - (
                bias_column * row_sum(live_edges[...]) + gain_column * norm_edges[...]
            )
        mean = means_end(1 - which)
        means_end_value[which] = mean
        for at_z in range(n_z):
            edge_part[which, at_z] = edges[at_z * quarter : (at_z + 1) * quarter]
        for tap in range(9):
            rows = slice(tap * strips, (tap + 1) * strips)
            total = product[rows] - edges[:, tap : tap + 1] * mean
            if sums is not None:
                total = total - (
                    bias_column * live_part[tap : tap + 1]
                    + gain_column * norm_part[rows]
                )
            for at_z in range(n_z):
                column_part[which, at_z, tap * quarter : (tap + 1) * quarter] = total[
                    at_z * quarter : (at_z + 1) * quarter
                ]
        for at_z in range(n_z):
            column_stage[which, at_z] = jnp.concatenate(
                halves(column_part[which, at_z])
            ).astype(BF16)
        for k, other in enumerate(far):
            send(
                column_stage.at[which, other(z)],
                column_all.at[which, k],
                column_recv.at[which, k],
                b,
                other(z) * PLANE + y,
            )
            send(
                edge_part.at[which, other(z)],
                edge_all.at[which, k],
                edge_recv.at[which, k],
                b,
                other(z) * PLANE + y,
            )

    def unfold(piece):
        return jnp.concatenate(
            [
                piece[at : at + 9 * quarter]
                for at in range(0, piece.shape[0], 9 * quarter)
            ],
            axis=1,
        )

    def quarters_start(which):
        for k in range(len(far)):
            await_bytes(column_all.at[which, k], column_recv.at[which, k])
            await_bytes(edge_all.at[which, k], edge_recv.at[which, k])
        mean = means_end_value[which]
        edges = edge_part[which, z]
        total = column_part[which, z]
        for k in range(len(far)):
            edges = edges + edge_all[which, k]
            total = total + unfold(column_all[which, k].astype(F32))
        back = jnp.concatenate([edges[:, tap : tap + 1] * mean for tap in range(9)])
        quarter_all[which, b] = jnp.concatenate(halves(total + back)).astype(BF16)
        for j in range(1, n_batch):
            part = quarter_all.at[which, b]
            send(part, part, quarter_recv.at[which, j], (b + j) % n_batch, p)

    def quarters_end(which):
        for j in range(1, n_batch):
            await_bytes(
                quarter_all.at[which, (b + n_batch - j) % n_batch],
                quarter_recv.at[which, j],
            )
        out_quarters[which] = quarter_all[which]

    live_taps[...] = jnp.zeros_like(live_taps)
    means_start(0, by_cell)
    core_end(0, weight1)
    first = conv(taps_x, weight1)
    masked = first * live
    sums_start(0, row_sum(masked), row_sum(masked * first))
    raw_start(0, raw_x)
    for s in range(n_seats):
        alive = live_of(*divmod(s, n_batch))
        live_rows[s : s + 1] = alive[0:1].astype(F32)
        for tap in range(9):
            live_taps[tap : tap + 1, s * cells : (s + 1) * cells] = moved(
                alive, tap
            )[0:1]
    core_start(1, weight2)
    total, square = sums_end(0)
    mean1 = total / live_cells
    var1 = square / live_cells - mean1 * mean1
    rstd1 = lax.rsqrt(var1 + epsilon)
    flat = (first - mean1) * rstd1
    normed1[...] = flat
    pre1 = gain1 * flat + bias1
    sigma1 = jax.nn.sigmoid(pre1)
    slope1[...] = sigma1 * (1.0 + pre1 * (1.0 - sigma1))
    hidden = pre1 * sigma1

    def put_h(lateral, where, value):
        taps_h[lateral, where] = value

    store_taps(put_h, hidden, block)
    raw_h[seat] = hidden.astype(BF16)
    means_start(1, hidden)
    core_end(1, weight2)

    second = conv(taps_h, weight2)
    masked = second * live
    sums_start(1, row_sum(masked), row_sum(masked * second))
    raw_start(1, raw_h)
    strips_start(2, normed1[...] * live)
    raw_forward(0, raw_x)
    total, square = sums_end(1)
    mean2 = total / live_cells
    var2 = square / live_cells - mean2 * mean2
    rstd2 = lax.rsqrt(var2 + epsilon)
    flat2 = (second - mean2) * rstd2
    normed2[...] = flat2
    pre2 = gain2 * flat2 + bias2 + field[...]
    sigma2 = jax.nn.sigmoid(pre2)
    block_out = pre2 * sigma2

    pooled = sum(block_out[i * block : (i + 1) * block] for i in range(SIDE))
    pooled = jnp.sum(pooled.reshape(images, SIDE, channels), axis=1) / float(
        SIDE * SIDE
    )
    head = head_all[...].reshape(channels, LANES).astype(F32)[:, 0 : head_here.shape[1]]
    logits = nn(pooled, head, highest) + head_bias_here[...]
    slots = labels_here.shape[1]
    image_at = lax.broadcasted_iota(jnp.int32, (images, slots), 0) + p * images
    picked = lax.broadcasted_iota(jnp.int32, (images, slots), 1) == image_at
    own_labels = jnp.sum(
        jnp.where(picked, labels_here[...], 0), axis=1, keepdims=True
    )
    own_teacher = nn(picked.astype(F32), teacher_here[...], highest)
    own_live = (image_at[:, 0:1] < count).astype(F32)
    per_image, slope = image_terms(logits, own_teacher, own_labels)
    grad_logits = slope * (own_live * (loss_scale / live_images))
    grad_pooled = nt(grad_logits, head, highest) / float(SIDE * SIDE)
    spread = jnp.concatenate(
        [
            jnp.broadcast_to(grad_pooled[m : m + 1], (SIDE, channels))
            for m in range(images)
        ]
    )
    spread = jnp.concatenate([spread] * SIDE)
    pre_grad2 = spread * (sigma2 * (1.0 + pre2 * (1.0 - sigma2)))
    grad_pre2[...] = pre_grad2
    sums_start(2, row_sum(pre_grad2), row_sum(pre_grad2 * flat2))

    raw_forward(1, raw_h)

    bias_grad2, gain_grad2 = sums_end(2)
    grad_second = (gain2 * rstd2) * (
        grad_pre2[...]
        - live * (bias_grad2 + normed2[...] * gain_grad2) / live_cells
    )
    strips_start(0, grad_second)

    def put_g(lateral, where, value):
        taps_g[lateral, where] = value

    store_taps(put_g, grad_second.astype(BF16).astype(F32), block)
    pre_grad1 = conv_back(taps_g, weight2) * slope1[...]
    sums_start(3, row_sum(pre_grad1), row_sum(pre_grad1 * normed1[...]))
    scale1 = gain1 * rstd1
    strips_start(1, scale1 * pre_grad1)
    classes = logits.shape[1]
    for q in range(n_mp):
        logit_stage[q] = jnp.zeros((2 * images, LANES), F32)
        logit_stage[q, 0:images, 0:classes] = grad_logits
        logit_stage[q, 0:images, classes : classes + 1] = own_live * per_image
        logit_stage[q, images : 2 * images, 0:width] = pooled[
            :, q * width : (q + 1) * width
        ]
    for k in range(1, n_mp):
        q = (p + k) % n_mp
        send(logit_stage.at[q], logit_all.at[p], logit_recv.at[k], b, q)
    logit_all[p] = logit_stage[p]
    raw_end(0, raw_x)
    norm_product(raw_x)
    raw_end(1, raw_h)
    product2, edges2 = strips_product(0, raw_h)
    column_send(0, product2, edges2)
    product1, edges1 = strips_product(1, raw_x)
    bias_grad1, gain_grad1 = sums_end(3)
    grad_first = (gain1 * rstd1) * (
        pre_grad1 - live * (bias_grad1 + normed1[...] * gain_grad1) / live_cells
    )
    column_send(1, product1, edges1, (scale1 * bias_grad1, scale1 * gain_grad1))
    store_taps(put_g, grad_first.astype(BF16).astype(F32), block)
    grad_in = conv_back(taps_g, weight1) + grad_pre2[...]
    cells_stage[...] = (
        images_first(grad_in, images).T.astype(BF16).reshape(n_mp, width, cells)
    )
    for k in (4, 5, 3, 6, 2, 7, 1):
        q = (p + k) % n_mp
        send(cells_stage.at[q], cells_out.at[p], out_recv.at[k], b, q)
    cells_out[p] = cells_stage[p]
    for k in range(1, n_mp):
        await_bytes(logit_all.at[(p + n_mp - k) % n_mp], logit_recv.at[k])
    both = logit_all[...]
    upper = lax.broadcasted_iota(jnp.int32, both.shape, 1) < images
    upper_logits = jnp.where(upper, both, 0.0).reshape(-1, LANES)
    lifted = jnp.where(upper, pltpu.roll(both, images, 1), 0.0).reshape(-1, LANES)
    head_part[b, 0:width] = tn(lifted, upper_logits, highest)[0:width]
    head_part[b, width : width + 8] = jnp.broadcast_to(
        row_sum(upper_logits), (8, LANES)
    )
    for j in range(1, n_batch):
        part = head_part.at[b]
        send(part, part, head_part_recv.at[j], (b + j) % n_batch, p)
    quarters_start(0)
    quarters_start(1)

    def own(row):
        pieces = halves(row)
        mine = pieces[0]
        for i in range(1, len(pieces)):
            mine = jnp.where(p // group == i, pieces[i], mine)
        return pltpu.roll(mine, (LANES - place) % LANES, 1)[:, 0:width]

    adjust = live_cells / (live_cells - 1.0)
    kept = 1.0 - momentum
    rows = [
        own(gain_grad1),
        own(bias_grad1),
        own(gain_grad2),
        own(bias_grad2),
        kept * params_here[4] + momentum * own(mean1),
        kept * params_here[5] + momentum * own(var1 * adjust),
        kept * params_here[6] + momentum * own(mean2),
        kept * params_here[7] + momentum * own(var2 * adjust),
    ]
    out_small[...] = jnp.zeros_like(out_small)
    for i, row in enumerate(rows):
        out_small[i : i + 1, 0:width] = row
    for j in range(1, n_batch):
        await_bytes(head_part.at[(b + n_batch - j) % n_batch], head_part_recv.at[j])
    head_sum = sum(head_part[at_b] for at_b in range(n_batch))
    out_small[16 : 16 + width] = head_sum[0:width]
    last = head_sum[width : width + 1]
    out_small[8:9] = last
    out_small[9:10] = jnp.broadcast_to(
        last[:, classes : classes + 1] / live_images, (1, LANES)
    )

    quarters_end(0)
    for k in range(1, n_mp):
        q = (p + n_mp - k) % n_mp
        await_bytes(cells_out.at[q], out_recv.at[k])
    out_cells[...] = cells_out[...]
    quarters_end(1)

    for copy in sent:
        copy.wait_send()
    for which in range(4):
        await_bytes(
            sums_all.at[which, pl.ds(0, everyone - 1), pl.ds(0, 4)],
            sums_send.at[which],
        )


def finish_kernel(
    cells_in,
    quarters_in,
    small,
    loss,
    features_out,
    conv1_out,
    gain1_out,
    bias1_out,
    conv2_out,
    gain2_out,
    bias2_out,
    head_out,
    head_bias_out,
    *stats_out,
):
    n_mp, _, cells = cells_in.shape
    for q in range(n_mp):
        features_out[:, q * cells : (q + 1) * cells] = cells_in[q].astype(F32)
    n_batch = quarters_in.shape[1]
    quarter = conv1_out.shape[1] // n_batch
    for which, out in enumerate((conv2_out, conv1_out)):
        for at_b in range(n_batch):
            whole = quarters_in[which, at_b].astype(F32)
            for start in range(0, whole.shape[0], quarter):
                tap, lanes = start // quarter % 9, start // quarter // 9 * LANES
                out[
                    tap, at_b * quarter : (at_b + 1) * quarter, lanes : lanes + LANES
                ] = whole[start : start + quarter]
    vectors = (gain1_out, bias1_out, gain2_out, bias2_out) + stats_out
    for i, out in enumerate(vectors):
        out[...] = small[i : i + 1, 0 : out.shape[1]]
    head_bias_out[...] = small[8:9, 0 : head_bias_out.shape[1]]
    loss[0] = small[9, 0]
    head_out[...] = small[16 : 16 + head_out.shape[0], 0 : head_out.shape[1]]


def block_device(
    n_batch,
    n_mp,
    features,
    counts,
    labels,
    teacher,
    conv1_weight,
    bn1_gain,
    bn1_bias,
    conv2_weight,
    bn2_gain,
    bn2_bias,
    head_weight,
    head_bias,
    run_mean1,
    run_var1,
    run_mean2,
    run_var2,
):
    width, cell_count = features.shape
    channels = width * n_mp
    classes = head_weight.shape[1]
    slots = cell_count // (SIDE * SIDE)
    images = slots // n_mp
    block = images * SIDE
    cells = block * SIDE
    n_z = n_mp // PLANE
    quarter = width // n_batch
    seats = n_batch * PLANE
    everyone = n_batch * n_mp
    tall = 9 * quarter * (channels // LANES)
    padded = cells + 2 * block

    def row(values):
        return values.reshape(1, -1)

    def taps_out(values):
        return values.transpose(1, 0, 2)

    def vmem(*shape, dtype=F32):
        return pltpu.VMEM(shape, dtype)

    def low(*shape):
        return pltpu.VMEM(shape, BF16)

    any_space = pl.BlockSpec(memory_space=pl.ANY)
    in_vmem = pl.BlockSpec(memory_space=pltpu.VMEM)
    in_smem = pl.BlockSpec(memory_space=pltpu.SMEM)
    shape = jax.ShapeDtypeStruct
    dma = pltpu.SemaphoreType.DMA
    grant = pltpu.CompilerParams(
        collective_id=0, has_side_effects=True, vmem_limit_bytes=60 * 2**20
    )
    packed = pl.pallas_call(
        functools.partial(block_kernel, (n_batch, n_mp, channels, images)),
        out_shape=(
            shape((n_mp, width, cells), BF16),
            shape((2, n_batch, tall, LANES), BF16),
            shape((16 + width, LANES), F32),
        ),
        in_specs=[any_space, in_smem] + [any_space] * 14,
        out_specs=(in_vmem,) * 3,
        scratch_shapes=[
            low(9, channels, channels),
            low(9, channels, channels),
            vmem(slots, classes),
            vmem(1, slots, dtype=jnp.int32),
            low(width, classes),
            vmem(1, classes),
            vmem(8, 1, width),
            low(n_mp, width, cells),
            vmem(n_mp, 8, LANES),
            vmem(n_batch, 8, LANES),
            low(n_mp, width, LANES),
            vmem(4, everyone, 8, LANES),
            vmem(n_mp, 2 * images, LANES),
            vmem(n_mp, 2 * images, LANES),
            vmem(n_batch, width + 8, LANES),
            vmem(cells, channels),
            vmem(cells, channels),
            vmem(cells, channels),
            vmem(cells, channels),
            vmem(cells, channels),
            low(3, padded, channels),
            low(3, padded, channels),
            low(3, padded, channels),
            low(seats, cells, channels),
            low(seats, cells, channels),
            low(9 * n_z * quarter, seats * cells),
            vmem(16, seats * cells),
            vmem(8, cells),
            vmem(9 * n_z * quarter, channels),
            vmem(n_z * quarter, LANES),
            vmem(16, channels),
            vmem(8, LANES),
            vmem(channels, LANES),
            low(3, seats, n_z * quarter, cells),
            low(3, seats, n_z * quarter, cells),
            vmem(2, n_z, 9 * quarter, channels),
            low(2, n_z, tall, LANES),
            low(2, n_z - 1, tall, LANES),
            vmem(2, n_z, 8, LANES),
            vmem(2, n_z, quarter, LANES),
            vmem(2, n_z - 1, quarter, LANES),
            low(2, n_batch, tall, LANES),
            low(n_mp, width, cells),
            low(n_mp, width, cells),
            dma((14,)),
            dma((160,)),
            dma((4,)),
            dma((4,)),
            dma((n_mp,)),
            dma((n_batch,)),
            dma((n_mp,)),
            dma((n_mp,)),
            dma((n_batch,)),
            dma((n_mp,)),
            dma((2, 17)),
            dma((2, 7)),
            dma((3, 7)),
            dma((2, n_z - 1)),
            dma((2, n_z - 1)),
            dma((2, n_z - 1)),
            dma((2, n_batch)),
            dma((n_mp,)),
        ],
        compiler_params=grant,
    )(
        features,
        counts,
        row(labels),
        teacher,
        taps_out(conv1_weight),
        taps_out(conv2_weight),
        head_weight,
        row(head_bias),
        row(bn1_gain),
        row(bn1_bias),
        row(bn2_gain),
        row(bn2_bias),
        row(run_mean1),
        row(run_var1),
        row(run_mean2),
        row(run_var2),
    )
    vector = shape((1, width), F32)
    results = pl.pallas_call(
        finish_kernel,
        out_shape=(
            shape((1,), F32),
            shape((width, cell_count), F32),
            shape((9, width, channels), F32),
            vector,
            vector,
            shape((9, width, channels), F32),
            vector,
            vector,
            shape((width, classes), F32),
            shape((1, classes), F32),
            vector,
            vector,
            vector,
            vector,
        ),
        in_specs=[in_vmem] * 3,
        out_specs=(in_smem,) + (in_vmem,) * 13,
        compiler_params=pltpu.CompilerParams(vmem_limit_bytes=60 * 2**20),
    )(*packed)
    loss, grad_features, conv1, gain1, bias1, conv2, gain2, bias2, head, *small = results
    return (
        loss.reshape(()),
        grad_features,
        taps_out(conv1),
        gain1.reshape(-1),
        bias1.reshape(-1),
        taps_out(conv2),
        gain2.reshape(-1),
        bias2.reshape(-1),
        head,
    ) + tuple(values.reshape(-1) for values in small)


def by_images(n_batch, n_mp, features, counts, *rest):
    width, cell_count = features.shape
    images = cell_count // (SIDE * SIDE) // n_mp
    fits = (
        n_batch == 4
        and n_mp == 8
        and width == 32
        and images == 4
        and head_fits(rest)
    )
    if not fits:
        return plain_device(features, counts, *rest)
    return block_device(n_batch, n_mp, features, counts, *rest)


def head_fits(rest):
    return rest[8].shape[1] < LANES


def solution(mesh):
    return jax.shard_map(
        functools.partial(by_images, mesh.shape["batch"], mesh.shape["mp"]),
        mesh=mesh,
        in_specs=(
            P("mp", "batch"),
            P("batch"),
            P("batch"),
            P("batch", None),
            P("mp", None, None),
            P("mp"),
            P("mp"),
            P("mp", None, None),
            P("mp"),
            P("mp"),
            P("mp", None),
            P(),
            P("mp"),
            P("mp"),
            P("mp"),
            P("mp"),
        ),
        out_specs=(
            P(),
            P("mp", "batch"),
            P("mp", None, None),
            P("mp"),
            P("mp"),
            P("mp", None, None),
            P("mp"),
            P("mp"),
            P("mp", None),
            P(),
            P("mp"),
            P("mp"),
            P("mp"),
            P("mp"),
        ),
        check_vma=False,
    )
```
